32 devices in a mesh: dp: 8 (over y, x, core), tensor: 4 (over z).
Axes of the slice: x: 2, y: 2, z: 4, core: 2. Of those that a mesh axis runs over, the one named last changes fastest.
Arguments:
- features: float32 [1024, 16, 100], P('tensor', 'dp'), may hold values from -40 to 40
- table_ids: int32 [1024, 16], P(None, 'dp'), may hold values from 0 to 4, as said below
- train_flags: int32 [1024, 16], P(None, 'dp'), may hold values from 0 to 1, as said below
- enc_w: bfloat16 [100, 512], replicated, may hold values from -0.625 to 0.625
- enc_b: float32 [512], replicated, may hold values from -3 to 3
- w_qkv: bfloat16 [2, 3, 512, 512], P(None, None, None, 'tensor'), may hold values from -0.25 to 0.25
- b_qv: float32 [2, 2, 512], P(None, None, 'tensor'), may hold values from -3 to 3
- w_out: bfloat16 [2, 512, 512], P(None, 'tensor'), may hold values from -1 to 1
- out_bias: float32 [2, 2, 512], replicated, may hold values from -2 to 2
- ln_gain: float32 [2, 2, 512], replicated, may hold values from 0.5 to 1.5
- ln_bias: float32 [2, 2, 512], replicated, may hold values from -2 to 2
- w_up: bfloat16 [2, 512, 1024], P(None, None, 'tensor'), may hold values from -0.25 to 0.25
- b_up: float32 [2, 1024], P(None, 'tensor'), may hold values from -3 to 3
- w_down: bfloat16 [2, 1024, 512], P(None, 'tensor'), may hold values from -0.1875 to 0.1875
- cotangent: bfloat16 [1024, 16, 512], P('tensor', 'dp'), may hold values from -6 to 6
Outputs:
- final_rows: bfloat16 [1024, 16, 512], P('tensor', 'dp')
- grad_features: float32 [1024, 16, 100], P('tensor', 'dp')
- grad_enc_w: float32 [100, 512], replicated
- grad_enc_b: float32 [512], replicated
- grad_w_qkv: float32 [2, 3, 512, 512], P(None, None, None, 'tensor')
- grad_b_qv: float32 [2, 2, 512], P(None, None, 'tensor')
- grad_w_out: float32 [2, 512, 512], P(None, 'tensor')
- grad_out_bias: float32 [2, 2, 512], replicated
- grad_ln_gain: float32 [2, 2, 512], replicated
- grad_ln_bias: float32 [2, 2, 512], replicated
- grad_w_up: float32 [2, 512, 1024], P(None, None, 'tensor')
- grad_b_up: float32 [2, 1024], P(None, 'tensor')
- grad_w_down: float32 [2, 1024, 512], P(None, 'tensor')
The draws below stay inside these ranges and needn't reach their ends.
Inputs may be any that keep to these rules, and one draw needn't show every extreme that they name: `table_ids`: along the rows of a sequence the table ids never fall, and all 5 tables occur in every sequence. `train_flags`: the first row of every table is a train row.
All inputs are finite; a program needn't handle non-finite values.
Results may differ from the reference program's by a relative error of at most 0.03.
Values may be sent and summed in bfloat16 or wider, within the bound.
No kernel may reach another device: no remote copies, remote signals or barrier semaphores. Data moves between devices by JAX's collectives and lax.ppermute only.
A program may use at most 128 MiB of HBM per device.

```python
import math
import jax
import jax.numpy as jnp
from jax import lax

D = 512
HEADS = 4
HD = 128
FF = 1024
F = 100
ROWS = 1024
NTAB = 5
LAYERS = 2
SEQS = 16


def table_layout(key):
    subkeys = jax.random.split(key, 5)
    cut_one = jax.random.randint(subkeys[0], (SEQS,), 1, 3)
    cut_two = jax.random.randint(subkeys[1], (SEQS,), ROWS // 16, ROWS // 4)
    cut_three = jax.random.randint(subkeys[2], (SEQS,), 3 * ROWS // 4 + 1, ROWS - ROWS // 16)
    cut_four = jax.random.randint(subkeys[3], (SEQS,), cut_three + 1, ROWS)
    position = jnp.arange(ROWS, dtype=jnp.int32)[:, None]
    tables = (position >= cut_one).astype(jnp.int32) + (position >= cut_two).astype(jnp.int32) + (position >= cut_three).astype(jnp.int32) + (position >= cut_four).astype(jnp.int32)
    starts = (position == 0) | (position == cut_one) | (position == cut_two) | (position == cut_three) | (position == cut_four)
    coin_flips = jax.random.randint(subkeys[4], (ROWS, SEQS), 0, 2)
    train_rows = jnp.maximum(coin_flips, starts.astype(jnp.int32))
    return (tables, train_rows)


def draw_table_ids(key, part):
    return table_layout(key)[0]


def draw_train_flags(key, part):
    return table_layout(key)[1]


def draw_features(key, part):
    key = jax.random.fold_in(key, 11)
    subkeys = jax.random.split(key, 3)
    position = jnp.arange(ROWS, dtype=jnp.float32)
    row_rise = (0.5 + position / ROWS)[:, None, None]
    column_scale = jnp.exp(jax.random.uniform(subkeys[1], (1, SEQS, F), minval=math.log(0.3), maxval=math.log(3.0)))
    column_shift = jnp.clip(jax.random.normal(subkeys[2], (1, SEQS, F)), -3.0, 3.0) * column_scale
    noise_draw = jnp.clip(jax.random.normal(subkeys[0], (ROWS, SEQS, F)), -5.0, 5.0)
    drawn_rows = noise_draw * row_rise * column_scale + column_shift
    return drawn_rows.astype(jnp.float32)


def steps_of(key, dims, shards, smallest, high):
    gain = 1.0
    for dim, parts in shards:
        heights = jax.random.uniform(jax.random.fold_in(jax.random.fold_in(key, 6), dim), (parts,), jnp.float32, smallest / len(shards), high / len(shards))
        gain = gain * jnp.repeat(jnp.exp(heights), dims[dim] // parts).reshape((-1,) + (1,) * (len(dims) - 1 - dim))
    return gain


def bell_draw(rng, shape, width, most, pieces=(), held_as=jnp.bfloat16):
    values = width * jax.random.normal(rng, shape, jnp.float32)
    if pieces:
        values = values * steps_of(rng, shape, pieces, -0.22, 0.18)
    return jnp.clip(values, -most, most).astype(held_as)


def setup_inputs(seed: int = 0) -> dict:
    arg_keys = jax.random.split(jax.random.key(seed), 16)
    return {
        "features": draw_features(jax.random.fold_in(arg_keys[15], 71), 0),
        "table_ids": draw_table_ids(jax.random.fold_in(arg_keys[15], 71), 0),
        "train_flags": draw_train_flags(jax.random.fold_in(arg_keys[15], 71), 0),
        "enc_w": bell_draw(arg_keys[3], (F, D), F ** -0.5, 0.625),
        "enc_b": bell_draw(arg_keys[4], (D,), 0.5, 3.0, (), jnp.float32),
        "w_qkv": bell_draw(arg_keys[5], (LAYERS, 3, D, D), D ** -0.5, 0.25, ((3, 4),)),
        "b_qv": bell_draw(arg_keys[6], (LAYERS, 2, D), 0.5, 3.0, ((2, 4),), jnp.float32),
        "w_out": bell_draw(arg_keys[7], (LAYERS, D, D), (D // 16) ** -0.5, 1.0, ((1, 4),)),
        "out_bias": bell_draw(arg_keys[8], (LAYERS, 2, D), 0.3, 2.0, (), jnp.float32),
        "ln_gain": jnp.clip(1.0 + 0.1 * jax.random.normal(arg_keys[9], (LAYERS, 2, D), jnp.float32), 0.5, 1.5),
        "ln_bias": bell_draw(arg_keys[10], (LAYERS, 2, D), 0.3, 2.0, (), jnp.float32),
        "w_up": bell_draw(arg_keys[11], (LAYERS, D, FF), D ** -0.5, 0.25, ((2, 4),)),
        "b_up": bell_draw(arg_keys[12], (LAYERS, FF), 0.5, 3.0, ((1, 4),), jnp.float32),
        "w_down": bell_draw(arg_keys[13], (LAYERS, FF, D), FF ** -0.5, 0.1875, ((1, 4),)),
        "cotangent": bell_draw(arg_keys[14], (ROWS, SEQS, D), 1.0, 6.0, ((0, 4), (1, 8))),
    }


spread_floor = 0.1
norm_eps = 1e-05
highest = lax.Precision.HIGHEST

@jax.custom_vjp
def low(v):
    return lax.optimization_barrier(v.astype(jnp.bfloat16)).astype(jnp.float32)

@jax.custom_vjp
def low_back(v):
    return v

def low_keep(v):
    return (low(v), None)

def low_pass(kept, grad):
    return (grad,)

def back_keep(v):
    return (v, None)

def back_low(kept, grad):
    return (low(grad),)
low.defvjp(low_keep, low_pass)
low_back.defvjp(back_keep, back_low)

def layer_norm(values, norm_gain, norm_shift):
    centre = values - lax.optimization_barrier(jnp.mean(values, -1, keepdims=True))
    spread = lax.optimization_barrier(jnp.mean(centre * centre, -1, keepdims=True))
    return centre * lax.rsqrt(spread + norm_eps) * norm_gain + norm_shift

def encode(enc_w, enc_b, feature_rows, member, picked):
    counts = lax.optimization_barrier(jnp.sum(picked, 0))
    sums_one = jnp.einsum('rgt,rgf->gtf', picked, feature_rows, precision=highest)
    sums_two = jnp.einsum('rgt,rgf->gtf', picked, feature_rows * feature_rows, precision=highest)
    table_means = sums_one / counts[..., None]
    excess = sums_two / counts[..., None] - table_means * table_means
    scales = lax.rsqrt(jnp.maximum(excess, spread_floor))
    mean_rows = jnp.einsum('rgt,gtf->rgf', member, table_means, precision=highest)
    scale_rows = jnp.einsum('rgt,gtf->rgf', member, scales, precision=highest)
    normed = low((feature_rows - mean_rows) * scale_rows)
    return low_back(jnp.einsum('rgf,fd->rgd', normed, enc_w, precision=highest) + enc_b)

def layer_block(current, layer_weights, allowed):
    w_qkv, b_qv, w_out, out_bias, ln_gain, ln_bias, w_up, b_up, w_down = layer_weights
    inputs_low = low(current)
    projected = jnp.einsum('rgd,cdh->crgh', inputs_low, w_qkv, precision=highest)
    queries = low(low_back(projected[0] + b_qv[0]))
    key_rows = low(low_back(projected[1]))
    value_rows = low(low_back(projected[2] + b_qv[1]))
    head_shape = queries.shape[:2] + (HEADS, HD)
    scores = jnp.einsum('qghd,kghd->ghqk', queries.reshape(head_shape), key_rows.reshape(head_shape), precision=highest)
    scores = low_back(scores * (1.0 / math.sqrt(HD)))
    scores = jnp.where(allowed[:, None], scores, -1e+30)
    probs = jax.nn.softmax(scores, axis=-1)
    mixture = jnp.einsum('ghqk,kghd->qghd', low(probs), value_rows.reshape(head_shape), precision=highest)
    mixture = low(low_back(mixture.reshape(queries.shape)))
    attention = low_back(jnp.einsum('rgh,hd->rgd', mixture, w_out, precision=highest) + out_bias[0])
    middle = layer_norm(current + attention, ln_gain[0], ln_bias[0])
    hidden = low_back(jnp.einsum('rgd,df->rgf', low(middle), w_up, precision=highest) + b_up)
    activation = low(jax.nn.gelu(hidden, approximate=False))
    feedforward = low_back(jnp.einsum('rgf,fd->rgd', activation, w_down, precision=highest) + out_bias[1])
    return layer_norm(middle + feedforward, ln_gain[1], ln_bias[1])

def forward(params, feature_rows, table_rows, train_rows):
    member = (table_rows[..., None] == jnp.arange(NTAB, dtype=jnp.int32)).astype(feature_rows.dtype)
    picked = member * train_rows[..., None].astype(feature_rows.dtype)
    current = encode(params[0], params[1], feature_rows, member, picked)
    table_cols = table_rows.T
    train_cols = train_rows.T
    allowed = (table_cols[:, :, None] == table_cols[:, None, :]) & (train_cols[:, None, :] > 0)
    for layer_index in range(LAYERS):
        current = layer_block(current, tuple((entry[layer_index] for entry in params[2:])), allowed)
    return current

def reference(features, table_ids, train_flags, enc_w, enc_b, w_qkv, b_qv, w_out, out_bias, ln_gain, ln_bias, w_up, b_up, w_down, cotangent):
    params = tuple((entry.astype(jnp.float32) for entry in (enc_w, enc_b, w_qkv, b_qv, w_out, out_bias, ln_gain, ln_bias, w_up, b_up, w_down)))
    per_group = math.gcd(SEQS, max(1, 4096 // ROWS))

    def by_group(array):
        array = array.reshape((array.shape[0], SEQS // per_group, per_group) + array.shape[2:])
        return jnp.moveaxis(array, 1, 0)

    def rejoin(array):
        array = jnp.moveaxis(array, 0, 1)
        return array.reshape((array.shape[0], SEQS) + array.shape[3:])

    def one_group(running, group_item):
        feature_rows, table_rows, train_rows, cot_rows = group_item
        outputs, pullback = jax.vjp(lambda weights, inputs: forward(weights, inputs, table_rows, train_rows), params, feature_rows)
        gradients, grad_inputs = pullback(cot_rows)
        running = jax.tree.map(lambda left, right: left + right, running, gradients)
        return (running, (outputs.astype(jnp.bfloat16), grad_inputs))
    zero_grads = tuple((jnp.zeros_like(entry) for entry in params))
    sequence_items = (by_group(features.astype(jnp.float32)), by_group(table_ids), by_group(train_flags), by_group(cotangent.astype(jnp.float32)))
    totals, (outputs, grad_inputs) = lax.scan(one_group, zero_grads, sequence_items)
    return (rejoin(outputs), rejoin(grad_inputs), totals[0], totals[1], totals[2], totals[3], totals[4], totals[5], totals[6], totals[7], totals[8], totals[9], totals[10])
```

```python
import math

import jax
import jax.numpy as jnp
from jax import lax
from jax.sharding import PartitionSpec as P

HD = 128
NTAB = 5
spread_floor = 0.1
norm_eps = 1e-05
highest = lax.Precision.HIGHEST
f32 = jnp.float32
bf16 = jnp.bfloat16


def dot(a, b, dims):
    return lax.dot_general(a, b, (dims, ((), ())), preferred_element_type=f32)


def swap_dp(values, mask):
    size = lax.axis_size("dp")
    return lax.ppermute(values, "dp", [(i, i ^ mask) for i in range(size)])


def swap_z(values, mask):
    size = lax.axis_size("tensor")
    return lax.ppermute(values, "tensor", [(i, i ^ mask) for i in range(size)])


def relay_pairs(step):
    size, width = lax.axis_size("dp"), lax.axis_size("tensor")
    pairs = []
    for i in range(size):
        for z in range(width):
            target = (i - i % 2 + z // 2) * width + 2 * (i % 2) + (step ^ (z & 1))
            pairs.append((i * width + z, target))
    return pairs


def to_sequences(blocks, z):
    odd = (z & 1) == 1
    got = []
    for step in range(2):
        block = jnp.where(odd, blocks[:, 1 - step], blocks[:, step])
        got.append(lax.ppermute(block, ("dp", "tensor"), relay_pairs(step)))
    return jnp.where(odd, jnp.concatenate([got[1], got[0]]), jnp.concatenate(got))


def from_sequences(rows, z):
    part = rows.shape[0] // 2
    odd = (z & 1) == 1
    first, second = rows[:part], rows[part:]
    got = []
    for step in range(2):
        block = jnp.where(odd, second, first) if step == 0 else jnp.where(odd, first, second)
        pairs = [(b, a) for a, b in relay_pairs(step)]
        got.append(lax.ppermute(block, ("dp", "tensor"), pairs))
    return jnp.where(odd, jnp.stack([got[1], got[0]], 1), jnp.stack(got, 1))


def flip_if(values, bit, axis):
    return jnp.where(bit == 1, jnp.flip(values, axis), values)


def pack_local(wq, wo, wu, wd):
    d, f = wq.shape[1], wu.shape[1]
    q = 8
    a = wq.reshape(3, q, d // q, HD).transpose(1, 0, 2, 3).reshape(q, -1, HD)
    b = wo.reshape(q, HD // q, d // HD, HD).transpose(0, 2, 1, 3).reshape(q, -1, HD)
    c = wu.reshape(q, d // q, f // HD, HD).transpose(0, 2, 1, 3).reshape(q, -1, HD)
    e = wd.reshape(q, f // q, d // HD, HD).transpose(0, 2, 1, 3).reshape(q, -1, HD)
    return jnp.concatenate([a, b, c, e], 1)


def unpack_local(pieces, d, f):
    q = 8
    s1 = 3 * d // q
    s2 = s1 + (HD // q) * (d // HD)
    s3 = s2 + (d // q) * (f // HD)
    wq = pieces[:, :s1].reshape(q, 3, d // q, HD).transpose(1, 0, 2, 3).reshape(3, d, HD)
    wo = pieces[:, s1:s2].reshape(q, d // HD, HD // q, HD).transpose(0, 2, 1, 3).reshape(HD, d)
    wu = pieces[:, s2:s3].reshape(q, f // HD, d // q, HD).transpose(0, 2, 1, 3).reshape(d, f)
    wd = pieces[:, s3:].reshape(q, d // HD, f // q, HD).transpose(0, 2, 1, 3).reshape(f, d)
    return wq, wo, wu, wd


def layer_norm_parts(values):
    centre = values - jnp.mean(values, -1, keepdims=True)
    inv = lax.rsqrt(jnp.mean(centre * centre, -1, keepdims=True) + norm_eps)
    return centre * inv, inv


def layer_norm_back(grad, normal, inv, gain):
    e = grad * gain
    return (
        (e - jnp.mean(e, -1, keepdims=True) - normal * jnp.mean(e * normal, -1, keepdims=True)) * inv,
        jnp.sum(grad * normal, 0),
        jnp.sum(grad, 0),
    )


def gelu_exact(values):
    return jax.nn.gelu(values, approximate=False)


def gather_weights(piece, p, o, z):
    width = lax.axis_size("tensor")
    rows = jnp.stack([piece] + [swap_z(piece, k) for k in range(1, width)])
    plane = jnp.stack([rows] + [swap_dp(rows, 2 * r) for r in range(1, 4)])
    whole = jnp.stack([plane, swap_dp(plane, 1)])
    whole = whole.reshape((2,) * 5 + piece.shape)
    for axis, bit in enumerate((p, o >> 1, o & 1, z >> 1, z & 1)):
        whole = flip_if(whole, bit, axis)
    return whole.reshape((8, width) + piece.shape)


def whole_weights(packed, d, f):
    width = packed.shape[1]
    parts = [unpack_local(packed[:, z], d, f) for z in range(width)]
    return (
        jnp.concatenate([e[0] for e in parts], 2),
        jnp.concatenate([e[1] for e in parts], 0),
        jnp.concatenate([e[2] for e in parts], 1),
        jnp.concatenate([e[3] for e in parts], 0),
    )


def pick(values, index):
    return lax.dynamic_index_in_dim(values, index, 0, keepdims=False)


def reduce_grads(packed, shared, p, o, z):
    width = packed.shape[1]
    piece_rows = packed.shape[2]
    flat = packed.reshape(8, width * piece_rows, HD)
    if shared is not None:
        flat = jnp.concatenate([flat, shared], 1)
    halves = flat.reshape((2, 4) + flat.shape[1:]).astype(bf16)
    own = pick(halves, p).astype(f32) + swap_dp(pick(halves, 1 - p), 1).astype(f32)
    own = own.astype(bf16)
    total = pick(own, o).astype(f32)
    for r in range(1, 4):
        total = total + swap_dp(pick(own, o ^ r), 2 * r).astype(f32)
    mask = 8
    while mask < lax.axis_size("dp"):
        total = total + swap_dp(total.astype(bf16), mask).astype(f32)
        mask *= 2
    low = total.astype(bf16)
    quarters = low[: width * piece_rows].reshape(width, piece_rows, HD)
    rest = low[width * piece_rows :]
    share = jnp.concatenate([pick(quarters, z), rest]).astype(f32)
    for k in range(1, width):
        share = share + swap_z(jnp.concatenate([pick(quarters, z ^ k), rest]), k).astype(f32)
    share = share.astype(bf16)
    plane = jnp.stack([share] + [swap_dp(share, 2 * r) for r in range(1, 4)])
    plane = plane.reshape((2, 2) + share.shape)
    plane = flip_if(flip_if(plane, o >> 1, 0), o & 1, 1).reshape((4,) + share.shape)
    whole = flip_if(jnp.stack([plane, swap_dp(plane, 1)]), p, 0)
    whole = whole.reshape((8,) + share.shape)
    return whole[:, :piece_rows].astype(f32), whole[:, piece_rows:].astype(f32)


def local(
    features,
    table_ids,
    train_flags,
    enc_w,
    enc_b,
    w_qkv,
    b_qv,
    w_out,
    out_bias,
    ln_gain,
    ln_bias,
    w_up,
    b_up,
    w_down,
    cotangent,
):
    part = features.shape[0]
    width = lax.axis_size("tensor")
    layers, d = w_qkv.shape[0], w_qkv.shape[2]
    f_part = w_up.shape[2]
    f_all = f_part * width
    heads = d // HD
    half = 2 * part
    di, z = lax.axis_index("dp"), lax.axis_index("tensor")
    p, o = di % 2, (di // 2) % 4
    q = p * 4 + o

    weights = []
    for l in range(layers):
        piece = pick(pack_local(w_qkv[l], w_out[l], w_up[l], w_down[l]), q)
        weights.append(whole_weights(gather_weights(piece, p, o, z), d, f_all // width))
    bias_local = jnp.concatenate([b_qv.reshape(-1, HD), b_up.reshape(-1, HD)])
    bias_all = lax.all_gather(bias_local, "tensor")
    nb = 2 * layers
    bqv_all = bias_all[:, :nb].transpose(1, 0, 2).reshape(layers, 2, d)
    bup_all = bias_all[:, nb:].reshape(width, layers, f_part).transpose(1, 0, 2).reshape(layers, f_all)

    feat_half = to_sequences(features, z)
    cot_half = to_sequences(cotangent, z)
    codes = (table_ids * 2 + train_flags).T
    other_codes = swap_dp(codes, 1)
    seq_codes = pick(jnp.where(p == z // 2, codes, other_codes), z & 1)
    code_own = lax.dynamic_slice_in_dim(seq_codes, p * half, half)
    code_other = lax.dynamic_slice_in_dim(seq_codes, (1 - p) * half, half)
    code_keys = jnp.concatenate([code_own, code_other])
    member = ((code_own >> 1)[:, None] == jnp.arange(NTAB, dtype=jnp.int32)).astype(f32)
    picked = member * (code_own & 1)[:, None].astype(f32)
    feat_other = swap_dp(feat_half, 1)
    feat_all = jnp.concatenate([feat_half, feat_other])
    picked_all = ((code_keys >> 1)[:, None] == jnp.arange(NTAB, dtype=jnp.int32)).astype(f32) * (
        code_keys & 1
    )[:, None].astype(f32)
    counts = jnp.sum(picked_all, 0)[:, None]
    table_means = jnp.einsum("rt,rf->tf", picked_all, feat_all, precision=highest) / counts
    excess = (
        jnp.einsum("rt,rf->tf", picked_all, feat_all * feat_all, precision=highest) / counts
        - table_means * table_means
    )
    scales = lax.rsqrt(jnp.maximum(excess, spread_floor))
    centred = feat_half - jnp.dot(member, table_means, precision=highest)
    scale_rows = jnp.dot(member, scales, precision=highest)
    normed = (centred * scale_rows).astype(bf16)
    current = dot(normed, enc_w, ((1,), (0,))) + enc_b
    allowed = ((code_own >> 1)[:, None] == (code_keys >> 1)[None, :]) & ((code_keys & 1) > 0)[None, :]
    scaling = 1.0 / math.sqrt(HD)

    saved = []
    for l in range(layers):
        wq, wo, wu, wd = weights[l]
        low = current.astype(bf16)
        queries = (dot(low, wq[0], ((1,), (0,))) + bqv_all[l, 0]).astype(bf16)
        keys = dot(low, wq[1], ((1,), (0,))).astype(bf16)
        values = (dot(low, wq[2], ((1,), (0,))) + bqv_all[l, 1]).astype(bf16)
        kv = jnp.concatenate([keys, values], 1)
        kv_all = jnp.concatenate([kv, swap_dp(kv, 1)])
        mixes, probs_all = [], []
        for h in range(heads):
            qh = queries[:, h * HD : (h + 1) * HD]
            kh = kv_all[:, h * HD : (h + 1) * HD]
            vh = kv_all[:, d + h * HD : d + (h + 1) * HD]
            scores = jnp.where(allowed, dot(qh, kh, ((1,), (1,))) * scaling, -1e30)
            e = jnp.exp(scores - jnp.max(scores, -1, keepdims=True))
            probs = e / jnp.sum(e, -1, keepdims=True)
            probs_all.append(probs)
            mixes.append(dot(probs.astype(bf16), vh, ((1,), (0,))))
        mixture = jnp.concatenate(mixes, 1).astype(bf16)
        before_middle = current + dot(mixture, wo, ((1,), (0,))) + out_bias[l, 0]
        n1, inv1 = layer_norm_parts(before_middle)
        middle = n1 * ln_gain[l, 0] + ln_bias[l, 0]
        middle_low = middle.astype(bf16)
        hidden = dot(middle_low, wu, ((1,), (0,))) + bup_all[l]
        act = gelu_exact(hidden).astype(bf16)
        before_out = middle + dot(act, wd, ((1,), (0,))) + out_bias[l, 1]
        n2, inv2 = layer_norm_parts(before_out)
        current = n2 * ln_gain[l, 1] + ln_bias[l, 1]
        saved.append((low, queries, kv_all, probs_all, mixture, n1, inv1, middle_low, hidden, act, n2, inv2))
    final_rows = from_sequences(current.astype(bf16), z)

    grad = cot_half.astype(f32)
    packs, vectors = [None] * layers, [None] * layers
    for l in reversed(range(layers)):
        low, queries, kv_all, probs_all, mixture, n1, inv1, middle_low, hidden, act, n2, inv2 = saved[l]
        wq, wo, wu, wd = weights[l]
        g_before_out, g_gain1, g_shift1 = layer_norm_back(grad, n2, inv2, ln_gain[l, 1])
        g_ffn = g_before_out.astype(bf16)
        d_down = dot(act, g_ffn, ((0,), (0,)))
        g_act = dot(g_ffn, wd, ((1,), (1,)))
        g_hidden = jax.vjp(gelu_exact, hidden)[1](g_act)[0].astype(bf16)
        d_bup = jnp.sum(g_hidden.astype(f32), 0)
        d_up = dot(middle_low, g_hidden, ((0,), (0,)))
        g_middle = g_before_out + dot(g_hidden, wu, ((1,), (1,)))
        g_before_middle, g_gain0, g_shift0 = layer_norm_back(g_middle, n1, inv1, ln_gain[l, 0])
        g_attn = g_before_middle.astype(bf16)
        d_out = dot(mixture, g_attn, ((0,), (0,)))
        g_mix = dot(g_attn, wo, ((1,), (1,))).astype(bf16)
        gq, gk, gv = [], [], []
        for h in range(heads):
            cols = slice(h * HD, (h + 1) * HD)
            kh, vh = kv_all[:, cols], kv_all[:, d + h * HD : d + (h + 1) * HD]
            probs = probs_all[h]
            g_probs = dot(g_mix[:, cols], vh, ((1,), (1,)))
            g_scores = (probs * (g_probs - jnp.sum(probs * g_probs, -1, keepdims=True))).astype(bf16)
            gq.append(dot(g_scores, kh, ((1,), (0,))) * scaling)
            gk.append(dot(g_scores, queries[:, cols], ((0,), (0,))) * scaling)
            gv.append(dot(probs.astype(bf16), g_mix[:, cols], ((0,), (0,))))
        g_queries = jnp.concatenate(gq, 1).astype(bf16)
        g_kv = jnp.concatenate(gk + gv, 1)
        g_kv = (g_kv[:half] + swap_dp(g_kv[half:].astype(bf16), 1).astype(f32)).astype(bf16)
        g_proj = jnp.concatenate([g_queries, g_kv], 1)
        d_qkv = dot(low, g_proj, ((0,), (0,)))
        g_proj_sum = jnp.sum(g_proj.astype(f32), 0)
        d_bqv = jnp.stack([g_proj_sum[:d], g_proj_sum[2 * d :]])
        wcat = jnp.concatenate([wq[0], wq[1], wq[2]], 1)
        grad = g_before_middle + dot(g_proj, wcat, ((1,), (1,)))
        packs[l] = jnp.stack(
            [
                pack_local(
                    jnp.stack([d_qkv[:, c * d + zz * HD : c * d + (zz + 1) * HD] for c in range(3)]),
                    d_out[zz * HD : (zz + 1) * HD],
                    d_up[:, zz * f_part : (zz + 1) * f_part],
                    d_down[zz * f_part : (zz + 1) * f_part],
                )
                for zz in range(width)
            ],
            1,
        ).astype(bf16)
        vectors[l] = jnp.concatenate(
            [
                jnp.stack([g_gain0, g_gain1, g_shift0, g_shift1]),
                jnp.stack([jnp.sum(g_attn.astype(f32), 0), jnp.sum(g_ffn.astype(f32), 0)]),
                d_bqv,
                d_bup.reshape(-1, d),
            ]
        )
    g_low = grad.astype(bf16)
    d_enc_b = jnp.sum(g_low.astype(f32), 0)
    d_enc_w = dot(normed, g_low, ((0,), (0,)))
    g_normed = dot(g_low, enc_w, ((1,), (1,)))
    sums = jnp.concatenate(
        [
            jnp.einsum("rt,rf->tf", member, g_normed, precision=highest),
            jnp.einsum("rt,rf->tf", member, g_normed * centred, precision=highest),
        ]
    )
    sums = sums + swap_dp(sums, 1)
    sum_plain, sum_centred = sums[:NTAB], sums[NTAB:]
    g_excess = jnp.where(excess > spread_floor, -0.5 * scales * scales * scales * sum_centred, 0.0)
    g_means = -scales * sum_plain - 2.0 * table_means * g_excess
    g_features = (
        g_normed * scale_rows
        + jnp.dot(picked, g_means / counts, precision=highest)
        + 2.0 * feat_half * jnp.dot(picked, g_excess / counts, precision=highest)
    )
    grad_features = from_sequences(g_features, z)

    per = vectors[0].shape[0]
    rows = jnp.concatenate(vectors + [d_enc_b[None], d_enc_w])
    used = rows.shape[0]
    pad = -used % 16
    shared = jnp.pad(rows, ((0, pad), (0, 0))).reshape(8, -1, HD)
    outs = [None] * layers
    for l in reversed(range(layers)):
        pieces, rest = reduce_grads(packs[l], shared if l == 0 else None, p, o, z)
        outs[l] = unpack_local(pieces, d, f_part)
    rows = rest.reshape(used + pad, d)[:used]
    vec = rows[: layers * per].reshape(layers, per, d)
    d_bqv = lax.dynamic_slice_in_dim(vec[:, 6:8], z * HD, HD, 2)
    d_bup = lax.dynamic_slice_in_dim(vec[:, 8:].reshape(layers, f_all), z * f_part, f_part, 1)
    return (
        final_rows,
        grad_features,
        rows[layers * per + 1 :],
        rows[layers * per],
        jnp.stack([e[0] for e in outs]),
        d_bqv,
        jnp.stack([e[1] for e in outs]),
        vec[:, 4:6],
        vec[:, 0:2],
        vec[:, 2:4],
        jnp.stack([e[2] for e in outs]),
        d_bup,
        jnp.stack([e[3] for e in outs]),
    )


def solution(mesh):
    rows, ids = P("tensor", "dp", None), P(None, "dp")
    qkv, bqv = P(None, None, None, "tensor"), P(None, None, "tensor")
    mid, last = P(None, "tensor", None), P(None, None, "tensor")
    in_specs = (rows, ids, ids, P(), P(), qkv, bqv, mid, P(), P(), P(), last, P(None, "tensor"), mid, rows)
    out_specs = (rows, rows, P(), P(), qkv, bqv, mid, P(), P(), P(), last, P(None, "tensor"), mid)
    return jax.shard_map(local, mesh=mesh, in_specs=in_specs, out_specs=out_specs, check_vma=False)
```

```python
import functools
import math

import jax
import jax.numpy as jnp
from jax import lax
from jax.experimental import pallas as pl
from jax.experimental.pallas import tpu as pltpu
from jax.sharding import PartitionSpec as P

HD = 128
NTAB = 5
spread_floor = 0.1
norm_eps = 1e-05
f32 = jnp.float32
bf16 = jnp.bfloat16
LOG2E = 1.4426950408889634
MIB = 1024 * 1024


def mm(a, b):
    return lax.dot_general(a, b, (((1,), (0,)), ((), ())), preferred_element_type=f32)


def mm_nt(a, b):
    return lax.dot_general(a, b, (((1,), (1,)), ((), ())), preferred_element_type=f32)


def mm_tn(a, b):
    return lax.dot_general(a, b, (((0,), (0,)), ((), ())), preferred_element_type=f32)


def call(body, outs, args, scratch=(), flops=0, name=None):
    shapes = [jax.ShapeDtypeStruct(shape, dtype) for shape, dtype in outs]
    moved = sum(a.size * a.dtype.itemsize for a in args) + sum(s.size * s.dtype.itemsize for s in shapes)
    vmem = pl.BlockSpec(memory_space=pltpu.VMEM)
    return pl.pallas_call(
        body,
        out_shape=shapes,
        in_specs=[pl.BlockSpec(memory_space=pltpu.SMEM)] + [vmem] * (len(args) - 1),
        out_specs=[vmem] * len(shapes),
        scratch_shapes=[pltpu.VMEM(shape, dtype) for shape, dtype in scratch],
        compiler_params=pltpu.CompilerParams(vmem_limit_bytes=56 * MIB),
        cost_estimate=pl.CostEstimate(flops=flops, bytes_accessed=moved, transcendentals=0),
        name=name,
    )(*args)


def blocks(kind, d, f_part, q, z):
    if kind == "qkv":
        n = d // 8
        return [(c * n, n, q * n, c * d + z * HD) for c in range(3)]
    if kind == "out":
        n = HD // 8
        return [(c * n, n, z * HD + q * n, c * HD) for c in range(d // HD)]
    if kind == "up":
        n = d // 8
        return [(c * n, n, q * n, z * f_part + c * HD) for c in range(f_part // HD)]
    n = f_part // 8
    return [(c * n, n, z * f_part + q * n, c * HD) for c in range(d // HD)]


def aligned(value, unit):
    return value if isinstance(value, int) else pl.multiple_of(value, unit)


def unpack(pos, halves, row0, kind, whole, d, f_part):
    for c in range(2):
        src = halves[c]

        def step(e, carry, src=src, c=c):
            q = pos[c * 4 + e]
            for k in range(src.shape[1]):
                for at, n, row, col in blocks(kind, d, f_part, q, pos[8 + k]):
                    whole[pl.ds(aligned(row, 16), n), pl.ds(aligned(col, HD), HD)] = src[
                        e, k, row0 + at : row0 + at + n, :
                    ]
            return carry

        lax.fori_loop(0, 4, step, 0)


def pack(pos, whole, row0, kind, halves, d, f_part, width, piece):
    for c in range(2):
        dst = halves[c]

        def step(e, carry, dst=dst, c=c):
            q = pos[c * 4 + e]
            for k in range(width):
                for at, n, row, col in blocks(kind, d, f_part, q, pos[8 + k]):
                    at += k * piece + row0
                    dst[e, at : at + n, :] = whole[
                        pl.ds(aligned(row, 16), n), pl.ds(aligned(col, HD), HD)
                    ]
            return carry

        lax.fori_loop(0, 4, step, 0)


def pack_kernel(pos, wqkv, wout, wup, wdown, bqv, bup, g0, g1, g2):
    q = pos[0]
    d, f_part = wqkv.shape[2], wup.shape[2]
    n, m, r = d // 8, HD // 8, f_part // 8
    for l in range(2):
        qkv_to, rest_to, base = (g0, g1, 0) if l == 0 else (g2, g2, 3 * n)
        for c in range(3):
            qkv_to[c * n : (c + 1) * n, :] = wqkv[l, c, pl.ds(pl.multiple_of(q * n, 16), n), :]
        for c in range(d // HD):
            rest_to[base + c * m : base + (c + 1) * m, :] = wout[
                l, pl.ds(pl.multiple_of(q * m, 16), m), c * HD : (c + 1) * HD
            ]
        base += d // HD * m
        for c in range(f_part // HD):
            rest_to[base + c * n : base + (c + 1) * n, :] = wup[
                l, pl.ds(pl.multiple_of(q * n, 16), n), c * HD : (c + 1) * HD
            ]
        base += f_part // HD * n
        for c in range(d // HD):
            rest_to[base + c * r : base + (c + 1) * r, :] = wdown[
                l, pl.ds(pl.multiple_of(q * r, 16), r), c * HD : (c + 1) * HD
            ]
    rows = jnp.concatenate([bqv[...], bup[...]], 0)
    high = rows.astype(bf16)
    g0[3 * n :, :] = jnp.concatenate([high, (rows - high.astype(f32)).astype(bf16)], 0)


def erf(x):
    x = jnp.clip(x, -3.7439211627767994, 3.7439211627767994)
    y = x * x
    top = 2.2905065861350646e-4
    for c in (3.4082910107109506e-3, 5.0955695062380861e-2, 1.8520832239976145e-1, 1.128379143519084):
        top = top * y + c
    low = -1.1791602954361697e-7
    for c in (
        2.3547966471313185e-5,
        1.0179625278914885e-3,
        1.4070470171167667e-2,
        1.1098505178285362e-1,
        4.9746925110067538e-1,
        1.0,
    ):
        low = low * y + c
    return x * top / low


def gelu_pair(h):
    cdf = 0.5 + 0.5 * erf(h * math.sqrt(0.5))
    return h * cdf, cdf + h * (jnp.exp2(h * h * (-0.5 * LOG2E)) * (1.0 / math.sqrt(2.0 * math.pi)))


def normalize(u):
    centre = u - jnp.mean(u, -1, keepdims=True)
    inv = lax.rsqrt(jnp.mean(centre * centre, -1, keepdims=True) + norm_eps)
    return centre * inv, inv


def norm_back(grad, normal, inv, gain):
    e = grad * gain
    return (e - jnp.mean(e, -1, keepdims=True) - normal * jnp.mean(e * normal, -1, keepdims=True)) * inv


def rowsum(x):
    return jnp.sum(x, 0, keepdims=True)


def features_kernel(pos, fa, fb, ca, cb, encw, encb, cur, low, normed, stats):
    own, other = fa[...], fb[...]
    code_a, code_b = ca[...], cb[...]
    mean_rows = jnp.zeros_like(own)
    scale_rows = jnp.zeros_like(own)
    for t in range(NTAB):
        pa = (code_a == 2 * t + 1).astype(f32)
        pb = (code_b == 2 * t + 1).astype(f32)
        count = rowsum(pa) + rowsum(pb)
        mean = (rowsum(pa * own) + rowsum(pb * other)) / count
        da, db = own - mean, other - mean
        excess = (rowsum(pa * da * da) + rowsum(pb * db * db)) / count
        scale = lax.rsqrt(jnp.maximum(excess, spread_floor))
        stats[t : t + 1, :] = mean
        stats[8 + t : 9 + t, :] = scale
        stats[16 + t : 17 + t, :] = excess
        stats[24 + t : 25 + t, :] = jnp.broadcast_to(count, mean.shape)
        here = (code_a >> 1) == t
        mean_rows = jnp.where(here, mean, mean_rows)
        scale_rows = jnp.where(here, scale, scale_rows)
    z = ((own - mean_rows) * scale_rows).astype(bf16)
    normed[...] = z
    out = mm(z, encw[...]) + encb[...]
    cur[...] = out
    low[...] = out.astype(bf16)


def project(x, w, bias, q, kv, layer, d):
    q[...] = (mm(x, w[:, :d]) + bias[2 * layer : 2 * layer + 1, :]).astype(bf16)
    kv[:, :d] = mm(x, w[:, d : 2 * d]).astype(bf16)
    kv[:, d:] = (mm(x, w[:, 2 * d :]) + bias[2 * layer + 1 : 2 * layer + 2, :]).astype(bf16)


def qkv_first_kernel(pos, low, ga, gb, q, kv, w, bqv, bup):
    d = low.shape[1]
    unpack(pos, (ga, gb), 0, "qkv", w, d, 0)
    base = 3 * d // 8
    f_part = 2 * HD
    for k in range(ga.shape[1]):
        z = pos[8 + k]
        rows = ga[0, k, base : base + 16, :].astype(f32)
        rows = rows[:8] + rows[8:]
        for j in range(4):
            bqv[j : j + 1, pl.ds(pl.multiple_of(z * HD, HD), HD)] = rows[j : j + 1]
            col = z * f_part + (j % 2) * HD
            bup[j // 2 : j // 2 + 1, pl.ds(pl.multiple_of(col, HD), HD)] = rows[4 + j : 5 + j]
    project(low[...], w, bqv, q, kv, 0, d)


def qkv_next_kernel(pos, low, ga, gb, bqv, q, kv, w):
    d = low.shape[1]
    unpack(pos, (ga, gb), 0, "qkv", w, d, 0)
    project(low[...], w, bqv, q, kv, 1, d)


def attention_rows(rows, q, kva, kvb, bias, mix, lse, d):
    n = kva.shape[0]
    factor = LOG2E / math.sqrt(HD)
    count = rows.size
    lane = lax.broadcasted_iota(jnp.int32, (count, HD), 1)
    totals = jnp.zeros((count, HD), f32)
    for h in range(d // HD):
        cols = slice(h * HD, (h + 1) * HD)
        vals = slice(d + h * HD, d + (h + 1) * HD)
        qh = q[rows, cols]
        ta = mm_nt(qh, kva[:, cols]) * factor + bias[rows, :n]
        tb = mm_nt(qh, kvb[:, cols]) * factor + bias[rows, n:]
        top = jnp.maximum(jnp.max(ta, -1, keepdims=True), jnp.max(tb, -1, keepdims=True))
        ea, eb = jnp.exp2(ta - top), jnp.exp2(tb - top)
        total = jnp.sum(ea, -1, keepdims=True) + jnp.sum(eb, -1, keepdims=True)
        out = mm(ea.astype(bf16), kva[:, vals]) + mm(eb.astype(bf16), kvb[:, vals])
        mix[rows, cols] = out / total
        totals = jnp.where(lane == h, top + jnp.log2(total), totals)
    lse[rows, :] = totals


def layer_rows(rows, cur, mix, wo, wu, wd, bup, ob, lg, lb, layer, n1, inv1, act, dgel, n2, inv2):
    l = layer
    u = cur + mm(mix[rows, :].astype(bf16), wo[...]) + ob[2 * l : 2 * l + 1, :]
    normal, inv = normalize(u)
    n1[rows, :] = normal
    inv1[rows, :] = jnp.broadcast_to(inv, (rows.size, HD))
    middle = normal * lg[2 * l : 2 * l + 1, :] + lb[2 * l : 2 * l + 1, :]
    hidden = mm(middle.astype(bf16), wu[...]) + bup[l : l + 1, :]
    value, slope = gelu_pair(hidden)
    value = value.astype(bf16)
    act[rows, :] = value
    dgel[rows, :] = slope.astype(bf16)
    u = middle + mm(value, wd[...]) + ob[2 * l + 1 : 2 * l + 2, :]
    normal, inv = normalize(u)
    n2[rows, :] = normal
    inv2[rows, :] = jnp.broadcast_to(inv, (rows.size, HD))
    return normal * lg[2 * l + 1 : 2 * l + 2, :] + lb[2 * l + 1 : 2 * l + 2, :]


def set_bias(bias, col, row):
    bias[...] = jnp.where(col[...] == row[...], 0.0, -1e30)


def first_layer_kernel(
    pos, q, kva, kvb, col, row, cur, ga, gb, bup, ob, lg, lb,
    mix, lse, n1, inv1, act, dgel, n2, inv2, low, wo, wu, wd,
    bias, raw,
):
    d = q.shape[1]
    f_part = wu.shape[1] // ga.shape[1]
    m = HD // 8 * (d // HD)
    unpack(pos, (ga, gb), 0, "out", wo, d, f_part)
    unpack(pos, (ga, gb), m, "up", wu, d, f_part)
    unpack(pos, (ga, gb), m + d // 8 * (f_part // HD), "down", wd, d, f_part)
    set_bias(bias, col, row)

    def step(i, carry):
        rows = pl.ds(pl.multiple_of(i * CHUNK, CHUNK), CHUNK)
        attention_rows(rows, q, kva, kvb, bias, mix, raw, d)
        out = layer_rows(
            rows, cur[rows, :], mix, wo, wu, wd, bup, ob, lg, lb, 0, n1, inv1, act, dgel, n2, inv2
        )
        low[rows, :] = out.astype(bf16)
        return carry

    lax.fori_loop(0, q.shape[0] // CHUNK, step, 0)
    lse[...] = raw[...].T[:8]


CHUNK = 256


def ffn_back(
    pos, grad, l, n1, inv1, act, dgel, n2, inv2, mix, wo, wu, wd, lg, lb,
    gmix, gbm, keep, send, vec, vrow, base, gl, gh, g1, dw, d, f_part, width, piece,
):
    gain0, gain1 = lg[2 * l : 2 * l + 1, :], lg[2 * l + 1 : 2 * l + 2, :]
    shift0 = lb[2 * l : 2 * l + 1, :]
    f = wu.shape[1]

    def step(i, carry):
        rows = pl.ds(pl.multiple_of(i * CHUNK, CHUNK), CHUNK)
        top = grad[rows, :].astype(f32)
        normal = n2[rows, :]
        bo = norm_back(top, normal, inv2[rows, :1], gain1)
        low = bo.astype(bf16)
        gl[rows, :] = low
        back = mm_nt(low, wd[...])
        back = (back * dgel[rows, :].astype(f32)).astype(bf16)
        gh[rows, :] = back
        gm = bo + mm_nt(back, wu[...])
        first = n1[rows, :]
        bm = norm_back(gm, first, inv1[rows, :1], gain0)
        gbm[rows, :] = bm
        attn = bm.astype(bf16)
        g1[rows, :] = attn
        gmix[rows, :] = mm_nt(attn, wo[...]).astype(bf16)
        sums = (
            rowsum(gm * first),
            rowsum(top * normal),
            rowsum(gm),
            rowsum(top),
            rowsum(attn.astype(f32)),
            rowsum(low.astype(f32)),
        )
        hidden = rowsum(back.astype(f32))
        for j in range(6):
            vec[vrow + j : vrow + j + 1, :] += sums[j]
        for j in range(f // d):
            at = vrow + 8 + j
            vec[at : at + 1, :] += hidden[:, j * d : (j + 1) * d]
        return carry

    lax.fori_loop(0, act.shape[0] // CHUNK, step, 0)
    m = HD // 8 * (d // HD)
    dw[:f, :d] = mm_tn(act[...], gl[...]).astype(bf16)
    pack(pos, dw, base + m + d // 8 * (f_part // HD), "down", (keep, send), d, f_part, width, piece)
    middle = (n1[...] * gain0 + shift0).astype(bf16)
    dw[:d, :f] = mm_tn(middle, gh[...]).astype(bf16)
    pack(pos, dw, base + m, "up", (keep, send), d, f_part, width, piece)
    dw[:d, :d] = mm_tn(mix[...].astype(bf16), g1[...]).astype(bf16)
    pack(pos, dw, base, "out", (keep, send), d, f_part, width, piece)


def last_layer_kernel(
    pos, q, kva, kvb, col, row, n2in, ga, gb, bup, ob, lg, lb, cot,
    mix, lse, final, gmix, gbm, keep, send, vec,
    bias, raw, wo, wu, wd, n1, inv1, act, dgel, n2, inv2, gl, gh, g1, dw,
):
    d = q.shape[1]
    f_part = wu.shape[1] // ga.shape[1]
    m = HD // 8 * (d // HD)
    first = 3 * d // 8
    unpack(pos, (ga, gb), first, "out", wo, d, f_part)
    unpack(pos, (ga, gb), first + m, "up", wu, d, f_part)
    unpack(pos, (ga, gb), first + m + d // 8 * (f_part // HD), "down", wd, d, f_part)
    set_bias(bias, col, row)

    def step(i, carry):
        rows = pl.ds(pl.multiple_of(i * CHUNK, CHUNK), CHUNK)
        attention_rows(rows, q, kva, kvb, bias, mix, raw, d)
        cur = n2in[rows, :] * lg[1:2, :] + lb[1:2, :]
        out = layer_rows(
            rows, cur, mix, wo, wu, wd, bup, ob, lg, lb, 1, n1, inv1, act, dgel, n2, inv2
        )
        final[rows, :] = out.astype(bf16)
        return carry

    lax.fori_loop(0, q.shape[0] // CHUNK, step, 0)
    lse[...] = raw[...].T[:8]
    vec[...] = jnp.zeros_like(vec)
    ffn_back(
        pos, cot, 1, n1, inv1, act, dgel, n2, inv2, mix, wo, wu, wd, lg, lb,
        gmix, gbm, keep, send, vec, 0, 0, gl, gh, g1, dw, d, f_part, ga.shape[1], keep.shape[1] // ga.shape[1],
    )


def attention_back_kernel(pos, q, kva, kvb, mix, gmix, lse, col, row, dq, dkva, dkvb, bias, acc):
    d = q.shape[1]
    n = kva.shape[0]
    scaling = 1.0 / math.sqrt(HD)
    factor = LOG2E * scaling
    bias[...] = jnp.where(col[...] == row[...], 0.0, -1e30)
    block = 256
    for h in range(d // HD):
        cols = slice(h * HD, (h + 1) * HD)
        vals = slice(d + h * HD, d + (h + 1) * HD)
        qh, gh = q[:, cols], gmix[:, cols]
        prod = gh.astype(f32) * mix[:, cols]
        delta = jnp.sum(prod.T, 0, keepdims=True)
        base = lse[h : h + 1, :]
        acc[...] = jnp.zeros_like(acc)
        for src, dst, off in ((kva, dkva, 0), (kvb, dkvb, n)):

            def step(i, carry, src=src, dst=dst, off=off):
                rows = pl.ds(pl.multiple_of(i * block, block), block)
                kh, vh = src[rows, cols], src[rows, vals]
                brow = pl.ds(pl.multiple_of(off + i * block, block), block)
                probs = jnp.exp2(mm_nt(kh, qh) * factor + bias[brow, :] - base)
                ds = (probs * (mm_nt(vh, gh) - delta)).astype(bf16)
                dst[rows, vals] = mm(probs.astype(bf16), gh).astype(dst.dtype)
                dst[rows, cols] = (mm(ds, qh) * scaling).astype(dst.dtype)
                acc[...] += mm_tn(kh, ds)
                return carry

            lax.fori_loop(0, n // block, step, 0)
        dq[:, cols] = (acc[...].T * scaling).astype(bf16)


def projection_back(pos, dq, dkva, dkvr, low, w, gbm, proj, dw, keep, send, vec, vrow, d, width, piece):
    proj[:, :d] = dq[...]
    proj[:, d:] = (dkva[...] + dkvr[...].astype(f32)).astype(bf16)
    dw[:d, : 3 * d] = mm_tn(low, proj[...]).astype(bf16)
    pack(pos, dw, 0, "qkv", (keep, send), d, 0, width, piece)
    vec[vrow : vrow + 1, :] = rowsum(dq[...].astype(f32))
    vec[vrow + 1 : vrow + 2, :] = rowsum(proj[:, 2 * d :].astype(f32))
    return gbm[...] + mm_nt(proj[...], w[...])


def middle_kernel(
    pos, dq, dkva, dkvr, w1, gbm1, n2, vec1, n1, inv1, act, dgel, inv2, mix, wo, wu, wd, lg, lb,
    gmix, gbm, keep, send, vec,
    proj, dw, grad, gl, gh, g1,
):
    d = dq.shape[1]
    width = d // HD
    piece = keep.shape[1] // width
    f_part = wu.shape[1] // width
    vec[...] = jnp.zeros_like(vec)
    for j in range(10):
        vec[10 + j : 11 + j, :] = vec1[j : j + 1, :]
    low1 = (n2[...] * lg[1:2, :] + lb[1:2, :]).astype(bf16)
    grad[...] = projection_back(
        pos, dq, dkva, dkvr, low1, w1, gbm1, proj, dw, keep, send, vec, 16, d, width, piece
    )
    ffn_back(
        pos, grad, 0, n1, inv1, act, dgel, n2, inv2, mix, wo, wu, wd, lg, lb,
        gmix, gbm, keep, send, vec, 0, 3 * d // 8, gl, gh, g1, dw, d, f_part, width, piece,
    )


def entry_kernel(
    pos, dq, dkva, dkvr, low0, w0, gbm0, vec, normed, fa, ca, stats, encw,
    keep, send, gnorm, sums,
    proj, dw, shared,
):
    d = dq.shape[1]
    features = encw.shape[0]
    width = d // HD
    first = 3 * d // 8
    shared[...] = jnp.zeros_like(shared)
    shared[:24, :] = vec[...]
    grad = projection_back(
        pos, dq, dkva, dkvr, low0[...], w0, gbm0, proj, dw, keep, send, shared, 6, d, width, first
    )
    low = grad.astype(bf16)
    shared[20:21, :] = rowsum(low.astype(f32))
    shared[24 : 24 + features, :] = mm_tn(normed[...], low)
    back = mm_nt(low, encw[...])
    gnorm[...] = back
    code = ca[...] >> 1
    centred = fa[...]
    sums[...] = jnp.zeros_like(sums)
    for t in range(NTAB):
        here = code == t
        part = jnp.where(here, back, 0.0)
        sums[t : t + 1, :] = rowsum(part)
        sums[8 + t : 9 + t, :] = rowsum(part * (centred - stats[t : t + 1, :]))
    share = shared.shape[0] // 8
    for c, dst in ((0, keep), (1, send)):

        def step(e, carry, dst=dst, c=c):
            row = pl.multiple_of(pos[c * 4 + e] * share, 8)
            for j in range(d // HD):
                piece = shared[pl.ds(row, share), j * HD : (j + 1) * HD].astype(bf16)
                at = width * first + j * share
                dst[e, at : at + share, :] = piece
            return carry

        lax.fori_loop(0, 4, step, 0)


def features_back_kernel(pos, gnorm, fa, ca, stats, mine, theirs, out):
    total = mine[...] + theirs[...]
    code = ca[...]
    x, back = fa[...], gnorm[...]
    scale_rows = jnp.zeros_like(x)
    flat = jnp.zeros_like(x)
    slope = jnp.zeros_like(x)
    for t in range(NTAB):
        mean, scale = stats[t : t + 1, :], stats[8 + t : 9 + t, :]
        excess, count = stats[16 + t : 17 + t, :], stats[24 + t : 25 + t, :]
        plain, centred = total[t : t + 1, :], total[8 + t : 9 + t, :]
        g_excess = jnp.where(excess > spread_floor, -0.5 * scale * scale * scale * centred, 0.0)
        g_mean = -scale * plain - 2.0 * mean * g_excess
        scale_rows = jnp.where((code >> 1) == t, scale, scale_rows)
        chosen = code == 2 * t + 1
        flat = jnp.where(chosen, g_mean / count, flat)
        slope = jnp.where(chosen, 2.0 * g_excess / count, slope)
    out[...] = back * scale_rows + flat + x * slope


def result_kernel(pos, a1, b1, a2, b2, a3, b3, gqkv, gout, gup, gdown, rows):
    d, f_part = gqkv.shape[2], gup.shape[2]
    n, m, r = d // 8, HD // 8, f_part // 8
    first = 3 * n
    share = rows.shape[0] // 8

    def rest(l, src, e, q, base):
        for c in range(d // HD):
            gout[l, pl.ds(pl.multiple_of(q * m, 16), m), c * HD : (c + 1) * HD] = src[
                e, base + c * m : base + (c + 1) * m, :
            ].astype(f32)
        base += d // HD * m
        for c in range(f_part // HD):
            gup[l, pl.ds(pl.multiple_of(q * n, 16), n), c * HD : (c + 1) * HD] = src[
                e, base + c * n : base + (c + 1) * n, :
            ].astype(f32)
        base += f_part // HD * n
        for c in range(d // HD):
            gdown[l, pl.ds(pl.multiple_of(q * r, 16), r), c * HD : (c + 1) * HD] = src[
                e, base + c * r : base + (c + 1) * r, :
            ].astype(f32)

    for half, (one, two, three) in enumerate(((a1, a2, a3), (b1, b2, b3))):

        def step(e, carry, half=half, one=one, two=two, three=three):
            q = pos[half * 4 + e]
            for l, src in ((1, two), (0, three)):
                for c in range(3):
                    gqkv[l, c, pl.ds(pl.multiple_of(q * n, 16), n), :] = src[
                        e, c * n : (c + 1) * n, :
                    ].astype(f32)
            rest(1, one, e, q, 0)
            rest(0, two, e, q, first)
            for j in range(d // HD):
                rows[pl.ds(pl.multiple_of(q * share, 8), share), j * HD : (j + 1) * HD] = three[
                    e, first + j * share : first + (j + 1) * share, :
                ].astype(f32)
            return carry

        lax.fori_loop(0, 4, step, 0)


def swap_dp(values, even, odd=None):
    size = lax.axis_size("dp")
    odd = even if odd is None else odd
    return lax.ppermute(values, "dp", [(i, i ^ (odd if i % 2 else even)) for i in range(size)])


def swap_z(values, mask):
    size = lax.axis_size("tensor")
    return lax.ppermute(values, "tensor", [(i, i ^ mask) for i in range(size)])


def relay_pairs(step):
    size, width = lax.axis_size("dp"), lax.axis_size("tensor")
    pairs = []
    for i in range(size):
        for z in range(width):
            target = (i - i % 2 + z // 2) * width + 2 * (i % 2) + (step ^ (z & 1))
            pairs.append((i * width + z, target))
    return pairs


def pick(values, index, axis=0):
    return lax.dynamic_index_in_dim(values, index, axis, keepdims=False)


def to_sequences(values, z):
    got = [
        lax.ppermute(pick(values, step ^ (z & 1), 1), ("dp", "tensor"), relay_pairs(step)) for step in range(2)
    ]
    return jnp.concatenate(got)


def from_sequences(values, z):
    part = values.shape[0] // 2
    got = [
        lax.ppermute(
            values[step * part : (step + 1) * part],
            ("dp", "tensor"),
            [(b, a) for a, b in relay_pairs(step)],
        )
        for step in range(2)
    ]
    odd = (z & 1) == 1
    return jnp.stack([jnp.where(odd, got[1], got[0]), jnp.where(odd, got[0], got[1])], 1)


def gather_pieces(piece):
    width = lax.axis_size("tensor")
    rows = jnp.stack([piece] + [swap_z(piece, k) for k in range(1, width)])
    two = jnp.stack([rows, swap_dp(rows, 4, 2)])
    four = jnp.concatenate([two, swap_dp(two, 2, 4)])
    return four, swap_dp(four, 1)


def reduce_pieces(keep, send, rows):
    width = lax.axis_size("tensor")
    four = (keep.astype(f32) + swap_dp(send, 1).astype(f32)).astype(bf16)
    two = (four[:2].astype(f32) + swap_dp(four[2:], 2, 4).astype(f32)).astype(bf16)
    one = (two[0].astype(f32) + swap_dp(two[1], 4, 2).astype(f32)).astype(bf16)
    mask = 8
    while mask < lax.axis_size("dp"):
        one = (one.astype(f32) + swap_dp(one, mask).astype(f32)).astype(bf16)
        mask *= 2

    def share(k):
        part = one[k * rows : (k + 1) * rows]
        return jnp.concatenate([part, one[width * rows :]]) if one.shape[0] > width * rows else part

    total = share(0).astype(f32)
    for k in range(1, width):
        total = total + swap_z(share(k), k).astype(f32)
    piece = total.astype(bf16)
    two = jnp.stack([piece, swap_dp(piece, 4, 2)])
    four = jnp.concatenate([two, swap_dp(two, 2, 4)])
    return four, swap_dp(four, 1)


def local(
    features,
    table_ids,
    train_flags,
    enc_w,
    enc_b,
    w_qkv,
    b_qv,
    w_out,
    out_bias,
    ln_gain,
    ln_bias,
    w_up,
    b_up,
    w_down,
    cotangent,
):
    part, _, fdim = features.shape
    width = lax.axis_size("tensor")
    layers, d, f_part = w_qkv.shape[0], w_qkv.shape[2], w_up.shape[2]
    f = f_part * width
    half = 2 * part
    n = 2 * half
    di, z = lax.axis_index("dp"), lax.axis_index("tensor")
    p, ox, oy = di & 1, (di >> 1) & 1, (di >> 2) & 1
    table = []
    for c in range(2):
        for r1 in range(2):
            for r2 in range(2):
                pd = p ^ c
                rx, ry = jnp.where(pd == 0, r1, r2), jnp.where(pd == 0, r2, r1)
                table.append(pd * 4 + (oy ^ ry) * 2 + (ox ^ rx))
    pos = jnp.stack(table + [z ^ k for k in range(width)]).astype(jnp.int32)
    rest = HD // 8 * (d // HD) + d // 8 * (f_part // HD) + f_part // 8 * (d // HD)
    first = 3 * d // 8

    feat_own = to_sequences(features, z)
    feat_other = swap_dp(feat_own, 1)
    g0, g1, g2 = call(
        pack_kernel,
        [((first + 16, HD), bf16), ((rest, HD), bf16), ((first + rest, HD), bf16)],
        [pos, w_qkv, w_out, w_up, w_down, b_qv.reshape(-1, HD), b_up.reshape(-1, HD)],
        name="pack_weights",
    )
    w0a, w0b = gather_pieces(g0)
    w1a, w1b = gather_pieces(g1)
    w2a, w2b = gather_pieces(g2)
    codes = (table_ids * 2 + train_flags).T
    codes = pick(jnp.where(p == z // 2, codes, swap_dp(codes, 1)), z & 1).reshape(2, 2, part)
    codes = jnp.where((z & 1) == 1, codes[:, ::-1], codes).reshape(2, half)
    code_own, code_other = pick(codes, p), pick(codes, 1 - p)
    keys = jnp.concatenate([code_own, code_other])
    key_table = jnp.where((keys & 1) == 1, keys >> 1, -1)
    own_col, other_col = code_own[:, None], code_other[:, None]
    table_col, table_row = own_col >> 1, (code_own >> 1)[None, :]
    key_col, key_row = key_table[:, None], key_table[None, :]
    cot = to_sequences(cotangent, z)

    cur0, low0, normed, stats = call(
        features_kernel,
        [((half, d), f32), ((half, d), bf16), ((half, fdim), bf16), ((32, fdim), f32)],
        [pos, feat_own, feat_other, own_col, other_col, enc_w, enc_b[None]],
        flops=2 * half * d * HD,
        name="features",
    )
    q0, kv0, wq0, bqv, bup = call(
        qkv_first_kernel,
        [((half, d), bf16), ((half, 2 * d), bf16), ((d, 3 * d), bf16), ((8, d), f32), ((8, f), f32)],
        [pos, low0, w0a, w0b],
        flops=2 * half * d * 3 * d,
        name="qkv_first",
    )
    kv0r = swap_dp(kv0, 1)
    ob, lg, lb = out_bias.reshape(-1, d), ln_gain.reshape(-1, d), ln_bias.reshape(-1, d)
    mix0, lse0, n1, inv1, act, dgel, n2, inv2, low1, wo, wu, wd = call(
        first_layer_kernel,
        [
            ((half, d), f32), ((8, half), f32), ((half, d), f32), ((half, HD), f32), ((half, f), bf16),
            ((half, f), bf16), ((half, d), f32), ((half, HD), f32), ((half, d), bf16),
            ((d, d), bf16), ((d, f), bf16), ((f, d), bf16),
        ],
        [pos, q0, kv0, kv0r, table_col, key_row, cur0, w1a, w1b, bup, ob, lg, lb],
        [((half, n), f32), ((half, HD), f32)],
        flops=2 * half * (2 * n * d + d * d + 2 * d * f),
        name="first_layer",
    )
    q1, kv1, wq1 = call(
        qkv_next_kernel,
        [((half, d), bf16), ((half, 2 * d), bf16), ((d, 3 * d), bf16)],
        [pos, low1, w2a, w2b, bqv],
        flops=2 * half * d * 3 * d,
        name="qkv_next",
    )
    kv1r = swap_dp(kv1, 1)
    mix1, lse1, final, gmix1, gbm1, keep1, send1, vec1 = call(
        last_layer_kernel,
        [
            ((half, d), f32), ((8, half), f32), ((half, d), bf16), ((half, d), bf16), ((half, d), f32),
            ((4, width * rest, HD), bf16), ((4, width * rest, HD), bf16), ((16, d), f32),
        ],
        [pos, q1, kv1, kv1r, table_col, key_row, n2, w2a, w2b, bup, ob, lg, lb, cot],
        [
            ((half, n), f32), ((half, HD), f32), ((d, d), bf16), ((d, f), bf16), ((f, d), bf16),
            ((half, d), f32), ((half, HD), f32), ((half, f), bf16), ((half, f), bf16), ((half, d), f32),
            ((half, HD), f32), ((half, d), bf16), ((half, f), bf16), ((half, d), bf16), ((f, max(f, 3 * d)), bf16),
        ],
        flops=2 * half * (2 * n * d + d * d + 2 * d * f) * 3,
        name="last_layer",
    )
    final_rows = from_sequences(final, z)
    r1a, r1b = reduce_pieces(keep1, send1, rest)

    def attention_back(q, kv, kvr, mix, gmix, lse, name):
        dq, dkva, dkvb = call(
            attention_back_kernel,
            [((half, d), bf16), ((half, 2 * d), f32), ((half, 2 * d), bf16)],
            [pos, q, kv, kvr, mix, gmix, lse, key_col, table_row],
            [((n, half), f32), ((HD, half), f32)],
            flops=2 * half * 5 * n * d,
            name=name,
        )
        return dq, dkva, swap_dp(dkvb, 1)

    dq1, dkva1, dkvr1 = attention_back(q1, kv1, kv1r, mix1, gmix1, lse1, "attention_back_last")
    gmix0, gbm0, keep2, send2, vec = call(
        middle_kernel,
        [
            ((half, d), bf16), ((half, d), f32),
            ((4, width * (first + rest), HD), bf16), ((4, width * (first + rest), HD), bf16), ((24, d), f32),
        ],
        [
            pos, dq1, dkva1, dkvr1, wq1, gbm1, n2, vec1, n1, inv1, act, dgel, inv2, mix0, wo, wu, wd, lg, lb,
        ],
        [
            ((half, 3 * d), bf16), ((f, max(f, 3 * d)), bf16), ((half, d), f32),
            ((half, d), bf16), ((half, f), bf16), ((half, d), bf16),
        ],
        flops=2 * half * (6 * d * d + 2 * d * d + 4 * d * f),
        name="middle",
    )
    r2a, r2b = reduce_pieces(keep2, send2, first + rest)
    dq0, dkva0, dkvr0 = attention_back(q0, kv0, kv0r, mix0, gmix0, lse0, "attention_back_first")
    shared_rows = -(-(24 + fdim) // 128) * 128
    share = shared_rows // 8 * (d // HD)
    keep3, send3, gnorm, sums = call(
        entry_kernel,
        [
            ((4, width * first + share, HD), bf16), ((4, width * first + share, HD), bf16),
            ((half, fdim), f32), ((16, fdim), f32),
        ],
        [pos, dq0, dkva0, dkvr0, low0, wq0, gbm0, vec, normed, feat_own, own_col, stats, enc_w],
        [((half, 3 * d), bf16), ((f, max(f, 3 * d)), bf16), ((shared_rows, d), f32)],
        flops=2 * half * (6 * d * d + 2 * d * HD),
        name="entry",
    )
    r3a, r3b = reduce_pieces(keep3, send3, first)
    (g_feat,) = call(
        features_back_kernel,
        [((half, fdim), f32)],
        [pos, gnorm, feat_own, own_col, stats, sums, swap_dp(sums, 1)],
        name="features_back",
    )
    grad_features = from_sequences(g_feat, z)
    g_qkv, g_out, g_up, g_down, rows = call(
        result_kernel,
        [
            ((layers, 3, d, HD), f32), ((layers, HD, d), f32), ((layers, d, f_part), f32),
            ((layers, f_part, d), f32), ((shared_rows, d), f32),
        ],
        [pos, r1a, r1b, r2a, r2b, r3a, r3b],
        name="results",
    )
    vec = rows[: 10 * layers].reshape(layers, 10, d)
    d_bqv = lax.dynamic_slice_in_dim(vec[:, 6:8], z * HD, HD, 2)
    d_bup = lax.dynamic_slice_in_dim(vec[:, 8:].reshape(layers, f), z * f_part, f_part, 1)
    return (
        final_rows,
        grad_features,
        rows[24 : 24 + fdim],
        rows[10 * layers],
        g_qkv,
        d_bqv,
        g_out,
        vec[:, 4:6],
        vec[:, 0:2],
        vec[:, 2:4],
        g_up,
        d_bup,
        g_down,
    )


def solution(mesh):
    rows, ids = P("tensor", "dp", None), P(None, "dp")
    qkv, bqv = P(None, None, None, "tensor"), P(None, None, "tensor")
    mid, last = P(None, "tensor", None), P(None, None, "tensor")
    in_specs = (rows, ids, ids, P(), P(), qkv, bqv, mid, P(), P(), P(), last, P(None, "tensor"), mid, rows)
    out_specs = (rows, rows, P(), P(), qkv, bqv, mid, P(), P(), P(), last, P(None, "tensor"), mid)
    return jax.shard_map(local, mesh=mesh, in_specs=in_specs, out_specs=out_specs, check_vma=False)
```

```python
import functools
import math

import jax
import jax.numpy as jnp
from jax import lax
from jax.experimental import pallas as pl
from jax.experimental.pallas import tpu as pltpu
from jax.sharding import PartitionSpec as P

HD = 128
NTAB = 5
spread_floor = 0.1
norm_eps = 1e-05
f32 = jnp.float32
bf16 = jnp.bfloat16
LOG2E = 1.4426950408889634
MIB = 1024 * 1024


def mm(a, b):
    return lax.dot_general(a, b, (((1,), (0,)), ((), ())), preferred_element_type=f32)


def mm_nt(a, b):
    return lax.dot_general(a, b, (((1,), (1,)), ((), ())), preferred_element_type=f32)


def mm_tn(a, b):
    return lax.dot_general(a, b, (((0,), (0,)), ((), ())), preferred_element_type=f32)


class Stage:
    def __init__(self, loads, stores):
        self.loads = {id(ref): copy for ref, copy in loads}
        self.stores = {id(ref): copy for ref, copy in stores}
        self.started = []
        for copy in self.loads.values():
            copy.start()

    def need(self, *refs):
        for ref in refs:
            copy = self.loads.pop(id(ref), None)
            if copy is not None:
                copy.wait()

    def done(self, *refs):
        for ref in refs:
            copy = self.stores.pop(id(ref), None)
            if copy is not None:
                copy.start()
                self.started.append(copy)

    def finish(self):
        for copy in self.stores.values():
            copy.start()
        for copy in list(self.loads.values()) + self.started + list(self.stores.values()):
            copy.wait()


def call(body, outs, args, scratch=(), flops=0, name=None, after=(), far=(), vmem=16, staged=False):
    shapes = [jax.ShapeDtypeStruct(shape, dtype) for shape, dtype in outs]
    size = lambda a: a.size * a.dtype.itemsize
    moved = sum(size(a) for a in args) + sum(size(a) for a in shapes)
    count, results, extra = len(args), len(shapes), len(scratch)
    large_in = [at for at in range(1, count) if staged and at not in far and size(args[at]) >= 65536]
    large_out = [at for at in range(results) if staged and size(shapes[at]) >= 65536]
    near = pl.BlockSpec(memory_space=pltpu.VMEM)
    hbm = pl.BlockSpec(memory_space=pl.ANY)

    def run(*refs):
        ins = list(refs[:count])
        out = list(refs[count + len(after) :][:results])
        rest = refs[count + len(after) + results :]
        mine, rest = rest[:extra], rest[extra:]
        held_in, held_out, sems = rest[: len(large_in)], rest[len(large_in) : -1], rest[-1]
        loads, stores = [], []
        for at, ref in zip(large_in, held_in):
            loads.append((ref, pltpu.make_async_copy(ins[at], ref, sems.at[len(loads)])))
            ins[at] = ref
        for at, ref in zip(large_out, held_out):
            stores.append((ref, pltpu.make_async_copy(ref, out[at], sems.at[len(loads) + len(stores)])))
            out[at] = ref
        stage = Stage(loads, stores)
        body(stage, *ins, *out, *mine)
        stage.finish()

    return pl.pallas_call(
        run,
        out_shape=shapes,
        in_specs=[pl.BlockSpec(memory_space=pltpu.SMEM)]
        + [hbm if at in far or at in large_in else near for at in range(1, count)]
        + [hbm] * len(after),
        out_specs=[hbm if at in large_out else near for at in range(results)],
        scratch_shapes=[
            pltpu.SemaphoreType.DMA(shape) if dtype is None else pltpu.VMEM(shape, dtype) for shape, dtype in scratch
        ]
        + [pltpu.VMEM(args[at].shape, args[at].dtype) for at in large_in]
        + [pltpu.VMEM(shapes[at].shape, shapes[at].dtype) for at in large_out]
        + [pltpu.SemaphoreType.DMA((max(1, len(large_in) + len(large_out)),))],
        compiler_params=pltpu.CompilerParams(vmem_limit_bytes=vmem * MIB),
        cost_estimate=pl.CostEstimate(flops=flops, bytes_accessed=moved, transcendentals=0),
        name=name,
    )(*args, *after)


def blocks(kind, d, f_part, q, z):
    if kind == "qkv":
        n = d // 8
        return [(c * n, n, q * n, c * d + z * HD) for c in range(3)]
    if kind == "out":
        n = HD // 8
        return [(c * n, n, z * HD + q * n, c * HD) for c in range(d // HD)]
    if kind == "up":
        n = d // 8
        return [(c * n, n, q * n, z * f_part + c * HD) for c in range(f_part // HD)]
    n = f_part // 8
    return [(c * n, n, z * f_part + q * n, c * HD) for c in range(d // HD)]


def aligned(value, unit):
    return value if isinstance(value, int) else pl.multiple_of(value, unit)


def unpack(pos, buffers, row0, kind, whole, d, f_part):
    base = 0
    for src in buffers:

        def step(e, carry, src=src, base=base):
            q = pos[base + e]
            for k in range(src.shape[1]):
                for at, n, row, col in blocks(kind, d, f_part, q, pos[8 + k]):
                    whole[pl.ds(aligned(row, 16), n), pl.ds(aligned(col, HD), HD)] = src[
                        e, k, row0 + at : row0 + at + n, :
                    ]
            return carry

        lax.fori_loop(0, src.shape[0], step, 0)
        base += src.shape[0]


def pack(pos, whole, row0, kind, halves, d, f_part, width, piece, order=12):
    for c in range(2):
        dst = halves[c]

        def step(e, carry, dst=dst, c=c):
            q = pos[order + c * 4 + e]
            for k in range(width):
                for at, n, row, col in blocks(kind, d, f_part, q, pos[8 + k]):
                    at += k * piece + row0
                    dst[e, at : at + n, :] = whole[
                        pl.ds(aligned(row, 16), n), pl.ds(aligned(col, HD), HD)
                    ]
            return carry

        lax.fori_loop(0, 4, step, 0)


def copy_all(pairs, sems):
    copies = [pltpu.make_async_copy(src, dst, sems.at[at]) for at, (src, dst) in enumerate(pairs)]
    for copy in copies:
        copy.start()
    for copy in copies:
        copy.wait()


def qkv_copies(l, q, wqkv, to):
    n = wqkv.shape[2] // 8
    row = pl.multiple_of(q * n, 16)
    return [(wqkv.at[l, c, pl.ds(row, n), :], to.at[pl.ds(c * n, n), :]) for c in range(3)]


def pack_first_kernel(stage, pos, wqkv, bqv, bup, g0, sems):
    d, f_part = wqkv.shape[2], bup.shape[1]
    rows = [bqv[0], bqv[1]]
    rows += [bup[l : l + 1, c * HD : (c + 1) * HD] for l in range(2) for c in range(f_part // HD)]
    rows = jnp.concatenate(rows, 0)
    high = rows.astype(bf16).astype(f32)
    g0[3 * d // 8 :, :] = jnp.concatenate([high, rows - high], 0).astype(bf16)
    copy_all(qkv_copies(0, pos[0], wqkv, g0), sems)


def rest_copies(l, q, wout, wup, wdown, to, base):
    d, f_part = wup.shape[1], wup.shape[2]
    n, m, r = d // 8, HD // 8, f_part // 8
    pairs = []
    for src, count, cols in ((wout, m, d), (wup, n, f_part), (wdown, r, d)):
        for c in range(cols // HD):
            block = src.at[l, pl.ds(pl.multiple_of(q * count, 16), count), pl.ds(c * HD, HD)]
            pairs.append((block, to.at[pl.ds(base, count), :]))
            base += count
    return pairs


def pack_rest_kernel(stage, pos, wout, wup, wdown, g1, sems):
    copy_all(rest_copies(0, pos[0], wout, wup, wdown, g1, 0), sems)


def pack_second_kernel(stage, pos, wqkv, wout, wup, wdown, g2, sems):
    pairs = qkv_copies(1, pos[0], wqkv, g2)
    copy_all(pairs + rest_copies(1, pos[0], wout, wup, wdown, g2, 3 * wqkv.shape[2] // 8), sems)


def add_kernel(stage, pos, a, b, low, high):
    m = a.shape[0] // 2
    low[...] = (a[:m].astype(f32) + b[:m].astype(f32)).astype(bf16)
    high[...] = (a[m:].astype(f32) + b[m:].astype(f32)).astype(bf16)


def join_kernel(stage, pos, b, c, *shares):
    m = b.shape[1] // len(shares)
    for k, out in enumerate(shares):
        at = slice(k * m, (k + 1) * m)
        out[...] = (b[0, at, :].astype(f32) + c[0, at, :].astype(f32)).astype(bf16)


def join_last_kernel(stage, pos, b, c, *shares):
    width = len(shares)
    m = (b.shape[1] - shares[0].shape[0]) // (width - 1)
    for k, out in enumerate(shares):
        at = slice(k * m, (k + 1) * m)
        out[:m, :] = (b[0, at, :].astype(f32) + c[0, at, :].astype(f32)).astype(bf16)
        at = slice(width * m, b.shape[1])
        out[m:, :] = (b[0, at, :].astype(f32) + c[0, at, :].astype(f32)).astype(bf16)


def erf(x):
    x = jnp.clip(x, -3.7439211627767994, 3.7439211627767994)
    y = x * x
    top = 2.2905065861350646e-4
    for c in (3.4082910107109506e-3, 5.0955695062380861e-2, 1.8520832239976145e-1, 1.128379143519084):
        top = top * y + c
    low = -1.1791602954361697e-7
    for c in (
        2.3547966471313185e-5,
        1.0179625278914885e-3,
        1.4070470171167667e-2,
        1.1098505178285362e-1,
        4.9746925110067538e-1,
        1.0,
    ):
        low = low * y + c
    return x * top / low


def gelu_pair(h):
    cdf = 0.5 + 0.5 * erf(h * math.sqrt(0.5))
    return h * cdf, cdf + h * (jnp.exp2(h * h * (-0.5 * LOG2E)) * (1.0 / math.sqrt(2.0 * math.pi)))


def normalize(u):
    centre = u - jnp.mean(u, -1, keepdims=True)
    inv = lax.rsqrt(jnp.mean(centre * centre, -1, keepdims=True) + norm_eps)
    return centre * inv, inv


def norm_back(grad, normal, inv, gain):
    e = grad * gain
    return (e - jnp.mean(e, -1, keepdims=True) - normal * jnp.mean(e * normal, -1, keepdims=True)) * inv


def rowsum(x):
    return jnp.sum(x, 0, keepdims=True)


def row_codes(block, features):
    return block[:, features : features + 1].astype(jnp.int32)


def key_tables(code):
    return jnp.where((code & 1) == 1, code >> 1, -1)


def features_kernel(stage, pos, fa, fb, encw, encb, cur, low, normed, stats, table_col, key_col, lines):
    stage.need(fa, fb, encw)
    features = encw.shape[0]
    half = fa.shape[0]
    own, other = fa[:, :features], fb[:, :features]
    code_a, code_b = row_codes(fa, features), row_codes(fb, features)
    table_col[...] = code_a >> 1
    key_col[:half, :] = key_tables(code_a)
    key_col[half:, :] = key_tables(code_b)
    line_a = fa[...].T[features : features + 1, :].astype(jnp.int32)
    line_b = fb[...].T[features : features + 1, :].astype(jnp.int32)
    lines[0:1, :half] = key_tables(line_a)
    lines[0:1, half:] = key_tables(line_b)
    lines[1:2, :half] = line_a >> 1
    mean_rows = jnp.zeros_like(own)
    scale_rows = jnp.zeros_like(own)
    for t in range(NTAB):
        pa = (code_a == 2 * t + 1).astype(f32)
        pb = (code_b == 2 * t + 1).astype(f32)
        count = rowsum(pa) + rowsum(pb)
        mean = (rowsum(pa * own) + rowsum(pb * other)) / count
        da, db = own - mean, other - mean
        excess = (rowsum(pa * da * da) + rowsum(pb * db * db)) / count
        scale = lax.rsqrt(jnp.maximum(excess, spread_floor))
        stats[t : t + 1, :] = mean
        stats[8 + t : 9 + t, :] = scale
        stats[16 + t : 17 + t, :] = excess
        stats[24 + t : 25 + t, :] = jnp.broadcast_to(count, mean.shape)
        here = (code_a >> 1) == t
        mean_rows = jnp.where(here, mean, mean_rows)
        scale_rows = jnp.where(here, scale, scale_rows)
    z = ((own - mean_rows) * scale_rows).astype(bf16)
    normed[...] = z
    out = mm(z, encw[...]) + encb[...].reshape(1, -1)
    cur[...] = out
    low[...] = out.astype(bf16)


def project(stage, x, w, bias, q, kv, layer, d):
    kv[:, :d] = mm(x, w[:, d : 2 * d]).astype(bf16)
    kv[:, d:] = (mm(x, w[:, 2 * d :]) + bias[2 * layer + 1 : 2 * layer + 2, :]).astype(bf16)
    stage.done(kv)
    q[...] = (mm(x, w[:, :d]) + bias[2 * layer : 2 * layer + 1, :]).astype(bf16)


def qkv_first_kernel(stage, pos, low, ga, gb, gc, gd, q, kv, w, bqv, bup):
    d = low.shape[1]
    buffers = (ga, gb, gc, gd)
    stage.need(*buffers)
    unpack(pos, buffers, 0, "qkv", w, d, 0)
    stage.done(w)
    base = 3 * d // 8
    f_part = 2 * HD
    for k in range(ga.shape[1]):
        z = pos[8 + k]
        rows = ga[0, k, base : base + 16, :].astype(f32)
        rows = rows[:8] + rows[8:]
        for j in range(4):
            bqv[j : j + 1, pl.ds(pl.multiple_of(z * HD, HD), HD)] = rows[j : j + 1]
            col = z * f_part + (j % 2) * HD
            bup[j // 2 : j // 2 + 1, pl.ds(pl.multiple_of(col, HD), HD)] = rows[4 + j : 5 + j]
    stage.need(low)
    project(stage, low[...], w, bqv, q, kv, 0, d)


def qkv_next_kernel(stage, pos, low, ga, gb, gc, gd, bqv, q, kv, w):
    d = low.shape[1]
    stage.need(ga, gb, gc, gd)
    unpack(pos, (ga, gb, gc, gd), 0, "qkv", w, d, 0)
    stage.done(w)
    stage.need(low)
    project(stage, low[...], w, bqv, q, kv, 1, d)


def attention_rows(rows, q, kva, kvb, bias, mix, lse, d):
    n = kva.shape[0]
    factor = LOG2E / math.sqrt(HD)
    count = rows.size
    lane = lax.broadcasted_iota(jnp.int32, (count, HD), 1)
    totals = jnp.zeros((count, HD), f32)
    for h in range(d // HD):
        cols = slice(h * HD, (h + 1) * HD)
        vals = slice(d + h * HD, d + (h + 1) * HD)
        qh = q[rows, cols]
        ta = mm_nt(qh, kva[:, cols]) * factor + bias[rows, :n]
        tb = mm_nt(qh, kvb[:, cols]) * factor + bias[rows, n:]
        top = jnp.maximum(jnp.max(ta, -1, keepdims=True), jnp.max(tb, -1, keepdims=True))
        ea, eb = jnp.exp2(ta - top), jnp.exp2(tb - top)
        total = jnp.sum(ea, -1, keepdims=True) + jnp.sum(eb, -1, keepdims=True)
        out = mm(ea.astype(bf16), kva[:, vals]) + mm(eb.astype(bf16), kvb[:, vals])
        mix[rows, cols] = out / total
        totals = jnp.where(lane == h, top + jnp.log2(total), totals)
    lse[rows, :] = totals


def layer_rows(rows, cur, mix, wo, wu, wd, bup, ob, lg, lb, layer, n1, inv1, act, dgel, n2, inv2):
    l = layer
    u = cur + mm(mix[rows, :].astype(bf16), wo[...]) + ob[l, 0:1, :]
    normal, inv = normalize(u)
    n1[rows, :] = normal
    inv1[rows, :] = jnp.broadcast_to(inv, (rows.size, HD))
    middle = normal * lg[l, 0:1, :] + lb[l, 0:1, :]
    hidden = mm(middle.astype(bf16), wu[...]) + bup[l : l + 1, :]
    value, slope = gelu_pair(hidden)
    value = value.astype(bf16)
    act[rows, :] = value
    dgel[rows, :] = slope.astype(bf16)
    u = middle + mm(value, wd[...]) + ob[l, 1:2, :]
    normal, inv = normalize(u)
    n2[rows, :] = normal
    inv2[rows, :] = jnp.broadcast_to(inv, (rows.size, HD))
    return normal * lg[l, 1:2, :] + lb[l, 1:2, :]


def set_bias(bias, col, line):
    bias[...] = jnp.where(col[...] == line, 0.0, -1e30)


def attention(stage, q, kva, kvb, col, lines, mix, lse, bias, raw, d):
    set_bias(bias, col, lines[0:1, :])
    stage.need(q, kva, kvb)

    def step(i, carry):
        rows = pl.ds(pl.multiple_of(i * CHUNK, CHUNK), CHUNK)
        attention_rows(rows, q, kva, kvb, bias, mix, raw, d)
        return carry

    lax.fori_loop(0, q.shape[0] // CHUNK, step, 0)
    stage.done(mix)
    lse[...] = raw[...].T[:8]


def unpack_rest(stage, pos, buffers, row0, wo, wu, wd, d, f_part):
    m = HD // 8 * (d // HD)
    stage.need(*buffers)
    unpack(pos, buffers, row0, "out", wo, d, f_part)
    unpack(pos, buffers, row0 + m, "up", wu, d, f_part)
    unpack(pos, buffers, row0 + m + d // 8 * (f_part // HD), "down", wd, d, f_part)
    stage.done(wo, wu, wd)


def first_layer_kernel(
    stage, pos, q, kva, kvb, col, lines, ga, gb, gc, gd, cur, bup, ob, lg, lb,
    mix, lse, n1, inv1, act, dgel, n2, inv2, low, wo, wu, wd,
    bias, raw,
):
    d = q.shape[1]
    attention(stage, q, kva, kvb, col, lines, mix, lse, bias, raw, d)
    unpack_rest(stage, pos, (ga, gb, gc, gd), 0, wo, wu, wd, d, wu.shape[1] // ga.shape[1])
    stage.need(cur)

    def step(i, carry):
        rows = pl.ds(pl.multiple_of(i * CHUNK, CHUNK), CHUNK)
        out = layer_rows(
            rows, cur[rows, :], mix, wo, wu, wd, bup, ob, lg, lb, 0, n1, inv1, act, dgel, n2, inv2
        )
        low[rows, :] = out.astype(bf16)
        return carry

    lax.fori_loop(0, q.shape[0] // CHUNK, step, 0)


CHUNK = 256


def ffn_back(
    stage, pos, grad, l, n1, inv1, act, dgel, n2, inv2, mix, wo, wu, wd, lg, lb,
    gmix, gbm, delta, keep, send, vec, vrow, gl, gh, g1, dwd, dwu, dwo, d, f_part, width, piece, order, base,
):
    gain0, gain1 = lg[l, 0:1, :], lg[l, 1:2, :]
    shift0 = lb[l, 0:1, :]
    f = wu.shape[1]

    def step(i, carry):
        rows = pl.ds(pl.multiple_of(i * CHUNK, CHUNK), CHUNK)
        top = grad[rows, :].astype(f32)
        normal = n2[rows, :]
        bo = norm_back(top, normal, inv2[rows, :1], gain1)
        low = bo.astype(bf16)
        gl[rows, :] = low
        back = mm_nt(low, wd[...])
        back = (back * dgel[rows, :].astype(f32)).astype(bf16)
        gh[rows, :] = back
        gm = bo + mm_nt(back, wu[...])
        first = n1[rows, :]
        bm = norm_back(gm, first, inv1[rows, :1], gain0)
        gbm[rows, :] = bm
        attn = bm.astype(bf16)
        g1[rows, :] = attn
        gmix[rows, :] = mm_nt(attn, wo[...]).astype(bf16)
        sums = (
            rowsum(gm * first),
            rowsum(top * normal),
            rowsum(gm),
            rowsum(top),
            rowsum(attn.astype(f32)),
            rowsum(low.astype(f32)),
        )
        hidden = rowsum(back.astype(f32))
        for j in range(6):
            vec[vrow + j : vrow + j + 1, :] += sums[j]
        for j in range(f // d):
            at = vrow + 8 + j
            vec[at : at + 1, :] += hidden[:, j * d : (j + 1) * d]
        return carry

    lax.fori_loop(0, act.shape[0] // CHUNK, step, 0)
    stage.done(gmix, gbm)
    for h in range(d // HD):
        cols = slice(h * HD, (h + 1) * HD)
        prod = gmix[:, cols].astype(f32) * mix[:, cols]
        delta[h : h + 1, :] = jnp.sum(prod.T, 0, keepdims=True)
    m = HD // 8 * (d // HD)
    dwd[...] = mm_tn(act[...], gl[...]).astype(bf16)
    middle = (n1[...] * gain0 + shift0).astype(bf16)
    dwu[...] = mm_tn(middle, gh[...]).astype(bf16)
    dwo[...] = mm_tn(mix[...].astype(bf16), g1[...]).astype(bf16)
    pack(pos, dwd, base + m + d // 8 * (f_part // HD), "down", (keep, send), d, f_part, width, piece, order)
    pack(pos, dwu, base + m, "up", (keep, send), d, f_part, width, piece, order)
    pack(pos, dwo, base, "out", (keep, send), d, f_part, width, piece, order)


def last_layer_kernel(
    stage, pos, q, kva, kvb, col, lines, ga, gb, gc, gd, n2in, cot, bup, ob, lg, lb,
    lse, final, gmix, gbm, delta, keep, send, vec,
    bias, raw, mix, wo, wu, wd, n1, inv1, act, dgel, n2, inv2, gl, gh, g1, dwd, dwu, dwo,
):
    d = q.shape[1]
    width = ga.shape[1]
    f_part = wu.shape[1] // width
    attention(stage, q, kva, kvb, col, lines, mix, lse, bias, raw, d)
    unpack_rest(stage, pos, (ga, gb, gc, gd), 3 * d // 8, wo, wu, wd, d, f_part)
    stage.need(n2in)

    def step(i, carry):
        rows = pl.ds(pl.multiple_of(i * CHUNK, CHUNK), CHUNK)
        cur = n2in[rows, :] * lg[0, 1:2, :] + lb[0, 1:2, :]
        out = layer_rows(
            rows, cur, mix, wo, wu, wd, bup, ob, lg, lb, 1, n1, inv1, act, dgel, n2, inv2
        )
        final[rows, :] = out.astype(bf16)
        return carry

    lax.fori_loop(0, q.shape[0] // CHUNK, step, 0)
    stage.done(final)
    vec[...] = jnp.zeros_like(vec)
    stage.need(cot)
    ffn_back(
        stage, pos, cot, 1, n1, inv1, act, dgel, n2, inv2, mix, wo, wu, wd, lg, lb,
        gmix, gbm, delta, keep, send, vec, 0, gl, gh, g1, dwd, dwu, dwo, d, f_part, width, keep.shape[1] // width, 0, 0,
    )


def attention_back_kernel(stage, pos, gmix, delta, q, kvb, kva, lse, col, lines, dq, dkva, dkvb, bias, acc):
    d = q.shape[1]
    n = kva.shape[0]
    scaling = 1.0 / math.sqrt(HD)
    factor = LOG2E * scaling
    set_bias(bias, col, lines[1:2, : q.shape[0]])
    block = 256
    stage.need(gmix)
    acc[...] = jnp.zeros_like(acc)
    stage.need(q)
    for src, dst, off in ((kvb, dkvb, n), (kva, dkva, 0)):
        stage.need(src)

        def step(i, carry, src=src, dst=dst, off=off):
            rows = pl.ds(pl.multiple_of(i * block, block), block)
            brow = pl.ds(pl.multiple_of(off + i * block, block), block)
            for h in range(d // HD):
                cols = slice(h * HD, (h + 1) * HD)
                vals = slice(d + h * HD, d + (h + 1) * HD)
                qh, gh = q[:, cols], gmix[:, cols]
                kh, vh = src[rows, cols], src[rows, vals]
                probs = jnp.exp2(mm_nt(kh, qh) * factor + bias[brow, :] - lse[h : h + 1, :])
                ds = (probs * (mm_nt(vh, gh) - delta[h : h + 1, :])).astype(bf16)
                dst[rows, vals] = mm(probs.astype(bf16), gh).astype(dst.dtype)
                dst[rows, cols] = (mm(ds, qh) * scaling).astype(dst.dtype)
                acc[h, :, :] += mm_tn(kh, ds)
            return carry

        lax.fori_loop(0, n // block, step, 0)
        stage.done(dst)
    for h in range(d // HD):
        dq[:, h * HD : (h + 1) * HD] = (acc[h].T * scaling).astype(bf16)


def projection_back(
    stage, pos, dq, dkva, dkvr, low, w, gbm, proj, dw, keep, send, vec, vrow, d, width, piece, order
):
    stage.need(dq, dkva, dkvr)
    proj[:, :d] = dq[...]
    proj[:, d:] = (dkva[...].astype(f32) + dkvr[...].astype(f32)).astype(bf16)
    vec[vrow : vrow + 1, :] = rowsum(dq[...].astype(f32))
    vec[vrow + 1 : vrow + 2, :] = rowsum(proj[:, 2 * d :].astype(f32))
    dw[...] = mm_tn(low(), proj[...]).astype(bf16)
    stage.need(w, gbm)
    grad = gbm[...] + mm_nt(proj[...], w[...])
    pack(pos, dw, 0, "qkv", (keep, send), d, 0, width, piece, order)
    return grad


def middle_kernel(
    stage, pos, dq, dkva, dkvr, w, gbm1, n2, inv2, wd, dgel, wu, n1, inv1, wo, act, mix, vec1, lg, lb,
    gmix, gbm, delta, keep, send, vec,
    proj, dw, grad, gl, gh, g1, dwd, dwu, dwo,
):
    d = grad.shape[1]
    width = d // HD
    first = 3 * d // 8
    piece = keep.shape[1] // width
    vec[...] = jnp.zeros_like(vec)
    for j in range(10):
        vec[10 + j : 11 + j, :] = vec1[j : j + 1, :]

    def low():
        return (n2[...] * lg[0, 1:2, :] + lb[0, 1:2, :]).astype(bf16)

    grad[...] = projection_back(
        stage, pos, dq, dkva, dkvr, low, w, gbm1, proj, dw, keep, send, vec, 16, d, width, piece, 0
    )
    ffn_back(
        stage, pos, grad, 0, n1, inv1, act, dgel, n2, inv2, mix, wo, wu, wd, lg, lb,
        gmix, gbm, delta, keep, send, vec, 0, gl, gh, g1, dwd, dwu, dwo, d, wu.shape[1] // width,
        width, piece, 0, first,
    )


def entry_kernel(
    stage, pos, dq, dkva, dkvr, low0, w0, gbm0, normed, encw, fa, vec, stats,
    keep, send, gnorm, sums,
    proj, dw, shared,
):
    d = dq.shape[1]
    features = encw.shape[0]
    width = d // HD
    first = 3 * d // 8
    shared[...] = jnp.zeros_like(shared)
    shared[:24, :] = vec[...]
    def low():
        stage.need(low0)
        return low0[...]

    grad = projection_back(
        stage, pos, dq, dkva, dkvr, low, w0, gbm0, proj, dw, keep, send, shared, 6, d, width, first, 0
    )
    stage.need(normed, encw, fa)
    low = grad.astype(bf16)
    shared[20:21, :] = rowsum(low.astype(f32))
    shared[24 : 24 + features, :] = mm_tn(normed[...], low)
    back = mm_nt(low, encw[...])
    gnorm[...] = back
    code = row_codes(fa, features) >> 1
    centred = fa[:, :features]
    sums[...] = jnp.zeros_like(sums)
    for t in range(NTAB):
        here = code == t
        part = jnp.where(here, back, 0.0)
        sums[t : t + 1, :] = rowsum(part)
        sums[8 + t : 9 + t, :] = rowsum(part * (centred - stats[t : t + 1, :]))
    share = shared.shape[0] // 8
    for c, dst in ((0, keep), (1, send)):

        def step(e, carry, dst=dst, c=c):
            row = pl.multiple_of(pos[c * 4 + e] * share, 8)
            for j in range(d // HD):
                piece = shared[pl.ds(row, share), j * HD : (j + 1) * HD].astype(bf16)
                at = width * first + j * share
                dst[e, at : at + share, :] = piece
            return carry

        lax.fori_loop(0, 4, step, 0)


def features_back_kernel(stage, pos, gnorm, fa, stats, mine, theirs, out):
    total = mine[...] + theirs[...]
    stage.need(gnorm, fa)
    back = gnorm[...]
    code = row_codes(fa, back.shape[1])
    x = fa[:, : back.shape[1]]
    scale_rows = jnp.zeros_like(x)
    flat = jnp.zeros_like(x)
    slope = jnp.zeros_like(x)
    for t in range(NTAB):
        mean, scale = stats[t : t + 1, :], stats[8 + t : 9 + t, :]
        excess, count = stats[16 + t : 17 + t, :], stats[24 + t : 25 + t, :]
        plain, centred = total[t : t + 1, :], total[8 + t : 9 + t, :]
        g_excess = jnp.where(excess > spread_floor, -0.5 * scale * scale * scale * centred, 0.0)
        g_mean = -scale * plain - 2.0 * mean * g_excess
        scale_rows = jnp.where((code >> 1) == t, scale, scale_rows)
        chosen = code == 2 * t + 1
        flat = jnp.where(chosen, g_mean / count, flat)
        slope = jnp.where(chosen, 2.0 * g_excess / count, slope)
    out[...] = back * scale_rows + flat + x * slope


def result_kernel(
    stage, pos, ra, rb, rc, rd, ea, eb, ec, ed, gqkv, gout, gup, gdown, genc_w, genc_b, gbqv, gob, glg, glb, gbup, rows
):
    d, f_part = gqkv.shape[2], gup.shape[2]
    n, m, r = d // 8, HD // 8, f_part // 8
    first = 3 * n
    share = rows.shape[0] // 8
    after = m * (d // HD) + n * (f_part // HD) + r * (d // HD)

    def rest(l, src, e, q, base):
        for c in range(d // HD):
            gout[l, pl.ds(pl.multiple_of(q * m, 16), m), c * HD : (c + 1) * HD] = src[
                e, base + c * m : base + (c + 1) * m, :
            ].astype(f32)
        base += d // HD * m
        for c in range(f_part // HD):
            gup[l, pl.ds(pl.multiple_of(q * n, 16), n), c * HD : (c + 1) * HD] = src[
                e, base + c * n : base + (c + 1) * n, :
            ].astype(f32)
        base += f_part // HD * n
        for c in range(d // HD):
            gdown[l, pl.ds(pl.multiple_of(q * r, 16), r), c * HD : (c + 1) * HD] = src[
                e, base + c * r : base + (c + 1) * r, :
            ].astype(f32)

    for part, (src, end) in enumerate(((ra, ea), (rb, eb), (rc, ec), (rd, ed))):
        stage.need(src, end)

        def step(e, carry, part=part, src=src, end=end):
            q = pos[part * 2 + e]
            for l, ref, base in ((1, src, after), (0, end, 0)):
                for c in range(3):
                    gqkv[l, c, pl.ds(pl.multiple_of(q * n, 16), n), :] = ref[
                        e, base + c * n : base + (c + 1) * n, :
                    ].astype(f32)
            rest(1, src, e, q, 0)
            rest(0, src, e, q, after + first)
            for j in range(d // HD):
                rows[pl.ds(pl.multiple_of(q * share, 8), share), j * HD : (j + 1) * HD] = end[
                    e, first + j * share : first + (j + 1) * share, :
                ].astype(f32)
            return carry

        lax.fori_loop(0, src.shape[0], step, 0)
    z = pos[8]
    d = genc_w.shape[1]
    layers = gob.shape[0]
    genc_w[...] = rows[24 : 24 + genc_w.shape[0], :]
    genc_b[...] = rows[10 * layers : 10 * layers + 1, :]
    for l in range(layers):
        at = 10 * l
        for j in range(2):
            glg[l, j : j + 1, :] = rows[at + j : at + j + 1, :]
            glb[l, j : j + 1, :] = rows[at + 2 + j : at + 3 + j, :]
            gob[l, j : j + 1, :] = rows[at + 4 + j : at + 5 + j, :]
            gbqv[l, j : j + 1, :] = rows[at + 6 + j : at + 7 + j, pl.ds(pl.multiple_of(z * HD, HD), HD)]
        row = at + 8 + (z * f_part) // d
        col = pl.multiple_of((z * f_part) % d, HD)
        gbup[l : l + 1, :] = rows[pl.ds(row, 1), pl.ds(col, f_part)]


def swap_dp(values, even, odd=None):
    odd = even if odd is None else odd
    return lax.ppermute(values, ("plane", "pair"), [(i, i ^ (odd if i % 2 else even)) for i in range(8)])


def swap_z(values, mask):
    size = lax.axis_size("tensor")
    return lax.ppermute(values, "tensor", [(i, i ^ mask) for i in range(size)])


def relay_pairs(step):
    width = lax.axis_size("tensor")
    return [
        (p * width + z, z // 2 * width + 2 * p + (step ^ (z & 1))) for p in range(2) for z in range(width)
    ]


def pick(values, index, axis=0):
    return lax.dynamic_index_in_dim(values, index, axis, keepdims=False)


def to_sequences(one_block, z):
    got = [lax.ppermute(one_block(step ^ (z & 1)), ("pair", "tensor"), relay_pairs(step)) for step in range(2)]
    return jnp.concatenate(got)


def from_sequences(values, z):
    part = values.shape[0] // 2
    got = [
        lax.ppermute(
            values[step * part : (step + 1) * part],
            ("pair", "tensor"),
            [(b, a) for a, b in relay_pairs(step)],
        )
        for step in range(2)
    ]
    odd = (z & 1) == 1
    return jnp.stack([jnp.where(odd, got[1], got[0]), jnp.where(odd, got[0], got[1])], 1)


def stack_kernel(stage, pos, *refs):
    out = refs[-1]
    for at, ref in enumerate(refs[:-1]):
        out[at] = ref[...]


def stack(pos, pieces, name, after=()):
    shape = (len(pieces),) + pieces[0].shape
    return call(stack_kernel, [(shape, bf16)], [pos] + pieces, name=name, after=after, vmem=6)[0]


def copy_kernel(stage, pos, src, out):
    out[...] = src[...]


def later(pos, values, name, after):
    return call(copy_kernel, [(values.shape, values.dtype)], [pos, values], name=name, after=after, vmem=4)[0]


def over_z(pos, piece, name, after=()):
    pieces = [piece] + [swap_z(piece, k) for k in range(1, lax.axis_size("tensor"))]
    return stack(pos, pieces, name, after)


def over_plane(pos, piece, name, after=()):
    two = stack(pos, [piece, swap_dp(piece, 4, 2)], name, after)
    return two, swap_dp(two, 2, 4)


def over_pair(two, more):
    return two, more, swap_dp(two, 1), swap_dp(more, 1)


def add(a, b):
    return (a.astype(f32) + b.astype(f32)).astype(bf16)


def sum_far(values):
    return lax.psum(values.astype(f32), "far").astype(bf16) if lax.axis_size("far") > 1 else values


def split(pos, a, b, name):
    outs = [((a.shape[0] // 2,) + a.shape[1:], bf16)] * 2
    return call(add_kernel, outs, [pos, a, b], name=name, vmem=12)


def sum_z(shares):
    total = shares[0].astype(f32)
    for k in range(1, len(shares)):
        total = total + swap_z(shares[k], k).astype(f32)
    return total.astype(bf16)


def local(
    features,
    table_ids,
    train_flags,
    enc_w,
    enc_b,
    w_qkv,
    b_qv,
    w_out,
    out_bias,
    ln_gain,
    ln_bias,
    w_up,
    b_up,
    w_down,
    cotangent,
):
    part, _, fdim = features.shape
    width = lax.axis_size("tensor")
    layers, d, f_part = w_qkv.shape[0], w_qkv.shape[2], w_up.shape[2]
    f = f_part * width
    half = 2 * part
    n = 2 * half
    z, p, o = lax.axis_index("tensor"), lax.axis_index("pair"), lax.axis_index("plane")
    ox, oy = o & 1, o >> 1
    relative, absolute = [], []
    for c in range(2):
        for r1 in range(2):
            for r2 in range(2):
                pd = p ^ c
                rx, ry = jnp.where(pd == 0, r1, r2), jnp.where(pd == 0, r2, r1)
                relative.append(pd * 4 + (oy ^ ry) * 2 + (ox ^ rx))
                absolute.append(pd * 4 + r1 * 2 + r2)
    pos = jnp.stack(relative + [z ^ k for k in range(width)] + absolute).astype(jnp.int32)
    rest = HD // 8 * (d // HD) + d // 8 * (f_part // HD) + f_part // 8 * (d // HD)
    first = 3 * d // 8

    codes = lax.dynamic_slice_in_dim(table_ids, z * part, part) * 2
    codes = (codes + lax.dynamic_slice_in_dim(train_flags, z * part, part)).astype(f32)

    def feature_block(j):
        space = jnp.zeros((part, HD - fdim - 1), f32)
        return jnp.concatenate([pick(features, j, 1), pick(codes, j, 1)[:, None], space], 1)

    feat_own = to_sequences(feature_block, z)
    feat_other = swap_dp(feat_own, 1)
    (g0,) = call(
        pack_first_kernel,
        [((first + 16, HD), bf16)],
        [pos, w_qkv, b_qv, b_up],
        [((3,), None)],
        name="pack_first",
        vmem=4,
        far=(1,),
    )
    w0z = over_z(pos, g0, "first_z", (feat_own,))
    w0p = over_plane(pos, w0z, "first_plane", (feat_other,))
    w0 = over_pair(*w0p)
    (g1,) = call(
        pack_rest_kernel,
        [((rest, HD), bf16)],
        [pos, w_out, w_up, w_down],
        [((16,), None)],
        name="pack_rest",
        vmem=4,
        far=(1, 2, 3),
        after=(w0z,),
    )
    w1z = over_z(pos, g1, "rest_z")
    cur0, low0, normed, stats, table_col, key_col, lines = call(
        features_kernel,
        [
            ((half, d), f32), ((half, d), bf16), ((half, fdim), bf16), ((32, fdim), f32),
            ((half, 1), jnp.int32), ((n, 1), jnp.int32), ((8, n), jnp.int32),
        ],
        [pos, feat_own, feat_other, enc_w, enc_b[None]],
        flops=2 * half * d * HD,
        name="features",
        vmem=8,
    )
    (g2,) = call(
        pack_second_kernel,
        [((first + rest, HD), bf16)],
        [pos, w_qkv, w_out, w_up, w_down],
        [((16,), None)],
        name="pack_second",
        vmem=4,
        far=(1, 2, 3, 4),
        after=(w1z,),
    )
    w1p = over_plane(pos, w1z, "rest_plane", (low0, g2, w0p[1]))
    w1 = over_pair(*w1p)
    q0, kv0, wq0, bqv, bup = call(
        qkv_first_kernel,
        [((half, d), bf16), ((half, 2 * d), bf16), ((d, 3 * d), bf16), ((8, d), f32), ((8, f), f32)],
        [pos, low0, *w0],
        flops=2 * half * d * 3 * d,
        name="qkv_first",
        vmem=10,
    )
    cot = to_sequences(lambda j: later(pos, pick(cotangent, j, 1), "cotangent", (w1p[0],)), z)
    w2z = over_z(pos, g2, "second_z", (w1p[0],))
    w2p = over_plane(pos, w2z, "second_plane", (w1p[1], q0, cot))

    kv0r = swap_dp(kv0, 1)
    ob, lg, lb = out_bias, ln_gain, ln_bias
    mix0, lse0, n1, inv1, act, dgel, n2, inv2, low1, wo, wu, wd = call(
        first_layer_kernel,
        [
            ((half, d), f32), ((8, half), f32), ((half, d), f32), ((half, HD), f32), ((half, f), bf16),
            ((half, f), bf16), ((half, d), f32), ((half, HD), f32), ((half, d), bf16),
            ((d, d), bf16), ((d, f), bf16), ((f, d), bf16),
        ],
        [pos, q0, kv0, kv0r, table_col, lines, *w1, cur0, bup, ob, lg, lb],
        [((half, n), f32), ((half, HD), f32)],
        flops=2 * half * (2 * n * d + d * d + 2 * d * f),
        name="first_layer",
        after=(w2p[0],),
        vmem=8,
    )
    w2 = (w2p[0], w2p[1], swap_dp(w2p[0], 1), swap_dp(later(pos, w2p[1], "second_copy", (low1,)), 1))
    q1, kv1, wq1 = call(
        qkv_next_kernel,
        [((half, d), bf16), ((half, 2 * d), bf16), ((d, 3 * d), bf16)],
        [pos, low1, *w2, bqv],
        flops=2 * half * d * 3 * d,
        name="qkv_next",
        vmem=12,
    )
    kv1r = swap_dp(kv1, 1)
    lse1, final, gmix1, gbm1, delta1, keep1, send1, vec1 = call(
        last_layer_kernel,
        [
            ((8, half), f32), ((half, d), bf16), ((half, d), bf16), ((half, d), f32), ((8, half), f32),
            ((4, width * rest, HD), bf16), ((4, width * rest, HD), bf16), ((16, d), f32),
        ],
        [pos, q1, kv1, kv1r, table_col, lines, *w2, n2, cot, bup, ob, lg, lb],
        [
            ((half, n), f32), ((half, HD), f32), ((half, d), f32), ((d, d), bf16), ((d, f), bf16), ((f, d), bf16),
            ((half, d), f32), ((half, HD), f32), ((half, f), bf16), ((half, f), bf16), ((half, d), f32),
            ((half, HD), f32), ((half, d), bf16), ((half, f), bf16), ((half, d), bf16), ((f, d), bf16), ((d, f), bf16),
            ((d, d), bf16),
        ],
        flops=2 * half * (2 * n * d + d * d + 2 * d * f) * 3,
        name="last_layer",
        vmem=18,
    )
    final_rows = from_sequences(final, z)
    four1 = split(pos, keep1, swap_dp(send1, 1), "add_pair_last")
    def attention_back(q, kv, kvr, delta, gmix, lse, name, after=()):
        dq, dkva, dkvb = call(
            attention_back_kernel,
            [((half, d), bf16), ((half, 2 * d), bf16), ((half, 2 * d), bf16)],
            [pos, gmix, delta, q, kvr, kv, lse, key_col, lines],
            [((n, half), f32), ((d // HD, HD, half), f32)],
            flops=2 * half * 5 * n * d,
            name=name,
            vmem=10,
            after=after,
        )
        return dq, dkva, swap_dp(dkvb, 1)

    dq1, dkva1, dkvr1 = attention_back(q1, kv1, kv1r, delta1, gmix1, lse1, "attention_back_last")
    gmix0, gbm0, delta0, keep2, send2, vec = call(
        middle_kernel,
        [
            ((half, d), bf16), ((half, d), f32), ((8, half), f32),
            ((4, width * (first + rest), HD), bf16), ((4, width * (first + rest), HD), bf16), ((24, d), f32),
        ],
        [
            pos, dq1, dkva1, dkvr1, wq1, gbm1, n2, inv2, wd, dgel, wu, n1, inv1, wo, act, mix0, vec1, lg, lb,
        ],
        [
            ((half, 3 * d), bf16), ((d, 3 * d), bf16), ((half, d), f32),
            ((half, d), bf16), ((half, f), bf16), ((half, d), bf16),
            ((f, d), bf16), ((d, f), bf16), ((d, d), bf16),
        ],
        flops=2 * half * (6 * d * d + 2 * d * d + 4 * d * f),
        name="middle",
        after=four1,
        vmem=13,
    )
    two1 = split(pos, four1[0], swap_dp(four1[1], 2, 4), "add_plane_last")
    four2 = split(pos, keep2, swap_dp(send2, 1), "add_pair")
    dq0, dkva0, dkvr0 = attention_back(
        q0, kv0, kv0r, delta0, gmix0, lse0, "attention_back_first", (*four2, *two1, final_rows)
    )
    two2 = split(pos, four2[0], swap_dp(four2[1], 2, 4), "add_plane")
    shares1 = call(
        join_kernel,
        [((rest, HD), bf16)] * width,
        [pos, two1[0], swap_dp(two1[1], 4, 2)],
        name="join_last",
        vmem=8,
    )
    shared_rows = -(-(24 + fdim) // 128) * 128
    share = shared_rows // 8 * (d // HD)
    keep3, send3, gnorm, sums = call(
        entry_kernel,
        [
            ((4, width * first + share, HD), bf16), ((4, width * first + share, HD), bf16),
            ((half, fdim), f32), ((16, fdim), f32),
        ],
        [pos, dq0, dkva0, dkvr0, low0, wq0, gbm0, normed, enc_w, feat_own, vec, stats],
        [((half, 3 * d), bf16), ((d, 3 * d), bf16), ((shared_rows, d), f32)],
        flops=2 * half * (6 * d * d + 2 * d * HD),
        name="entry",
        after=(*two2, *shares1),
        vmem=12,
    )
    shares2 = call(
        join_kernel,
        [((first + rest, HD), bf16)] * width,
        [pos, two2[0], swap_dp(two2[1], 4, 2)],
        name="join",
        vmem=10,
    )
    four3 = split(pos, keep3, swap_dp(send3, 1), "add_pair_entry")
    two3 = split(pos, four3[0], swap_dp(four3[1], 2, 4), "add_plane_entry")
    shares3 = call(
        join_last_kernel,
        [((first + share, HD), bf16)] * width,
        [pos, two3[0], swap_dp(two3[1], 4, 2)],
        name="join_entry",
        vmem=6,
    )
    piece = jnp.concatenate([sum_z([sum_far(part) for part in shares1]), sum_z([sum_far(part) for part in shares2])])
    r1 = over_pair(*over_plane(pos, piece, "results_plane"))
    r2 = over_pair(*over_plane(pos, sum_z([sum_far(part) for part in shares3]), "results_plane_entry"))
    (g_feat,) = call(
        features_back_kernel,
        [((half, fdim), f32)],
        [pos, gnorm, feat_own, stats, sums, swap_dp(sums, 1)],
        name="features_back",
        vmem=6,
    )
    grad_features = from_sequences(g_feat, z)
    g_qkv, g_out, g_up, g_down, g_enc_w, g_enc_b, g_bqv, g_ob, g_lg, g_lb, g_bup = call(
        result_kernel,
        [
            ((layers, 3, d, HD), f32), ((layers, HD, d), f32), ((layers, d, f_part), f32), ((layers, f_part, d), f32),
            ((fdim, d), f32), ((1, d), f32), ((layers, 2, HD), f32), ((layers, 2, d), f32), ((layers, 2, d), f32),
            ((layers, 2, d), f32), ((layers, f_part), f32),
        ],
        [pos, *r1, *r2],
        [((shared_rows, d), f32)],
        name="results",
        vmem=10,
    )
    return (
        final_rows, grad_features, g_enc_w, g_enc_b[0], g_qkv, g_bqv, g_out, g_ob, g_lg, g_lb, g_up, g_bup, g_down,
    )


def solution(mesh):
    size, width = mesh.shape["dp"], mesh.shape["tensor"]
    mesh = jax.sharding.Mesh(mesh.devices.reshape(size // 8, 4, 2, width), ("far", "plane", "pair", "tensor"))
    dp = ("far", "plane", "pair")
    rows, ids = P("tensor", dp, None), P(None, dp)
    qkv, bqv = P(None, None, None, "tensor"), P(None, None, "tensor")
    mid, last = P(None, "tensor", None), P(None, None, "tensor")
    in_specs = (rows, ids, ids, P(), P(), qkv, bqv, mid, P(), P(), P(), last, P(None, "tensor"), mid, rows)
    out_specs = (rows, rows, P(), P(), qkv, bqv, mid, P(), P(), P(), last, P(None, "tensor"), mid)
    return jax.shard_map(local, mesh=mesh, in_specs=in_specs, out_specs=out_specs, check_vma=False)
```

```python
import functools
import math

import jax
import jax.numpy as jnp
from jax import lax
from jax.experimental import pallas as pl
from jax.experimental.pallas import tpu as pltpu
from jax.sharding import PartitionSpec as P

HD = 128
NTAB = 5
spread_floor = 0.1
norm_eps = 1e-05
f32 = jnp.float32
bf16 = jnp.bfloat16
LOG2E = 1.4426950408889634
MIB = 1024 * 1024


def mm(a, b):
    return lax.dot_general(a, b, (((1,), (0,)), ((), ())), preferred_element_type=f32)


def mm_nt(a, b):
    return lax.dot_general(a, b, (((1,), (1,)), ((), ())), preferred_element_type=f32)


def mm_tn(a, b):
    return lax.dot_general(a, b, (((0,), (0,)), ((), ())), preferred_element_type=f32)


class Stage:
    def __init__(self, loads, stores):
        self.loads = {id(ref): copy for ref, copy in loads}
        self.stores = {id(ref): copy for ref, copy in stores}
        self.started = []
        for copy in self.loads.values():
            copy.start()

    def need(self, *refs):
        for ref in refs:
            copy = self.loads.pop(id(ref), None)
            if copy is not None:
                copy.wait()

    def done(self, *refs):
        for ref in refs:
            copy = self.stores.pop(id(ref), None)
            if copy is not None:
                copy.start()
                self.started.append(copy)

    def finish(self):
        for copy in self.stores.values():
            copy.start()
        for copy in list(self.loads.values()) + self.started + list(self.stores.values()):
            copy.wait()


def call(body, outs, args, scratch=(), flops=0, name=None, after=(), far=(), vmem=16, staged=False):
    shapes = [jax.ShapeDtypeStruct(shape, dtype) for shape, dtype in outs]
    size = lambda a: a.size * a.dtype.itemsize
    moved = sum(size(a) for a in args) + sum(size(a) for a in shapes)
    count, results, extra = len(args), len(shapes), len(scratch)
    large_in = [at for at in range(1, count) if staged and at not in far and size(args[at]) >= 65536]
    large_out = [at for at in range(results) if staged and size(shapes[at]) >= 65536]
    near = pl.BlockSpec(memory_space=pltpu.VMEM)
    hbm = pl.BlockSpec(memory_space=pl.ANY)

    def run(*refs):
        ins = list(refs[:count])
        out = list(refs[count + len(after) :][:results])
        rest = refs[count + len(after) + results :]
        mine, rest = rest[:extra], rest[extra:]
        held_in, held_out, sems = rest[: len(large_in)], rest[len(large_in) : -1], rest[-1]
        loads, stores = [], []
        for at, ref in zip(large_in, held_in):
            loads.append((ref, pltpu.make_async_copy(ins[at], ref, sems.at[len(loads)])))
            ins[at] = ref
        for at, ref in zip(large_out, held_out):
            stores.append((ref, pltpu.make_async_copy(ref, out[at], sems.at[len(loads) + len(stores)])))
            out[at] = ref
        stage = Stage(loads, stores)
        body(stage, *ins, *out, *mine)
        stage.finish()

    return pl.pallas_call(
        run,
        out_shape=shapes,
        in_specs=[pl.BlockSpec(memory_space=pltpu.SMEM)]
        + [hbm if at in far or at in large_in else near for at in range(1, count)]
        + [hbm] * len(after),
        out_specs=[hbm if at in large_out else near for at in range(results)],
        scratch_shapes=[
            pltpu.SemaphoreType.DMA(shape) if dtype is None else pltpu.VMEM(shape, dtype) for shape, dtype in scratch
        ]
        + [pltpu.VMEM(args[at].shape, args[at].dtype) for at in large_in]
        + [pltpu.VMEM(shapes[at].shape, shapes[at].dtype) for at in large_out]
        + [pltpu.SemaphoreType.DMA((max(1, len(large_in) + len(large_out)),))],
        compiler_params=pltpu.CompilerParams(vmem_limit_bytes=vmem * MIB),
        cost_estimate=pl.CostEstimate(flops=flops, bytes_accessed=moved, transcendentals=0),
        name=name,
    )(*args, *after)


def blocks(kind, d, f_part, q, z):
    if kind == "qkv":
        n = d // 8
        return [(c * n, n, q * n, c * d + z * HD) for c in range(3)]
    if kind == "out":
        n = HD // 8
        return [(c * n, n, z * HD + q * n, c * HD) for c in range(d // HD)]
    if kind == "up":
        n = d // 8
        return [(c * n, n, q * n, z * f_part + c * HD) for c in range(f_part // HD)]
    n = f_part // 8
    return [(c * n, n, z * f_part + q * n, c * HD) for c in range(d // HD)]


def aligned(value, unit):
    return value if isinstance(value, int) else pl.multiple_of(value, unit)


def unpack(pos, buffers, row0, kind, whole, d, f_part):
    base = 0
    for src in buffers:

        def step(e, carry, src=src, base=base):
            q = pos[base + e]
            for k in range(src.shape[1]):
                for at, n, row, col in blocks(kind, d, f_part, q, pos[8 + k]):
                    whole[pl.ds(aligned(row, 16), n), pl.ds(aligned(col, HD), HD)] = src[
                        e, k, row0 + at : row0 + at + n, :
                    ]
            return carry

        lax.fori_loop(0, src.shape[0], step, 0)
        base += src.shape[0]


def pack(pos, whole, row0, kind, halves, d, f_part, width, piece, order=12):
    for c in range(2):
        dst = halves[c]

        def step(e, carry, dst=dst, c=c):
            q = pos[order + c * 4 + e]
            for k in range(width):
                for at, n, row, col in blocks(kind, d, f_part, q, pos[8 + k]):
                    at += k * piece + row0
                    dst[e, at : at + n, :] = whole[
                        pl.ds(aligned(row, 16), n), pl.ds(aligned(col, HD), HD)
                    ]
            return carry

        lax.fori_loop(0, 4, step, 0)


def copy_all(pairs, sems):
    copies = [pltpu.make_async_copy(src, dst, sems.at[at]) for at, (src, dst) in enumerate(pairs)]
    for copy in copies:
        copy.start()
    for copy in copies:
        copy.wait()


def qkv_copies(l, q, wqkv, to):
    n = wqkv.shape[2] // 8
    row = pl.multiple_of(q * n, 16)
    return [(wqkv.at[l, c, pl.ds(row, n), :], to.at[pl.ds(c * n, n), :]) for c in range(3)]


def pack_first_kernel(stage, pos, wqkv, bqv, bup, g0, sems):
    d, f_part = wqkv.shape[2], bup.shape[1]
    rows = [bqv[0], bqv[1]]
    rows += [bup[l : l + 1, c * HD : (c + 1) * HD] for l in range(2) for c in range(f_part // HD)]
    rows = jnp.concatenate(rows, 0)
    high = rows.astype(bf16).astype(f32)
    g0[3 * d // 8 :, :] = jnp.concatenate([high, rows - high], 0).astype(bf16)
    copy_all(qkv_copies(0, pos[0], wqkv, g0), sems)


def rest_copies(l, q, wout, wup, wdown, to, base):
    d, f_part = wup.shape[1], wup.shape[2]
    n, m, r = d // 8, HD // 8, f_part // 8
    pairs = []
    for src, count, cols in ((wout, m, d), (wup, n, f_part), (wdown, r, d)):
        for c in range(cols // HD):
            block = src.at[l, pl.ds(pl.multiple_of(q * count, 16), count), pl.ds(c * HD, HD)]
            pairs.append((block, to.at[pl.ds(base, count), :]))
            base += count
    return pairs


def pack_rest_kernel(stage, pos, wout, wup, wdown, g1, sems):
    copy_all(rest_copies(0, pos[0], wout, wup, wdown, g1, 0), sems)


def pack_second_kernel(stage, pos, wqkv, wout, wup, wdown, g2, sems):
    pairs = qkv_copies(1, pos[0], wqkv, g2)
    copy_all(pairs + rest_copies(1, pos[0], wout, wup, wdown, g2, 3 * wqkv.shape[2] // 8), sems)


def add_kernel(stage, pos, a, b, low, high):
    m = a.shape[0] // 2
    low[...] = (a[:m].astype(f32) + b[:m].astype(f32)).astype(bf16)
    high[...] = (a[m:].astype(f32) + b[m:].astype(f32)).astype(bf16)


def join_kernel(stage, pos, b, c, *shares):
    m = b.shape[1] // len(shares)
    for k, out in enumerate(shares):
        at = slice(k * m, (k + 1) * m)
        out[...] = (b[0, at, :].astype(f32) + c[0, at, :].astype(f32)).astype(bf16)


def join_last_kernel(stage, pos, b, c, *shares):
    width = len(shares)
    m = (b.shape[1] - shares[0].shape[0]) // (width - 1)
    for k, out in enumerate(shares):
        at = slice(k * m, (k + 1) * m)
        out[:m, :] = (b[0, at, :].astype(f32) + c[0, at, :].astype(f32)).astype(bf16)
        at = slice(width * m, b.shape[1])
        out[m:, :] = (b[0, at, :].astype(f32) + c[0, at, :].astype(f32)).astype(bf16)


def gelu_pair(h):
    bell = jnp.exp2(h * h * (-0.5 * LOG2E))
    t = 1.0 / (1.0 + jnp.abs(h) * (0.3275911 * math.sqrt(0.5)))
    poly = 0.5 * 1.061405429
    for c in (-1.453152027, 1.421413741, -0.284496736, 0.254829592):
        poly = poly * t + 0.5 * c
    tail = poly * t * bell
    cdf = jnp.where(h < 0.0, tail, 1.0 - tail)
    return h * cdf, cdf + h * bell * (1.0 / math.sqrt(2.0 * math.pi))


def normalize(u):
    centre = u - jnp.mean(u, -1, keepdims=True)
    inv = lax.rsqrt(jnp.mean(centre * centre, -1, keepdims=True) + norm_eps)
    return centre * inv, inv


def norm_back(grad, normal, inv, gain):
    e = grad * gain
    return (e - jnp.mean(e, -1, keepdims=True) - normal * jnp.mean(e * normal, -1, keepdims=True)) * inv


def rowsum(x):
    return jnp.sum(x, 0, keepdims=True)


def row_codes(block, features):
    return block[:, features : features + 1].astype(jnp.int32)


def query_mask(code):
    lane = lax.broadcasted_iota(jnp.int32, (code.shape[0], HD), 1)
    return jnp.where((lane > NTAB) | (lane == (code >> 1)), 0.0, -1e30).astype(bf16)


def key_mask(code):
    lane = lax.broadcasted_iota(jnp.int32, (code.shape[0], HD), 1)
    return jnp.where((lane == (code >> 1)) | ((lane == NTAB) & ((code & 1) == 0)), 1.0, 0.0).astype(bf16)


def features_kernel(stage, pos, fa, fb, encw, encb, cur, low, normed, stats, qmask, kmask):
    stage.need(fa, fb, encw)
    features = encw.shape[0]
    half = fa.shape[0]
    own, other = fa[:, :features], fb[:, :features]
    code_a, code_b = row_codes(fa, features), row_codes(fb, features)
    qmask[...] = query_mask(code_a)
    kmask[:half, :] = key_mask(code_a)
    kmask[half:, :] = key_mask(code_b)
    mean_rows = jnp.zeros_like(own)
    scale_rows = jnp.zeros_like(own)
    for t in range(NTAB):
        pa = (code_a == 2 * t + 1).astype(f32)
        pb = (code_b == 2 * t + 1).astype(f32)
        count = rowsum(pa) + rowsum(pb)
        mean = (rowsum(pa * own) + rowsum(pb * other)) / count
        da, db = own - mean, other - mean
        excess = (rowsum(pa * da * da) + rowsum(pb * db * db)) / count
        scale = lax.rsqrt(jnp.maximum(excess, spread_floor))
        stats[t : t + 1, :] = mean
        stats[8 + t : 9 + t, :] = scale
        stats[16 + t : 17 + t, :] = excess
        stats[24 + t : 25 + t, :] = jnp.broadcast_to(count, mean.shape)
        here = (code_a >> 1) == t
        mean_rows = jnp.where(here, mean, mean_rows)
        scale_rows = jnp.where(here, scale, scale_rows)
    z = ((own - mean_rows) * scale_rows).astype(bf16)
    normed[...] = z
    out = mm(z, encw[...]) + encb[...].reshape(1, -1)
    cur[...] = out
    low[...] = out.astype(bf16)


def project(stage, x, w, bias, q, kv, layer, d):
    kv[:, :d] = mm(x, w[:, d : 2 * d]).astype(bf16)
    kv[:, d:] = (mm(x, w[:, 2 * d :]) + bias[2 * layer + 1 : 2 * layer + 2, :]).astype(bf16)
    stage.done(kv)
    q[...] = (mm(x, w[:, :d]) + bias[2 * layer : 2 * layer + 1, :]).astype(bf16)


def qkv_first_kernel(stage, pos, low, ga, gb, gc, gd, q, kv, w, bqv, bup):
    d = low.shape[1]
    buffers = (ga, gb, gc, gd)
    stage.need(*buffers)
    unpack(pos, buffers, 0, "qkv", w, d, 0)
    stage.done(w)
    base = 3 * d // 8
    f_part = 2 * HD
    for k in range(ga.shape[1]):
        z = pos[8 + k]
        rows = ga[0, k, base : base + 16, :].astype(f32)
        rows = rows[:8] + rows[8:]
        for j in range(4):
            bqv[j : j + 1, pl.ds(pl.multiple_of(z * HD, HD), HD)] = rows[j : j + 1]
            col = z * f_part + (j % 2) * HD
            bup[j // 2 : j // 2 + 1, pl.ds(pl.multiple_of(col, HD), HD)] = rows[4 + j : 5 + j]
    stage.need(low)
    project(stage, low[...], w, bqv, q, kv, 0, d)


def qkv_next_kernel(stage, pos, low, ga, gb, gc, gd, bqv, q, kv, w):
    d = low.shape[1]
    stage.need(ga, gb, gc, gd)
    unpack(pos, (ga, gb, gc, gd), 0, "qkv", w, d, 0)
    stage.done(w)
    stage.need(low)
    project(stage, low[...], w, bqv, q, kv, 1, d)


def attention_rows(rows, q, kva, kvb, qmask, kmask, mix, lse, d):
    n = kva.shape[0]
    factor = LOG2E / math.sqrt(HD)
    count = rows.size
    lane = lax.broadcasted_iota(jnp.int32, (count, HD), 1)
    totals = jnp.zeros((count, HD), f32)
    for h in range(d // HD):
        cols = slice(h * HD, (h + 1) * HD)
        vals = slice(d + h * HD, d + (h + 1) * HD)
        qh = jnp.concatenate([q[rows, cols], qmask[rows, :]], 1)
        ta = mm_nt(qh, jnp.concatenate([kva[:, cols], kmask[:n, :]], 1))
        tb = mm_nt(qh, jnp.concatenate([kvb[:, cols], kmask[n:, :]], 1))
        top = jnp.maximum(jnp.max(ta, -1, keepdims=True), jnp.max(tb, -1, keepdims=True)) * factor
        ea, eb = jnp.exp2(ta * factor - top), jnp.exp2(tb * factor - top)
        total = jnp.sum(ea, -1, keepdims=True) + jnp.sum(eb, -1, keepdims=True)
        out = mm(ea.astype(bf16), kva[:, vals]) + mm(eb.astype(bf16), kvb[:, vals])
        mix[rows, cols] = out / total
        totals = jnp.where(lane == h, top + jnp.log2(total), totals)
    lse[rows, :] = totals


def layer_rows(rows, cur, mix, wo, wu, wd, bup, ob, lg, lb, layer, n1, inv1, act, dgel, n2, inv2):
    l = layer
    u = cur + mm(mix[rows, :].astype(bf16), wo[...]) + ob[l, 0:1, :]
    normal, inv = normalize(u)
    n1[rows, :] = normal
    inv1[rows, :] = jnp.broadcast_to(inv, (rows.size, HD))
    middle = normal * lg[l, 0:1, :] + lb[l, 0:1, :]
    hidden = mm(middle.astype(bf16), wu[...]) + bup[l : l + 1, :]
    value, slope = gelu_pair(hidden)
    value = value.astype(bf16)
    act[rows, :] = value
    dgel[rows, :] = slope.astype(bf16)
    u = middle + mm(value, wd[...]) + ob[l, 1:2, :]
    normal, inv = normalize(u)
    n2[rows, :] = normal
    inv2[rows, :] = jnp.broadcast_to(inv, (rows.size, HD))
    return normal * lg[l, 1:2, :] + lb[l, 1:2, :]


def attention(stage, q, kva, kvb, qmask, kmask, mix, lse, raw, d):
    stage.need(q, kva, kvb)

    def step(i, carry):
        rows = pl.ds(pl.multiple_of(i * CHUNK, CHUNK), CHUNK)
        attention_rows(rows, q, kva, kvb, qmask, kmask, mix, raw, d)
        return carry

    lax.fori_loop(0, q.shape[0] // CHUNK, step, 0)
    stage.done(mix)
    lse[...] = raw[...].T[:8]


def unpack_rest(stage, pos, buffers, row0, wo, wu, wd, d, f_part):
    m = HD // 8 * (d // HD)
    stage.need(*buffers)
    unpack(pos, buffers, row0, "out", wo, d, f_part)
    unpack(pos, buffers, row0 + m, "up", wu, d, f_part)
    unpack(pos, buffers, row0 + m + d // 8 * (f_part // HD), "down", wd, d, f_part)
    stage.done(wo, wu, wd)


def first_layer_kernel(
    stage, pos, q, kva, kvb, qmask, kmask, ga, gb, gc, gd, cur, bup, ob, lg, lb,
    mix, lse, n1, inv1, act, dgel, n2, inv2, low, wo, wu, wd,
    raw,
):
    d = q.shape[1]
    attention(stage, q, kva, kvb, qmask, kmask, mix, lse, raw, d)
    unpack_rest(stage, pos, (ga, gb, gc, gd), 0, wo, wu, wd, d, wu.shape[1] // ga.shape[1])
    stage.need(cur)

    def step(i, carry):
        rows = pl.ds(pl.multiple_of(i * CHUNK, CHUNK), CHUNK)
        out = layer_rows(
            rows, cur[rows, :], mix, wo, wu, wd, bup, ob, lg, lb, 0, n1, inv1, act, dgel, n2, inv2
        )
        low[rows, :] = out.astype(bf16)
        return carry

    lax.fori_loop(0, q.shape[0] // CHUNK, step, 0)


CHUNK = 512


def ffn_back(
    stage, pos, grad, l, n1, inv1, act, dgel, n2, inv2, mix, wo, wu, wd, lg, lb,
    gmix, gbm, delta, keep, send, vec, vrow, gl, gh, g1, dwd, dwu, dwo, d, f_part, width, piece, order, base,
):
    gain0, gain1 = lg[l, 0:1, :], lg[l, 1:2, :]
    shift0 = lb[l, 0:1, :]
    f = wu.shape[1]

    def step(i, carry):
        rows = pl.ds(pl.multiple_of(i * CHUNK, CHUNK), CHUNK)
        top = grad[rows, :].astype(f32)
        normal = n2[rows, :]
        bo = norm_back(top, normal, inv2[rows, :1], gain1)
        low = bo.astype(bf16)
        gl[rows, :] = low
        back = mm_nt(low, wd[...])
        back = (back * dgel[rows, :].astype(f32)).astype(bf16)
        gh[rows, :] = back
        gm = bo + mm_nt(back, wu[...])
        first = n1[rows, :]
        bm = norm_back(gm, first, inv1[rows, :1], gain0)
        gbm[rows, :] = bm
        attn = bm.astype(bf16)
        g1[rows, :] = attn
        gmix[rows, :] = mm_nt(attn, wo[...]).astype(bf16)
        sums = (
            rowsum(gm * first),
            rowsum(top * normal),
            rowsum(gm),
            rowsum(top),
            rowsum(attn.astype(f32)),
            rowsum(low.astype(f32)),
        )
        hidden = rowsum(back.astype(f32))
        for j in range(6):
            vec[vrow + j : vrow + j + 1, :] += sums[j]
        for j in range(f // d):
            at = vrow + 8 + j
            vec[at : at + 1, :] += hidden[:, j * d : (j + 1) * d]
        return carry

    lax.fori_loop(0, act.shape[0] // CHUNK, step, 0)
    stage.done(gmix, gbm)
    for h in range(d // HD):
        cols = slice(h * HD, (h + 1) * HD)
        prod = gmix[:, cols].astype(f32) * mix[:, cols]
        delta[h : h + 1, :] = jnp.sum(prod.T, 0, keepdims=True)
    m = HD // 8 * (d // HD)
    dwd[...] = mm_tn(act[...], gl[...]).astype(bf16)
    middle = (n1[...] * gain0 + shift0).astype(bf16)
    dwu[...] = mm_tn(middle, gh[...]).astype(bf16)
    dwo[...] = mm_tn(mix[...].astype(bf16), g1[...]).astype(bf16)
    pack(pos, dwd, base + m + d // 8 * (f_part // HD), "down", (keep, send), d, f_part, width, piece, order)
    pack(pos, dwu, base + m, "up", (keep, send), d, f_part, width, piece, order)
    pack(pos, dwo, base, "out", (keep, send), d, f_part, width, piece, order)


def last_layer_kernel(
    stage, pos, q, kva, kvb, qmask, kmask, ga, gb, gc, gd, n2in, cot, bup, ob, lg, lb,
    lse, final, gmix, gbm, delta, keep, send, vec,
    raw, mix, wo, wu, wd, n1, inv1, act, dgel, n2, inv2, gl, gh, g1, dwd, dwu, dwo,
):
    d = q.shape[1]
    width = ga.shape[1]
    f_part = wu.shape[1] // width
    attention(stage, q, kva, kvb, qmask, kmask, mix, lse, raw, d)
    unpack_rest(stage, pos, (ga, gb, gc, gd), 3 * d // 8, wo, wu, wd, d, f_part)
    stage.need(n2in)

    def step(i, carry):
        rows = pl.ds(pl.multiple_of(i * CHUNK, CHUNK), CHUNK)
        cur = n2in[rows, :] * lg[0, 1:2, :] + lb[0, 1:2, :]
        out = layer_rows(
            rows, cur, mix, wo, wu, wd, bup, ob, lg, lb, 1, n1, inv1, act, dgel, n2, inv2
        )
        final[rows, :] = out.astype(bf16)
        return carry

    lax.fori_loop(0, q.shape[0] // CHUNK, step, 0)
    stage.done(final)
    vec[...] = jnp.zeros_like(vec)
    stage.need(cot)
    ffn_back(
        stage, pos, cot, 1, n1, inv1, act, dgel, n2, inv2, mix, wo, wu, wd, lg, lb,
        gmix, gbm, delta, keep, send, vec, 0, gl, gh, g1, dwd, dwu, dwo, d, f_part, width, keep.shape[1] // width, 0, 0,
    )


def attention_back_kernel(stage, pos, gmix, delta, q, kvb, kva, lse, qmask, kmask, dq, dkva, dkvb, acc):
    d = q.shape[1]
    n = kva.shape[0]
    scaling = 1.0 / math.sqrt(HD)
    factor = LOG2E * scaling
    block = 512
    stage.need(gmix)
    acc[...] = jnp.zeros_like(acc)
    stage.need(q)
    for src, dst, off in ((kvb, dkvb, n), (kva, dkva, 0)):
        stage.need(src)

        def step(i, carry, src=src, dst=dst, off=off):
            rows = pl.ds(pl.multiple_of(i * block, block), block)
            brow = pl.ds(pl.multiple_of(off + i * block, block), block)
            for h in range(d // HD):
                cols = slice(h * HD, (h + 1) * HD)
                vals = slice(d + h * HD, d + (h + 1) * HD)
                qh, gh = q[:, cols], gmix[:, cols]
                kh, vh = src[rows, cols], src[rows, vals]
                scores = mm_nt(
                    jnp.concatenate([kh, kmask[brow, :]], 1), jnp.concatenate([qh, qmask[...]], 1)
                )
                probs = jnp.exp2(scores * factor - lse[h : h + 1, :])
                ds = (probs * (mm_nt(vh, gh) - delta[h : h + 1, :])).astype(bf16)
                dst[rows, vals] = mm(probs.astype(bf16), gh).astype(dst.dtype)
                dst[rows, cols] = (mm(ds, qh) * scaling).astype(dst.dtype)
                acc[h, :, :] += mm_tn(kh, ds)
            return carry

        lax.fori_loop(0, n // block, step, 0)
        stage.done(dst)
    for h in range(d // HD):
        dq[:, h * HD : (h + 1) * HD] = (acc[h].T * scaling).astype(bf16)


def projection_back(
    stage, pos, dq, dkva, dkvr, low, w, gbm, proj, dw, keep, send, vec, vrow, d, width, piece, order
):
    stage.need(dq, dkva, dkvr)
    proj[:, :d] = dq[...]
    proj[:, d:] = (dkva[...].astype(f32) + dkvr[...].astype(f32)).astype(bf16)
    vec[vrow : vrow + 1, :] = rowsum(dq[...].astype(f32))
    vec[vrow + 1 : vrow + 2, :] = rowsum(proj[:, 2 * d :].astype(f32))
    dw[...] = mm_tn(low(), proj[...]).astype(bf16)
    stage.need(w, gbm)
    grad = gbm[...] + mm_nt(proj[...], w[...])
    pack(pos, dw, 0, "qkv", (keep, send), d, 0, width, piece, order)
    return grad


def middle_kernel(
    stage, pos, dq, dkva, dkvr, w, gbm1, n2, inv2, wd, dgel, wu, n1, inv1, wo, act, mix, vec1, lg, lb,
    gmix, gbm, delta, keep, send, vec,
    proj, dw, grad, gl, gh, g1, dwd, dwu, dwo,
):
    d = grad.shape[1]
    width = d // HD
    first = 3 * d // 8
    piece = keep.shape[1] // width
    vec[...] = jnp.zeros_like(vec)
    for j in range(10):
        vec[10 + j : 11 + j, :] = vec1[j : j + 1, :]

    def low():
        return (n2[...] * lg[0, 1:2, :] + lb[0, 1:2, :]).astype(bf16)

    grad[...] = projection_back(
        stage, pos, dq, dkva, dkvr, low, w, gbm1, proj, dw, keep, send, vec, 16, d, width, piece, 0
    )
    ffn_back(
        stage, pos, grad, 0, n1, inv1, act, dgel, n2, inv2, mix, wo, wu, wd, lg, lb,
        gmix, gbm, delta, keep, send, vec, 0, gl, gh, g1, dwd, dwu, dwo, d, wu.shape[1] // width,
        width, piece, 0, first,
    )


def entry_kernel(
    stage, pos, dq, dkva, dkvr, low0, w0, gbm0, normed, encw, fa, vec, stats,
    keep, send, gnorm, sums,
    proj, dw, shared,
):
    d = dq.shape[1]
    features = encw.shape[0]
    width = d // HD
    first = 3 * d // 8
    shared[...] = jnp.zeros_like(shared)
    shared[:24, :] = vec[...]
    def low():
        stage.need(low0)
        return low0[...]

    grad = projection_back(
        stage, pos, dq, dkva, dkvr, low, w0, gbm0, proj, dw, keep, send, shared, 6, d, width, first, 0
    )
    stage.need(normed, encw, fa)
    low = grad.astype(bf16)
    shared[20:21, :] = rowsum(low.astype(f32))
    shared[24 : 24 + features, :] = mm_tn(normed[...], low)
    back = mm_nt(low, encw[...])
    gnorm[...] = back
    code = row_codes(fa, features) >> 1
    centred = fa[:, :features]
    sums[...] = jnp.zeros_like(sums)
    for t in range(NTAB):
        here = code == t
        part = jnp.where(here, back, 0.0)
        sums[t : t + 1, :] = rowsum(part)
        sums[8 + t : 9 + t, :] = rowsum(part * (centred - stats[t : t + 1, :]))
    share = shared.shape[0] // 8
    for c, dst in ((0, keep), (1, send)):

        def step(e, carry, dst=dst, c=c):
            row = pl.multiple_of(pos[c * 4 + e] * share, 8)
            for j in range(d // HD):
                piece = shared[pl.ds(row, share), j * HD : (j + 1) * HD].astype(bf16)
                at = width * first + j * share
                dst[e, at : at + share, :] = piece
            return carry

        lax.fori_loop(0, 4, step, 0)


def features_back_kernel(stage, pos, gnorm, fa, stats, mine, theirs, out):
    total = mine[...] + theirs[...]
    stage.need(gnorm, fa)
    back = gnorm[...]
    code = row_codes(fa, back.shape[1])
    x = fa[:, : back.shape[1]]
    scale_rows = jnp.zeros_like(x)
    flat = jnp.zeros_like(x)
    slope = jnp.zeros_like(x)
    for t in range(NTAB):
        mean, scale = stats[t : t + 1, :], stats[8 + t : 9 + t, :]
        excess, count = stats[16 + t : 17 + t, :], stats[24 + t : 25 + t, :]
        plain, centred = total[t : t + 1, :], total[8 + t : 9 + t, :]
        g_excess = jnp.where(excess > spread_floor, -0.5 * scale * scale * scale * centred, 0.0)
        g_mean = -scale * plain - 2.0 * mean * g_excess
        scale_rows = jnp.where((code >> 1) == t, scale, scale_rows)
        chosen = code == 2 * t + 1
        flat = jnp.where(chosen, g_mean / count, flat)
        slope = jnp.where(chosen, 2.0 * g_excess / count, slope)
    out[...] = back * scale_rows + flat + x * slope


def result_kernel(
    stage, pos, ra, rb, rc, rd, ea, eb, ec, ed, gqkv, gout, gup, gdown, genc_w, genc_b, gbqv, gob, glg, glb, gbup, rows
):
    d, f_part = gqkv.shape[2], gup.shape[2]
    n, m, r = d // 8, HD // 8, f_part // 8
    first = 3 * n
    share = rows.shape[0] // 8
    after = m * (d // HD) + n * (f_part // HD) + r * (d // HD)

    def rest(l, src, e, q, base):
        for c in range(d // HD):
            gout[l, pl.ds(pl.multiple_of(q * m, 16), m), c * HD : (c + 1) * HD] = src[
                e, base + c * m : base + (c + 1) * m, :
            ].astype(f32)
        base += d // HD * m
        for c in range(f_part // HD):
            gup[l, pl.ds(pl.multiple_of(q * n, 16), n), c * HD : (c + 1) * HD] = src[
                e, base + c * n : base + (c + 1) * n, :
            ].astype(f32)
        base += f_part // HD * n
        for c in range(d // HD):
            gdown[l, pl.ds(pl.multiple_of(q * r, 16), r), c * HD : (c + 1) * HD] = src[
                e, base + c * r : base + (c + 1) * r, :
            ].astype(f32)

    for part, (src, end) in enumerate(((ra, ea), (rb, eb), (rc, ec), (rd, ed))):
        stage.need(src, end)

        def step(e, carry, part=part, src=src, end=end):
            q = pos[part * 2 + e]
            for l, ref, base in ((1, src, after), (0, end, 0)):
                for c in range(3):
                    gqkv[l, c, pl.ds(pl.multiple_of(q * n, 16), n), :] = ref[
                        e, base + c * n : base + (c + 1) * n, :
                    ].astype(f32)
            rest(1, src, e, q, 0)
            rest(0, src, e, q, after + first)
            for j in range(d // HD):
                rows[pl.ds(pl.multiple_of(q * share, 8), share), j * HD : (j + 1) * HD] = end[
                    e, first + j * share : first + (j + 1) * share, :
                ].astype(f32)
            return carry

        lax.fori_loop(0, src.shape[0], step, 0)
    z = pos[8]
    d = genc_w.shape[1]
    layers = gob.shape[0]
    genc_w[...] = rows[24 : 24 + genc_w.shape[0], :]
    genc_b[...] = rows[10 * layers : 10 * layers + 1, :]
    for l in range(layers):
        at = 10 * l
        for j in range(2):
            glg[l, j : j + 1, :] = rows[at + j : at + j + 1, :]
            glb[l, j : j + 1, :] = rows[at + 2 + j : at + 3 + j, :]
            gob[l, j : j + 1, :] = rows[at + 4 + j : at + 5 + j, :]
            gbqv[l, j : j + 1, :] = rows[at + 6 + j : at + 7 + j, pl.ds(pl.multiple_of(z * HD, HD), HD)]
        row = at + 8 + (z * f_part) // d
        col = pl.multiple_of((z * f_part) % d, HD)
        gbup[l : l + 1, :] = rows[pl.ds(row, 1), pl.ds(col, f_part)]


def swap_dp(values, even, odd=None):
    odd = even if odd is None else odd
    return lax.ppermute(values, ("plane", "pair"), [(i, i ^ (odd if i % 2 else even)) for i in range(8)])


def swap_z(values, mask):
    size = lax.axis_size("tensor")
    return lax.ppermute(values, "tensor", [(i, i ^ mask) for i in range(size)])


def relay_pairs(step):
    width = lax.axis_size("tensor")
    return [
        (p * width + z, z // 2 * width + 2 * p + (step ^ (z & 1))) for p in range(2) for z in range(width)
    ]


def pick(values, index, axis=0):
    return lax.dynamic_index_in_dim(values, index, axis, keepdims=False)


def to_sequences(one_block, z):
    got = [lax.ppermute(one_block(step ^ (z & 1)), ("pair", "tensor"), relay_pairs(step)) for step in range(2)]
    return jnp.concatenate(got)


def from_sequences(values, z, sent=None):
    part = values.shape[0] // 2
    got = [
        lax.ppermute(
            values[step * part : (step + 1) * part],
            ("pair", "tensor"),
            [(b, a) for a, b in relay_pairs(step)],
        )
        for step in range(2)
    ]
    if sent is not None:
        sent.extend(got)
    odd = (z & 1) == 1
    return jnp.stack([jnp.where(odd, got[1], got[0]), jnp.where(odd, got[0], got[1])], 1)


def stack_kernel(stage, pos, *refs):
    out = refs[-1]
    for at, ref in enumerate(refs[:-1]):
        out[at] = ref[...]


def stack(pos, pieces, name, after=()):
    shape = (len(pieces),) + pieces[0].shape
    return call(stack_kernel, [(shape, bf16)], [pos] + pieces, name=name, after=after, vmem=6)[0]


def copy_kernel(stage, pos, src, out):
    out[...] = src[...]


def later(pos, values, name, after):
    return call(copy_kernel, [(values.shape, values.dtype)], [pos, values], name=name, after=after, vmem=4)[0]


def over_z(pos, piece, name, after=()):
    pieces = [piece] + [swap_z(piece, k) for k in range(1, lax.axis_size("tensor"))]
    return stack(pos, pieces, name, after)


def over_plane(pos, piece, name, after=()):
    two = stack(pos, [piece, swap_dp(piece, 4, 2)], name, after)
    return two, swap_dp(two, 2, 4)


def over_pair(two, more):
    return two, more, swap_dp(two, 1), swap_dp(more, 1)


def add(a, b):
    return (a.astype(f32) + b.astype(f32)).astype(bf16)


def sum_far(values):
    return lax.psum(values.astype(f32), "far").astype(bf16) if lax.axis_size("far") > 1 else values


def split(pos, a, b, name, after=()):
    outs = [((a.shape[0] // 2,) + a.shape[1:], bf16)] * 2
    return call(add_kernel, outs, [pos, a, b], name=name, vmem=12, after=after)


def sum_z(shares):
    total = shares[0].astype(f32)
    for k in range(1, len(shares)):
        total = total + swap_z(shares[k], k).astype(f32)
    return total.astype(bf16)


def local(
    features,
    table_ids,
    train_flags,
    enc_w,
    enc_b,
    w_qkv,
    b_qv,
    w_out,
    out_bias,
    ln_gain,
    ln_bias,
    w_up,
    b_up,
    w_down,
    cotangent,
):
    part, _, fdim = features.shape
    width = lax.axis_size("tensor")
    layers, d, f_part = w_qkv.shape[0], w_qkv.shape[2], w_up.shape[2]
    f = f_part * width
    half = 2 * part
    n = 2 * half
    z, p, o = lax.axis_index("tensor"), lax.axis_index("pair"), lax.axis_index("plane")
    ox, oy = o & 1, o >> 1
    relative, absolute = [], []
    for c in range(2):
        for r1 in range(2):
            for r2 in range(2):
                pd = p ^ c
                rx, ry = jnp.where(pd == 0, r1, r2), jnp.where(pd == 0, r2, r1)
                relative.append(pd * 4 + (oy ^ ry) * 2 + (ox ^ rx))
                absolute.append(pd * 4 + r1 * 2 + r2)
    pos = jnp.stack(relative + [z ^ k for k in range(width)] + absolute).astype(jnp.int32)
    rest = HD // 8 * (d // HD) + d // 8 * (f_part // HD) + f_part // 8 * (d // HD)
    first = 3 * d // 8

    codes = lax.dynamic_slice_in_dim(table_ids, z * part, part) * 2
    codes = (codes + lax.dynamic_slice_in_dim(train_flags, z * part, part)).astype(f32)

    def feature_block(j):
        space = jnp.zeros((part, HD - fdim - 1), f32)
        return jnp.concatenate([pick(features, j, 1), pick(codes, j, 1)[:, None], space], 1)

    feat_own = to_sequences(feature_block, z)
    feat_other = swap_dp(feat_own, 1)
    (g0,) = call(
        pack_first_kernel,
        [((first + 16, HD), bf16)],
        [pos, w_qkv, b_qv, b_up],
        [((3,), None)],
        name="pack_first",
        vmem=4,
        far=(1,),
    )
    w0z = over_z(pos, g0, "first_z", (feat_own,))
    w0p = over_plane(pos, w0z, "first_plane", (feat_other,))
    w0 = over_pair(*w0p)
    (g1,) = call(
        pack_rest_kernel,
        [((rest, HD), bf16)],
        [pos, w_out, w_up, w_down],
        [((16,), None)],
        name="pack_rest",
        vmem=4,
        far=(1, 2, 3),
        after=(w0z,),
    )
    w1z = over_z(pos, g1, "rest_z")
    cur0, low0, normed, stats, qmask, kmask = call(
        features_kernel,
        [
            ((half, d), f32), ((half, d), bf16), ((half, fdim), bf16), ((32, fdim), f32),
            ((half, HD), bf16), ((n, HD), bf16),
        ],
        [pos, feat_own, feat_other, enc_w, enc_b[None]],
        flops=2 * half * d * HD,
        name="features",
        vmem=8,
    )
    (g2,) = call(
        pack_second_kernel,
        [((first + rest, HD), bf16)],
        [pos, w_qkv, w_out, w_up, w_down],
        [((16,), None)],
        name="pack_second",
        vmem=4,
        far=(1, 2, 3, 4),
        after=(w1z,),
    )
    w1p = over_plane(pos, w1z, "rest_plane", (low0, g2, w0p[1]))
    w1 = over_pair(*w1p)
    q0, kv0, wq0, bqv, bup = call(
        qkv_first_kernel,
        [((half, d), bf16), ((half, 2 * d), bf16), ((d, 3 * d), bf16), ((8, d), f32), ((8, f), f32)],
        [pos, low0, *w0],
        flops=2 * half * d * 3 * d,
        name="qkv_first",
        vmem=10,
    )
    cot = to_sequences(lambda j: later(pos, pick(cotangent, j, 1), "cotangent", (w1p[0],)), z)
    w2z = over_z(pos, g2, "second_z", (w1p[0],))
    w2p = over_plane(pos, w2z, "second_plane", (w1p[1], q0, cot))

    kv0r = swap_dp(kv0, 1)
    ob, lg, lb = out_bias, ln_gain, ln_bias
    mix0, lse0, n1, inv1, act, dgel, n2, inv2, low1, wo, wu, wd = call(
        first_layer_kernel,
        [
            ((half, d), f32), ((8, half), f32), ((half, d), f32), ((half, HD), f32), ((half, f), bf16),
            ((half, f), bf16), ((half, d), f32), ((half, HD), f32), ((half, d), bf16),
            ((d, d), bf16), ((d, f), bf16), ((f, d), bf16),
        ],
        [pos, q0, kv0, kv0r, qmask, kmask, *w1, cur0, bup, ob, lg, lb],
        [((half, HD), f32)],
        flops=2 * half * (2 * n * d + d * d + 2 * d * f),
        name="first_layer",
        after=(w2p[0],),
        vmem=8,
    )
    w2 = (w2p[0], w2p[1], swap_dp(w2p[0], 1), swap_dp(later(pos, w2p[1], "second_copy", (low1,)), 1))
    q1, kv1, wq1 = call(
        qkv_next_kernel,
        [((half, d), bf16), ((half, 2 * d), bf16), ((d, 3 * d), bf16)],
        [pos, low1, *w2, bqv],
        flops=2 * half * d * 3 * d,
        name="qkv_next",
        vmem=12,
    )
    kv1r = swap_dp(kv1, 1)
    lse1, final, gmix1, gbm1, delta1, keep1, send1, vec1 = call(
        last_layer_kernel,
        [
            ((8, half), f32), ((half, d), bf16), ((half, d), bf16), ((half, d), f32), ((8, half), f32),
            ((4, width * rest, HD), bf16), ((4, width * rest, HD), bf16), ((16, d), f32),
        ],
        [pos, q1, kv1, kv1r, qmask, kmask, *w2, n2, cot, bup, ob, lg, lb],
        [
            ((half, HD), f32), ((half, d), f32), ((d, d), bf16), ((d, f), bf16), ((f, d), bf16),
            ((half, d), f32), ((half, HD), f32), ((half, f), bf16), ((half, f), bf16), ((half, d), f32),
            ((half, HD), f32), ((half, d), bf16), ((half, f), bf16), ((half, d), bf16), ((f, d), bf16), ((d, f), bf16),
            ((d, d), bf16),
        ],
        flops=2 * half * (2 * n * d + d * d + 2 * d * f) * 3,
        name="last_layer",
        vmem=18,
    )
    sent = []
    final_rows = from_sequences(final, z, sent)
    four1 = split(pos, keep1, swap_dp(send1, 1), "add_pair_last")
    def attention_back(q, kv, kvr, delta, gmix, lse, name, after=()):
        dq, dkva, dkvb = call(
            attention_back_kernel,
            [((half, d), bf16), ((half, 2 * d), bf16), ((half, 2 * d), bf16)],
            [pos, gmix, delta, q, kvr, kv, lse, qmask, kmask],
            [((d // HD, HD, half), f32)],
            flops=2 * half * 5 * n * d,
            name=name,
            vmem=10,
            after=after,
        )
        return dq, dkva, swap_dp(dkvb, 1)

    dq1, dkva1, dkvr1 = attention_back(q1, kv1, kv1r, delta1, gmix1, lse1, "attention_back_last")
    gmix0, gbm0, delta0, keep2, send2, vec = call(
        middle_kernel,
        [
            ((half, d), bf16), ((half, d), f32), ((8, half), f32),
            ((4, width * (first + rest), HD), bf16), ((4, width * (first + rest), HD), bf16), ((24, d), f32),
        ],
        [
            pos, dq1, dkva1, dkvr1, wq1, gbm1, n2, inv2, wd, dgel, wu, n1, inv1, wo, act, mix0, vec1, lg, lb,
        ],
        [
            ((half, 3 * d), bf16), ((d, 3 * d), bf16), ((half, d), f32),
            ((half, d), bf16), ((half, f), bf16), ((half, d), bf16),
            ((f, d), bf16), ((d, f), bf16), ((d, d), bf16),
        ],
        flops=2 * half * (6 * d * d + 2 * d * d + 4 * d * f),
        name="middle",
        after=four1,
        vmem=13,
    )
    late1 = swap_dp(four1[1], 2, 4)
    two1 = split(pos, four1[0], late1, "add_plane_last")
    four2 = split(pos, keep2, swap_dp(later(pos, send2, "grads_middle", (late1,)), 1), "add_pair", (two1[0],))
    dq0, dkva0, dkvr0 = attention_back(
        q0, kv0, kv0r, delta0, gmix0, lse0, "attention_back_first", (*four2, *two1)
    )
    two2 = split(pos, four2[0], swap_dp(four2[1], 2, 4), "add_plane")
    shares1 = call(
        join_kernel,
        [((rest, HD), bf16)] * width,
        [pos, two1[0], swap_dp(two1[1], 4, 2)],
        name="join_last",
        vmem=8,
    )
    shared_rows = -(-(24 + fdim) // 128) * 128
    share = shared_rows // 8 * (d // HD)
    keep3, send3, gnorm, sums = call(
        entry_kernel,
        [
            ((4, width * first + share, HD), bf16), ((4, width * first + share, HD), bf16),
            ((half, fdim), f32), ((16, fdim), f32),
        ],
        [pos, dq0, dkva0, dkvr0, low0, wq0, gbm0, normed, enc_w, feat_own, vec, stats],
        [((half, 3 * d), bf16), ((d, 3 * d), bf16), ((shared_rows, d), f32)],
        flops=2 * half * (6 * d * d + 2 * d * HD),
        name="entry",
        after=(*two2, *shares1, *sent),
        vmem=12,
    )
    shares2 = call(
        join_kernel,
        [((first + rest, HD), bf16)] * width,
        [pos, two2[0], swap_dp(two2[1], 4, 2)],
        name="join",
        vmem=10,
    )
    four3 = split(pos, keep3, swap_dp(send3, 1), "add_pair_entry")
    two3 = split(pos, four3[0], swap_dp(four3[1], 2, 4), "add_plane_entry")
    shares3 = call(
        join_last_kernel,
        [((first + share, HD), bf16)] * width,
        [pos, two3[0], swap_dp(two3[1], 4, 2)],
        name="join_entry",
        vmem=6,
    )
    piece = jnp.concatenate([sum_z([sum_far(part) for part in shares1]), sum_z([sum_far(part) for part in shares2])])
    r1 = over_pair(*over_plane(pos, piece, "results_plane"))
    r2 = over_pair(*over_plane(pos, sum_z([sum_far(part) for part in shares3]), "results_plane_entry"))
    (g_feat,) = call(
        features_back_kernel,
        [((half, fdim), f32)],
        [pos, gnorm, feat_own, stats, sums, swap_dp(sums, 1)],
        name="features_back",
        vmem=6,
    )
    grad_features = from_sequences(g_feat, z)
    g_qkv, g_out, g_up, g_down, g_enc_w, g_enc_b, g_bqv, g_ob, g_lg, g_lb, g_bup = call(
        result_kernel,
        [
            ((layers, 3, d, HD), f32), ((layers, HD, d), f32), ((layers, d, f_part), f32), ((layers, f_part, d), f32),
            ((fdim, d), f32), ((1, d), f32), ((layers, 2, HD), f32), ((layers, 2, d), f32), ((layers, 2, d), f32),
            ((layers, 2, d), f32), ((layers, f_part), f32),
        ],
        [pos, *r1, *r2],
        [((shared_rows, d), f32)],
        name="results",
        vmem=10,
    )
    return (
        final_rows, grad_features, g_enc_w, g_enc_b[0], g_qkv, g_bqv, g_out, g_ob, g_lg, g_lb, g_up, g_bup, g_down,
    )


def solution(mesh):
    size, width = mesh.shape["dp"], mesh.shape["tensor"]
    mesh = jax.sharding.Mesh(mesh.devices.reshape(size // 8, 4, 2, width), ("far", "plane", "pair", "tensor"))
    dp = ("far", "plane", "pair")
    rows, ids = P("tensor", dp, None), P(None, dp)
    qkv, bqv = P(None, None, None, "tensor"), P(None, None, "tensor")
    mid, last = P(None, "tensor", None), P(None, None, "tensor")
    in_specs = (rows, ids, ids, P(), P(), qkv, bqv, mid, P(), P(), P(), last, P(None, "tensor"), mid, rows)
    out_specs = (rows, rows, P(), P(), qkv, bqv, mid, P(), P(), P(), last, P(None, "tensor"), mid)
    return jax.shard_map(local, mesh=mesh, in_specs=in_specs, out_specs=out_specs, check_vma=False)
```

```python
import functools
import math

import jax
import jax.numpy as jnp
from jax import lax
from jax.experimental import pallas as pl
from jax.experimental.pallas import tpu as pltpu
from jax.sharding import PartitionSpec as P

HD = 128
NTAB = 5
spread_floor = 0.1
norm_eps = 1e-05
f32 = jnp.float32
bf16 = jnp.bfloat16
LOG2E = 1.4426950408889634
MIB = 1024 * 1024


def mm(a, b):
    return lax.dot_general(a, b, (((1,), (0,)), ((), ())), preferred_element_type=f32)


def mm_nt(a, b):
    return lax.dot_general(a, b, (((1,), (1,)), ((), ())), preferred_element_type=f32)


def mm_tn(a, b):
    return lax.dot_general(a, b, (((0,), (0,)), ((), ())), preferred_element_type=f32)


class Stage:
    def __init__(self, loads, stores):
        self.loads = {id(ref): copy for ref, copy in loads}
        self.stores = {id(ref): copy for ref, copy in stores}
        self.started = []
        for copy in self.loads.values():
            copy.start()

    def need(self, *refs):
        for ref in refs:
            copy = self.loads.pop(id(ref), None)
            if copy is not None:
                copy.wait()

    def done(self, *refs):
        for ref in refs:
            copy = self.stores.pop(id(ref), None)
            if copy is not None:
                copy.start()
                self.started.append(copy)

    def finish(self):
        for copy in self.stores.values():
            copy.start()
        for copy in list(self.loads.values()) + self.started + list(self.stores.values()):
            copy.wait()


def call(body, outs, args, scratch=(), flops=0, name=None, after=(), far=(), vmem=16, staged=False):
    shapes = [jax.ShapeDtypeStruct(shape, dtype) for shape, dtype in outs]
    size = lambda a: a.size * a.dtype.itemsize
    moved = sum(size(a) for a in args) + sum(size(a) for a in shapes)
    count, results, extra = len(args), len(shapes), len(scratch)
    large_in = [at for at in range(1, count) if staged and at not in far and size(args[at]) >= 65536]
    large_out = [at for at in range(results) if staged and size(shapes[at]) >= 65536]
    near = pl.BlockSpec(memory_space=pltpu.VMEM)
    hbm = pl.BlockSpec(memory_space=pl.ANY)

    def run(*refs):
        ins = list(refs[:count])
        out = list(refs[count + len(after) :][:results])
        rest = refs[count + len(after) + results :]
        mine, rest = rest[:extra], rest[extra:]
        held_in, held_out, sems = rest[: len(large_in)], rest[len(large_in) : -1], rest[-1]
        loads, stores = [], []
        for at, ref in zip(large_in, held_in):
            loads.append((ref, pltpu.make_async_copy(ins[at], ref, sems.at[len(loads)])))
            ins[at] = ref
        for at, ref in zip(large_out, held_out):
            stores.append((ref, pltpu.make_async_copy(ref, out[at], sems.at[len(loads) + len(stores)])))
            out[at] = ref
        stage = Stage(loads, stores)
        body(stage, *ins, *out, *mine)
        stage.finish()

    return pl.pallas_call(
        run,
        out_shape=shapes,
        in_specs=[pl.BlockSpec(memory_space=pltpu.SMEM)]
        + [hbm if at in far or at in large_in else near for at in range(1, count)]
        + [hbm] * len(after),
        out_specs=[hbm if at in large_out else near for at in range(results)],
        scratch_shapes=[
            pltpu.SemaphoreType.DMA(shape) if dtype is None else pltpu.VMEM(shape, dtype) for shape, dtype in scratch
        ]
        + [pltpu.VMEM(args[at].shape, args[at].dtype) for at in large_in]
        + [pltpu.VMEM(shapes[at].shape, shapes[at].dtype) for at in large_out]
        + [pltpu.SemaphoreType.DMA((max(1, len(large_in) + len(large_out)),))],
        compiler_params=pltpu.CompilerParams(vmem_limit_bytes=vmem * MIB),
        cost_estimate=pl.CostEstimate(flops=flops, bytes_accessed=moved, transcendentals=0),
        name=name,
    )(*args, *after)


def blocks(kind, d, f_part, q, z):
    if kind == "qkv":
        n = d // 8
        return [(c * n, n, q * n, c * d + z * HD) for c in range(3)]
    if kind == "out":
        n = HD // 8
        return [(c * n, n, z * HD + q * n, c * HD) for c in range(d // HD)]
    if kind == "up":
        n = d // 8
        return [(c * n, n, q * n, z * f_part + c * HD) for c in range(f_part // HD)]
    n = f_part // 8
    return [(c * n, n, z * f_part + q * n, c * HD) for c in range(d // HD)]


def aligned(value, unit):
    return value if isinstance(value, int) else pl.multiple_of(value, unit)


def unpack(pos, buffers, row0, kind, whole, d, f_part):
    base = 0
    for src in buffers:

        def step(e, carry, src=src, base=base):
            q = pos[base + e]
            for k in range(src.shape[1]):
                for at, n, row, col in blocks(kind, d, f_part, q, pos[8 + k]):
                    whole[pl.ds(aligned(row, 16), n), pl.ds(aligned(col, HD), HD)] = src[
                        e, k, row0 + at : row0 + at + n, :
                    ]
            return carry

        lax.fori_loop(0, src.shape[0], step, 0)
        base += src.shape[0]


def pack(pos, whole, row0, kind, halves, d, f_part, width, piece, order=12):
    for c in range(2):
        dst = halves[c]

        def step(e, carry, dst=dst, c=c):
            q = pos[order + c * 4 + e]
            for k in range(width):
                for at, n, row, col in blocks(kind, d, f_part, q, pos[8 + k]):
                    at += k * piece + row0
                    dst[e, at : at + n, :] = whole[
                        pl.ds(aligned(row, 16), n), pl.ds(aligned(col, HD), HD)
                    ]
            return carry

        lax.fori_loop(0, 4, step, 0)


def copy_all(pairs, sems):
    copies = [pltpu.make_async_copy(src, dst, sems.at[at]) for at, (src, dst) in enumerate(pairs)]
    for copy in copies:
        copy.start()
    for copy in copies:
        copy.wait()


def qkv_copies(l, q, wqkv, to):
    n = wqkv.shape[2] // 8
    row = pl.multiple_of(q * n, 16)
    return [(wqkv.at[l, c, pl.ds(row, n), :], to.at[pl.ds(c * n, n), :]) for c in range(3)]


def pack_first_kernel(stage, pos, wqkv, bqv, bup, g0, sems):
    d, f_part = wqkv.shape[2], bup.shape[1]
    rows = [bqv[0], bqv[1]]
    rows += [bup[l : l + 1, c * HD : (c + 1) * HD] for l in range(2) for c in range(f_part // HD)]
    rows = jnp.concatenate(rows, 0)
    high = rows.astype(bf16).astype(f32)
    g0[3 * d // 8 :, :] = jnp.concatenate([high, rows - high], 0).astype(bf16)
    copy_all(qkv_copies(0, pos[0], wqkv, g0), sems)


def rest_copies(l, q, wout, wup, wdown, to, base):
    d, f_part = wup.shape[1], wup.shape[2]
    n, m, r = d // 8, HD // 8, f_part // 8
    pairs = []
    for src, count, cols in ((wout, m, d), (wup, n, f_part), (wdown, r, d)):
        for c in range(cols // HD):
            block = src.at[l, pl.ds(pl.multiple_of(q * count, 16), count), pl.ds(c * HD, HD)]
            pairs.append((block, to.at[pl.ds(base, count), :]))
            base += count
    return pairs


def pack_rest_kernel(stage, pos, wout, wup, wdown, g1, sems):
    copy_all(rest_copies(0, pos[0], wout, wup, wdown, g1, 0), sems)


def pack_second_kernel(stage, pos, wqkv, wout, wup, wdown, g2, sems):
    pairs = qkv_copies(1, pos[0], wqkv, g2)
    copy_all(pairs + rest_copies(1, pos[0], wout, wup, wdown, g2, 3 * wqkv.shape[2] // 8), sems)


def add_kernel(stage, pos, a, b, low, high):
    m = a.shape[0] // 2
    low[...] = (a[:m].astype(f32) + b[:m].astype(f32)).astype(bf16)
    high[...] = (a[m:].astype(f32) + b[m:].astype(f32)).astype(bf16)


def join_kernel(stage, pos, b, c, *shares):
    m = b.shape[1] // len(shares)
    for k, out in enumerate(shares):
        at = slice(k * m, (k + 1) * m)
        out[...] = (b[0, at, :].astype(f32) + c[0, at, :].astype(f32)).astype(bf16)


def join_last_kernel(stage, pos, b, c, *shares):
    width = len(shares)
    m = (b.shape[1] - shares[0].shape[0]) // (width - 1)
    for k, out in enumerate(shares):
        at = slice(k * m, (k + 1) * m)
        out[:m, :] = (b[0, at, :].astype(f32) + c[0, at, :].astype(f32)).astype(bf16)
        at = slice(width * m, b.shape[1])
        out[m:, :] = (b[0, at, :].astype(f32) + c[0, at, :].astype(f32)).astype(bf16)


def gelu_pair(h):
    bell = jnp.exp2(h * h * (-0.5 * LOG2E))
    t = 1.0 / (1.0 + jnp.abs(h) * (0.3275911 * math.sqrt(0.5)))
    poly = 0.5 * 1.061405429
    for c in (-1.453152027, 1.421413741, -0.284496736, 0.254829592):
        poly = poly * t + 0.5 * c
    tail = poly * t * bell
    cdf = jnp.where(h < 0.0, tail, 1.0 - tail)
    return h * cdf, cdf + h * bell * (1.0 / math.sqrt(2.0 * math.pi))


def normalize(u):
    centre = u - jnp.mean(u, -1, keepdims=True)
    inv = lax.rsqrt(jnp.mean(centre * centre, -1, keepdims=True) + norm_eps)
    return centre * inv, inv


def norm_back(grad, normal, inv, gain):
    e = grad * gain
    return (e - jnp.mean(e, -1, keepdims=True) - normal * jnp.mean(e * normal, -1, keepdims=True)) * inv


def rowsum(x):
    return jnp.sum(x, 0, keepdims=True)


def row_codes(block, features):
    return block[:, features : features + 1].astype(jnp.int32)


def query_mask(code):
    lane = lax.broadcasted_iota(jnp.int32, (code.shape[0], HD), 1)
    return jnp.where((lane > NTAB) | (lane == (code >> 1)), 0.0, -1e30).astype(bf16)


def key_mask(code):
    lane = lax.broadcasted_iota(jnp.int32, (code.shape[0], HD), 1)
    return jnp.where((lane == (code >> 1)) | ((lane == NTAB) & ((code & 1) == 0)), 1.0, 0.0).astype(bf16)


def features_kernel(stage, pos, fa, fb, encw, encb, cur, low, normed, stats, qmask, kmask):
    stage.need(fa, fb, encw)
    features = encw.shape[0]
    half = fa.shape[0]
    own, other = fa[:, :features], fb[:, :features]
    code_a, code_b = row_codes(fa, features), row_codes(fb, features)
    qmask[...] = query_mask(code_a)
    kmask[:half, :] = key_mask(code_a)
    kmask[half:, :] = key_mask(code_b)
    mean_rows = jnp.zeros_like(own)
    scale_rows = jnp.zeros_like(own)
    for t in range(NTAB):
        pa = (code_a == 2 * t + 1).astype(f32)
        pb = (code_b == 2 * t + 1).astype(f32)
        count = rowsum(pa) + rowsum(pb)
        mean = (rowsum(pa * own) + rowsum(pb * other)) / count
        da, db = own - mean, other - mean
        excess = (rowsum(pa * da * da) + rowsum(pb * db * db)) / count
        scale = lax.rsqrt(jnp.maximum(excess, spread_floor))
        stats[t : t + 1, :] = mean
        stats[8 + t : 9 + t, :] = scale
        stats[16 + t : 17 + t, :] = excess
        stats[24 + t : 25 + t, :] = jnp.broadcast_to(count, mean.shape)
        here = (code_a >> 1) == t
        mean_rows = jnp.where(here, mean, mean_rows)
        scale_rows = jnp.where(here, scale, scale_rows)
    z = ((own - mean_rows) * scale_rows).astype(bf16)
    normed[...] = z
    out = mm(z, encw[...]) + encb[...].reshape(1, -1)
    cur[...] = out
    low[...] = out.astype(bf16)


def project(stage, x, w, bias, q, kv, layer, d):
    kv[:, :d] = mm(x, w[:, d : 2 * d]).astype(bf16)
    kv[:, d:] = (mm(x, w[:, 2 * d :]) + bias[2 * layer + 1 : 2 * layer + 2, :]).astype(bf16)
    stage.done(kv)
    q[...] = (mm(x, w[:, :d]) + bias[2 * layer : 2 * layer + 1, :]).astype(bf16)


def qkv_first_kernel(stage, pos, low, ga, gb, gc, gd, q, kv, w, bqv, bup):
    d = low.shape[1]
    buffers = (ga, gb, gc, gd)
    stage.need(*buffers)
    unpack(pos, buffers, 0, "qkv", w, d, 0)
    stage.done(w)
    base = 3 * d // 8
    f_part = 2 * HD
    for k in range(ga.shape[1]):
        z = pos[8 + k]
        rows = ga[0, k, base : base + 16, :].astype(f32)
        rows = rows[:8] + rows[8:]
        for j in range(4):
            bqv[j : j + 1, pl.ds(pl.multiple_of(z * HD, HD), HD)] = rows[j : j + 1]
            col = z * f_part + (j % 2) * HD
            bup[j // 2 : j // 2 + 1, pl.ds(pl.multiple_of(col, HD), HD)] = rows[4 + j : 5 + j]
    stage.need(low)
    project(stage, low[...], w, bqv, q, kv, 0, d)


def qkv_next_kernel(stage, pos, low, ga, gb, gc, gd, bqv, q, kv, w):
    d = low.shape[1]
    stage.need(ga, gb, gc, gd)
    unpack(pos, (ga, gb, gc, gd), 0, "qkv", w, d, 0)
    stage.done(w)
    stage.need(low)
    project(stage, low[...], w, bqv, q, kv, 1, d)


def attention_rows(rows, q, kva, kvb, qmask, kmask, mix, lse, d):
    n = kva.shape[0]
    factor = LOG2E / math.sqrt(HD)
    count = rows.size
    lane = lax.broadcasted_iota(jnp.int32, (count, HD), 1)
    totals = jnp.zeros((count, HD), f32)
    for h in range(d // HD):
        cols = slice(h * HD, (h + 1) * HD)
        vals = slice(d + h * HD, d + (h + 1) * HD)
        qh = jnp.concatenate([q[rows, cols], qmask[rows, :]], 1)
        ta = mm_nt(qh, jnp.concatenate([kva[:, cols], kmask[:n, :]], 1))
        tb = mm_nt(qh, jnp.concatenate([kvb[:, cols], kmask[n:, :]], 1))
        top = jnp.maximum(jnp.max(ta, -1, keepdims=True), jnp.max(tb, -1, keepdims=True)) * factor
        ea, eb = jnp.exp2(ta * factor - top), jnp.exp2(tb * factor - top)
        total = jnp.sum(ea, -1, keepdims=True) + jnp.sum(eb, -1, keepdims=True)
        out = mm(ea.astype(bf16), kva[:, vals]) + mm(eb.astype(bf16), kvb[:, vals])
        mix[rows, cols] = out / total
        totals = jnp.where(lane == h, top + jnp.log2(total), totals)
    lse[rows, :] = totals


def layer_rows(rows, cur, mix, wo, wu, wd, bup, ob, lg, lb, layer, n1, inv1, act, dgel, n2, inv2):
    l = layer
    u = cur + mm(mix[rows, :].astype(bf16), wo[...]) + ob[l, 0:1, :]
    normal, inv = normalize(u)
    n1[rows, :] = normal
    inv1[rows, :] = jnp.broadcast_to(inv, (rows.size, HD))
    middle = normal * lg[l, 0:1, :] + lb[l, 0:1, :]
    hidden = mm(middle.astype(bf16), wu[...]) + bup[l : l + 1, :]
    value, slope = gelu_pair(hidden)
    value = value.astype(bf16)
    act[rows, :] = value
    dgel[rows, :] = slope.astype(bf16)
    u = middle + mm(value, wd[...]) + ob[l, 1:2, :]
    normal, inv = normalize(u)
    n2[rows, :] = normal
    inv2[rows, :] = jnp.broadcast_to(inv, (rows.size, HD))
    return normal * lg[l, 1:2, :] + lb[l, 1:2, :]


def attention(stage, q, kva, kvb, qmask, kmask, mix, lse, raw, d):
    stage.need(q, kva, kvb)

    def step(i, carry):
        rows = pl.ds(pl.multiple_of(i * CHUNK, CHUNK), CHUNK)
        attention_rows(rows, q, kva, kvb, qmask, kmask, mix, raw, d)
        return carry

    lax.fori_loop(0, q.shape[0] // CHUNK, step, 0)
    stage.done(mix)
    lse[...] = raw[...].T[:8]


def unpack_rest(stage, pos, buffers, row0, wo, wu, wd, d, f_part):
    m = HD // 8 * (d // HD)
    stage.need(*buffers)
    unpack(pos, buffers, row0, "out", wo, d, f_part)
    unpack(pos, buffers, row0 + m, "up", wu, d, f_part)
    unpack(pos, buffers, row0 + m + d // 8 * (f_part // HD), "down", wd, d, f_part)
    stage.done(wo, wu, wd)


def first_layer_kernel(
    stage, pos, q, kva, kvb, qmask, kmask, ga, gb, gc, gd, cur, bup, ob, lg, lb,
    mix, lse, n1, inv1, act, dgel, n2, inv2, low, wo, wu, wd,
    raw,
):
    d = q.shape[1]
    attention(stage, q, kva, kvb, qmask, kmask, mix, lse, raw, d)
    unpack_rest(stage, pos, (ga, gb, gc, gd), 0, wo, wu, wd, d, wu.shape[1] // ga.shape[1])
    stage.need(cur)

    def step(i, carry):
        rows = pl.ds(pl.multiple_of(i * CHUNK, CHUNK), CHUNK)
        out = layer_rows(
            rows, cur[rows, :], mix, wo, wu, wd, bup, ob, lg, lb, 0, n1, inv1, act, dgel, n2, inv2
        )
        low[rows, :] = out.astype(bf16)
        return carry

    lax.fori_loop(0, q.shape[0] // CHUNK, step, 0)


CHUNK = 512


def ffn_back(
    stage, pos, grad, l, n1, inv1, act, dgel, n2, inv2, mix, wo, wu, wd, lg, lb,
    gmix, gbm, delta, keep, send, vec, vrow, gl, gh, g1, dwd, dwu, dwo, d, f_part, width, piece, order, base,
):
    gain0, gain1 = lg[l, 0:1, :], lg[l, 1:2, :]
    shift0 = lb[l, 0:1, :]
    f = wu.shape[1]

    def step(i, carry):
        rows = pl.ds(pl.multiple_of(i * CHUNK, CHUNK), CHUNK)
        top = grad[rows, :].astype(f32)
        normal = n2[rows, :]
        bo = norm_back(top, normal, inv2[rows, :1], gain1)
        low = bo.astype(bf16)
        gl[rows, :] = low
        back = mm_nt(low, wd[...])
        back = (back * dgel[rows, :].astype(f32)).astype(bf16)
        gh[rows, :] = back
        gm = bo + mm_nt(back, wu[...])
        first = n1[rows, :]
        bm = norm_back(gm, first, inv1[rows, :1], gain0)
        gbm[rows, :] = bm
        attn = bm.astype(bf16)
        g1[rows, :] = attn
        gmix[rows, :] = mm_nt(attn, wo[...]).astype(bf16)
        sums = (
            rowsum(gm * first),
            rowsum(top * normal),
            rowsum(gm),
            rowsum(top),
            rowsum(attn.astype(f32)),
            rowsum(low.astype(f32)),
        )
        hidden = rowsum(back.astype(f32))
        for j in range(6):
            vec[vrow + j : vrow + j + 1, :] += sums[j]
        for j in range(f // d):
            at = vrow + 8 + j
            vec[at : at + 1, :] += hidden[:, j * d : (j + 1) * d]
        return carry

    lax.fori_loop(0, act.shape[0] // CHUNK, step, 0)
    stage.done(gmix, gbm)
    for h in range(d // HD):
        cols = slice(h * HD, (h + 1) * HD)
        prod = gmix[:, cols].astype(f32) * mix[:, cols]
        delta[h : h + 1, :] = jnp.sum(prod.T, 0, keepdims=True)
    m = HD // 8 * (d // HD)
    dwd[...] = mm_tn(act[...], gl[...]).astype(bf16)
    middle = (n1[...] * gain0 + shift0).astype(bf16)
    dwu[...] = mm_tn(middle, gh[...]).astype(bf16)
    dwo[...] = mm_tn(mix[...].astype(bf16), g1[...]).astype(bf16)
    pack(pos, dwd, base + m + d // 8 * (f_part // HD), "down", (keep, send), d, f_part, width, piece, order)
    pack(pos, dwu, base + m, "up", (keep, send), d, f_part, width, piece, order)
    pack(pos, dwo, base, "out", (keep, send), d, f_part, width, piece, order)


def last_layer_kernel(
    stage, pos, q, kva, kvb, qmask, kmask, ga, gb, gc, gd, n2in, cot, bup, ob, lg, lb,
    lse, final, gmix, gbm, delta, keep, send, vec,
    raw, mix, wo, wu, wd, n1, inv1, act, dgel, n2, inv2, gl, gh, g1, dwd, dwu, dwo,
):
    d = q.shape[1]
    width = ga.shape[1]
    f_part = wu.shape[1] // width
    attention(stage, q, kva, kvb, qmask, kmask, mix, lse, raw, d)
    unpack_rest(stage, pos, (ga, gb, gc, gd), 3 * d // 8, wo, wu, wd, d, f_part)
    stage.need(n2in)

    def step(i, carry):
        rows = pl.ds(pl.multiple_of(i * CHUNK, CHUNK), CHUNK)
        cur = n2in[rows, :] * lg[0, 1:2, :] + lb[0, 1:2, :]
        out = layer_rows(
            rows, cur, mix, wo, wu, wd, bup, ob, lg, lb, 1, n1, inv1, act, dgel, n2, inv2
        )
        final[rows, :] = out.astype(bf16)
        return carry

    lax.fori_loop(0, q.shape[0] // CHUNK, step, 0)
    stage.done(final)
    vec[...] = jnp.zeros_like(vec)
    stage.need(cot)
    ffn_back(
        stage, pos, cot, 1, n1, inv1, act, dgel, n2, inv2, mix, wo, wu, wd, lg, lb,
        gmix, gbm, delta, keep, send, vec, 0, gl, gh, g1, dwd, dwu, dwo, d, f_part, width, keep.shape[1] // width, 0, 0,
    )


def attention_back_kernel(stage, pos, gmix, delta, q, kvb, kva, lse, qmask, kmask, dq, dkva, dkvb, acc):
    d = q.shape[1]
    n = kva.shape[0]
    scaling = 1.0 / math.sqrt(HD)
    factor = LOG2E * scaling
    block = 512
    stage.need(gmix)
    acc[...] = jnp.zeros_like(acc)
    stage.need(q)
    for src, dst, off in ((kvb, dkvb, n), (kva, dkva, 0)):
        stage.need(src)

        def step(i, carry, src=src, dst=dst, off=off):
            rows = pl.ds(pl.multiple_of(i * block, block), block)
            brow = pl.ds(pl.multiple_of(off + i * block, block), block)
            for h in range(d // HD):
                cols = slice(h * HD, (h + 1) * HD)
                vals = slice(d + h * HD, d + (h + 1) * HD)
                qh, gh = q[:, cols], gmix[:, cols]
                kh, vh = src[rows, cols], src[rows, vals]
                scores = mm_nt(
                    jnp.concatenate([kh, kmask[brow, :]], 1), jnp.concatenate([qh, qmask[...]], 1)
                )
                probs = jnp.exp2(scores * factor - lse[h : h + 1, :])
                ds = (probs * (mm_nt(vh, gh) - delta[h : h + 1, :])).astype(bf16)
                dst[rows, vals] = mm(probs.astype(bf16), gh).astype(dst.dtype)
                dst[rows, cols] = (mm(ds, qh) * scaling).astype(dst.dtype)
                acc[h, :, :] += mm_tn(kh, ds)
            return carry

        lax.fori_loop(0, n // block, step, 0)
        stage.done(dst)
    for h in range(d // HD):
        dq[:, h * HD : (h + 1) * HD] = (acc[h].T * scaling).astype(bf16)


def projection_back(
    stage, pos, dq, dkva, dkvr, low, w, gbm, proj, dw, keep, send, vec, vrow, d, width, piece, order
):
    stage.need(dq, dkva, dkvr)
    proj[:, :d] = dq[...]
    proj[:, d:] = (dkva[...].astype(f32) + dkvr[...].astype(f32)).astype(bf16)
    vec[vrow : vrow + 1, :] = rowsum(dq[...].astype(f32))
    vec[vrow + 1 : vrow + 2, :] = rowsum(proj[:, 2 * d :].astype(f32))
    dw[...] = mm_tn(low(), proj[...]).astype(bf16)
    stage.need(w, gbm)
    grad = gbm[...] + mm_nt(proj[...], w[...])
    pack(pos, dw, 0, "qkv", (keep, send), d, 0, width, piece, order)
    return grad


def middle_kernel(
    stage, pos, dq, dkva, dkvr, w, gbm1, n2, inv2, wd, dgel, wu, n1, inv1, wo, act, mix, vec1, lg, lb,
    gmix, gbm, delta, keep, send, vec,
    proj, dw, grad, gl, gh, g1, dwd, dwu, dwo,
):
    d = grad.shape[1]
    width = d // HD
    first = 3 * d // 8
    piece = keep.shape[1] // width
    vec[...] = jnp.zeros_like(vec)
    for j in range(10):
        vec[10 + j : 11 + j, :] = vec1[j : j + 1, :]

    def low():
        return (n2[...] * lg[0, 1:2, :] + lb[0, 1:2, :]).astype(bf16)

    grad[...] = projection_back(
        stage, pos, dq, dkva, dkvr, low, w, gbm1, proj, dw, keep, send, vec, 16, d, width, piece, 0
    )
    ffn_back(
        stage, pos, grad, 0, n1, inv1, act, dgel, n2, inv2, mix, wo, wu, wd, lg, lb,
        gmix, gbm, delta, keep, send, vec, 0, gl, gh, g1, dwd, dwu, dwo, d, wu.shape[1] // width,
        width, piece, 0, first,
    )


def entry_kernel(
    stage, pos, dq, dkva, dkvr, low0, w0, gbm0, normed, encw, fa, vec, stats,
    keep, send, gnorm, sums,
    proj, dw, shared,
):
    d = dq.shape[1]
    features = encw.shape[0]
    width = d // HD
    first = 3 * d // 8
    shared[...] = jnp.zeros_like(shared)
    shared[:24, :] = vec[...]
    def low():
        stage.need(low0)
        return low0[...]

    grad = projection_back(
        stage, pos, dq, dkva, dkvr, low, w0, gbm0, proj, dw, keep, send, shared, 6, d, width, first, 0
    )
    stage.need(normed, encw, fa)
    low = grad.astype(bf16)
    shared[20:21, :] = rowsum(low.astype(f32))
    shared[24 : 24 + features, :] = mm_tn(normed[...], low)
    back = mm_nt(low, encw[...])
    gnorm[...] = back
    code = row_codes(fa, features) >> 1
    centred = fa[:, :features]
    sums[...] = jnp.zeros_like(sums)
    for t in range(NTAB):
        here = code == t
        part = jnp.where(here, back, 0.0)
        sums[t : t + 1, :] = rowsum(part)
        sums[8 + t : 9 + t, :] = rowsum(part * (centred - stats[t : t + 1, :]))
    share = shared.shape[0] // 8
    for c, dst in ((0, keep), (1, send)):

        def step(e, carry, dst=dst, c=c):
            row = pl.multiple_of(pos[c * 4 + e] * share, 8)
            for j in range(d // HD):
                piece = shared[pl.ds(row, share), j * HD : (j + 1) * HD].astype(bf16)
                at = width * first + j * share
                dst[e, at : at + share, :] = piece
            return carry

        lax.fori_loop(0, 4, step, 0)


def features_back_kernel(stage, pos, gnorm, fa, stats, mine, theirs, out):
    total = mine[...] + theirs[...]
    stage.need(gnorm, fa)
    back = gnorm[...]
    code = row_codes(fa, back.shape[1])
    x = fa[:, : back.shape[1]]
    scale_rows = jnp.zeros_like(x)
    flat = jnp.zeros_like(x)
    slope = jnp.zeros_like(x)
    for t in range(NTAB):
        mean, scale = stats[t : t + 1, :], stats[8 + t : 9 + t, :]
        excess, count = stats[16 + t : 17 + t, :], stats[24 + t : 25 + t, :]
        plain, centred = total[t : t + 1, :], total[8 + t : 9 + t, :]
        g_excess = jnp.where(excess > spread_floor, -0.5 * scale * scale * scale * centred, 0.0)
        g_mean = -scale * plain - 2.0 * mean * g_excess
        scale_rows = jnp.where((code >> 1) == t, scale, scale_rows)
        chosen = code == 2 * t + 1
        flat = jnp.where(chosen, g_mean / count, flat)
        slope = jnp.where(chosen, 2.0 * g_excess / count, slope)
    out[...] = back * scale_rows + flat + x * slope


def result_kernel(
    stage, pos, ra, rb, rc, rd, ea, eb, ec, ed, gqkv, gout, gup, gdown, genc_w, genc_b, gbqv, gob, glg, glb, gbup, rows
):
    d, f_part = gqkv.shape[2], gup.shape[2]
    n, m, r = d // 8, HD // 8, f_part // 8
    first = 3 * n
    share = rows.shape[0] // 8
    after = m * (d // HD) + n * (f_part // HD) + r * (d // HD)

    def rest(l, src, e, q, base):
        for c in range(d // HD):
            gout[l, pl.ds(pl.multiple_of(q * m, 16), m), c * HD : (c + 1) * HD] = src[
                e, base + c * m : base + (c + 1) * m, :
            ].astype(f32)
        base += d // HD * m
        for c in range(f_part // HD):
            gup[l, pl.ds(pl.multiple_of(q * n, 16), n), c * HD : (c + 1) * HD] = src[
                e, base + c * n : base + (c + 1) * n, :
            ].astype(f32)
        base += f_part // HD * n
        for c in range(d // HD):
            gdown[l, pl.ds(pl.multiple_of(q * r, 16), r), c * HD : (c + 1) * HD] = src[
                e, base + c * r : base + (c + 1) * r, :
            ].astype(f32)

    for part, (src, end) in enumerate(((ra, ea), (rb, eb), (rc, ec), (rd, ed))):
        stage.need(src, end)

        def step(e, carry, part=part, src=src, end=end):
            q = pos[part * 2 + e]
            for l, ref, base in ((1, src, after), (0, end, 0)):
                for c in range(3):
                    gqkv[l, c, pl.ds(pl.multiple_of(q * n, 16), n), :] = ref[
                        e, base + c * n : base + (c + 1) * n, :
                    ].astype(f32)
            rest(1, src, e, q, 0)
            rest(0, src, e, q, after + first)
            for j in range(d // HD):
                rows[pl.ds(pl.multiple_of(q * share, 8), share), j * HD : (j + 1) * HD] = end[
                    e, first + j * share : first + (j + 1) * share, :
                ].astype(f32)
            return carry

        lax.fori_loop(0, src.shape[0], step, 0)
    z = pos[8]
    d = genc_w.shape[1]
    layers = gob.shape[0]
    genc_w[...] = rows[24 : 24 + genc_w.shape[0], :]
    genc_b[...] = rows[10 * layers : 10 * layers + 1, :]
    for l in range(layers):
        at = 10 * l
        for j in range(2):
            glg[l, j : j + 1, :] = rows[at + j : at + j + 1, :]
            glb[l, j : j + 1, :] = rows[at + 2 + j : at + 3 + j, :]
            gob[l, j : j + 1, :] = rows[at + 4 + j : at + 5 + j, :]
            gbqv[l, j : j + 1, :] = rows[at + 6 + j : at + 7 + j, pl.ds(pl.multiple_of(z * HD, HD), HD)]
        row = at + 8 + (z * f_part) // d
        col = pl.multiple_of((z * f_part) % d, HD)
        gbup[l : l + 1, :] = rows[pl.ds(row, 1), pl.ds(col, f_part)]


def swap_dp(values, even, odd=None):
    odd = even if odd is None else odd
    return lax.ppermute(values, ("plane", "pair"), [(i, i ^ (odd if i % 2 else even)) for i in range(8)])


def swap_z(values, mask):
    size = lax.axis_size("tensor")
    return lax.ppermute(values, "tensor", [(i, i ^ mask) for i in range(size)])


def relay_pairs(step):
    width = lax.axis_size("tensor")
    return [
        (p * width + z, z // 2 * width + 2 * p + (step ^ (z & 1))) for p in range(2) for z in range(width)
    ]


def pick(values, index, axis=0):
    return lax.dynamic_index_in_dim(values, index, axis, keepdims=False)


def to_sequences(one_block, z):
    got = [lax.ppermute(one_block(step ^ (z & 1)), ("pair", "tensor"), relay_pairs(step)) for step in range(2)]
    return jnp.concatenate(got)


def from_sequences(values, z, sent=None):
    part = values.shape[0] // 2
    got = [
        lax.ppermute(
            values[step * part : (step + 1) * part],
            ("pair", "tensor"),
            [(b, a) for a, b in relay_pairs(step)],
        )
        for step in range(2)
    ]
    if sent is not None:
        sent.extend(got)
    odd = (z & 1) == 1
    return jnp.stack([jnp.where(odd, got[1], got[0]), jnp.where(odd, got[0], got[1])], 1)


def stack_kernel(stage, pos, *refs):
    out = refs[-1]
    for at, ref in enumerate(refs[:-1]):
        out[at] = ref[...]


def stack(pos, pieces, name, after=()):
    shape = (len(pieces),) + pieces[0].shape
    return call(stack_kernel, [(shape, bf16)], [pos] + pieces, name=name, after=after, vmem=6)[0]


def copy_kernel(stage, pos, src, out):
    out[...] = src[...]


def later(pos, values, name, after):
    return call(copy_kernel, [(values.shape, values.dtype)], [pos, values], name=name, after=after, vmem=4)[0]


def over_z(pos, piece, name, after=()):
    pieces = [piece] + [swap_z(piece, k) for k in range(1, lax.axis_size("tensor"))]
    return stack(pos, pieces, name, after)


def over_plane(pos, piece, name, after=()):
    two = stack(pos, [piece, swap_dp(piece, 4, 2)], name, after)
    return two, swap_dp(two, 2, 4)


def over_pair(two, more):
    return two, more, swap_dp(two, 1), swap_dp(more, 1)


def add(a, b):
    return (a.astype(f32) + b.astype(f32)).astype(bf16)


def sum_far(values):
    return lax.psum(values.astype(f32), "far").astype(bf16) if lax.axis_size("far") > 1 else values


def split(pos, a, b, name, after=()):
    outs = [((a.shape[0] // 2,) + a.shape[1:], bf16)] * 2
    return call(add_kernel, outs, [pos, a, b], name=name, vmem=12, after=after)


def sum_z(shares):
    total = shares[0].astype(f32)
    for k in range(1, len(shares)):
        total = total + swap_z(shares[k], k).astype(f32)
    return total.astype(bf16)


def local(
    features,
    table_ids,
    train_flags,
    enc_w,
    enc_b,
    w_qkv,
    b_qv,
    w_out,
    out_bias,
    ln_gain,
    ln_bias,
    w_up,
    b_up,
    w_down,
    cotangent,
):
    part, _, fdim = features.shape
    width = lax.axis_size("tensor")
    layers, d, f_part = w_qkv.shape[0], w_qkv.shape[2], w_up.shape[2]
    f = f_part * width
    half = 2 * part
    n = 2 * half
    z, p, o = lax.axis_index("tensor"), lax.axis_index("pair"), lax.axis_index("plane")
    ox, oy = o & 1, o >> 1
    relative, absolute = [], []
    for c in range(2):
        for r1 in range(2):
            for r2 in range(2):
                pd = p ^ c
                rx, ry = jnp.where(pd == 0, r1, r2), jnp.where(pd == 0, r2, r1)
                relative.append(pd * 4 + (oy ^ ry) * 2 + (ox ^ rx))
                absolute.append(pd * 4 + r1 * 2 + r2)
    pos = jnp.stack(relative + [z ^ k for k in range(width)] + absolute).astype(jnp.int32)
    rest = HD // 8 * (d // HD) + d // 8 * (f_part // HD) + f_part // 8 * (d // HD)
    first = 3 * d // 8

    codes = lax.dynamic_slice_in_dim(table_ids, z * part, part) * 2
    codes = (codes + lax.dynamic_slice_in_dim(train_flags, z * part, part)).astype(f32)

    def feature_block(j):
        space = jnp.zeros((part, HD - fdim - 1), f32)
        return jnp.concatenate([pick(features, j, 1), pick(codes, j, 1)[:, None], space], 1)

    feat_own = to_sequences(feature_block, z)
    feat_other = swap_dp(feat_own, 1)
    (g0,) = call(
        pack_first_kernel,
        [((first + 16, HD), bf16)],
        [pos, w_qkv, b_qv, b_up],
        [((3,), None)],
        name="pack_first",
        vmem=4,
        far=(1,),
    )
    w0z = over_z(pos, g0, "first_z", (feat_own,))
    w0p = over_plane(pos, w0z, "first_plane", (feat_other,))
    w0 = over_pair(*w0p)
    (g1,) = call(
        pack_rest_kernel,
        [((rest, HD), bf16)],
        [pos, w_out, w_up, w_down],
        [((16,), None)],
        name="pack_rest",
        vmem=4,
        far=(1, 2, 3),
        after=(w0z,),
    )
    w1z = over_z(pos, g1, "rest_z")
    cur0, low0, normed, stats, qmask, kmask = call(
        features_kernel,
        [
            ((half, d), f32), ((half, d), bf16), ((half, fdim), bf16), ((32, fdim), f32),
            ((half, HD), bf16), ((n, HD), bf16),
        ],
        [pos, feat_own, feat_other, enc_w, enc_b[None]],
        flops=2 * half * d * HD,
        name="features",
        vmem=8,
    )
    (g2,) = call(
        pack_second_kernel,
        [((first + rest, HD), bf16)],
        [pos, w_qkv, w_out, w_up, w_down],
        [((16,), None)],
        name="pack_second",
        vmem=4,
        far=(1, 2, 3, 4),
        after=(w1z,),
    )
    w1p = over_plane(pos, w1z, "rest_plane", (low0, g2, w0p[1]))
    w1 = over_pair(*w1p)
    q0, kv0, wq0, bqv, bup = call(
        qkv_first_kernel,
        [((half, d), bf16), ((half, 2 * d), bf16), ((d, 3 * d), bf16), ((8, d), f32), ((8, f), f32)],
        [pos, low0, *w0],
        flops=2 * half * d * 3 * d,
        name="qkv_first",
        vmem=10,
    )
    cot = to_sequences(lambda j: later(pos, pick(cotangent, j, 1), "cotangent", (w1p[0],)), z)
    w2z = over_z(pos, g2, "second_z", (w1p[0],))
    w2p = over_plane(pos, w2z, "second_plane", (w1p[1], q0, cot))

    kv0r = swap_dp(kv0, 1)
    ob, lg, lb = out_bias, ln_gain, ln_bias
    mix0, lse0, n1, inv1, act, dgel, n2, inv2, low1, wo, wu, wd = call(
        first_layer_kernel,
        [
            ((half, d), f32), ((8, half), f32), ((half, d), f32), ((half, HD), f32), ((half, f), bf16),
            ((half, f), bf16), ((half, d), f32), ((half, HD), f32), ((half, d), bf16),
            ((d, d), bf16), ((d, f), bf16), ((f, d), bf16),
        ],
        [pos, q0, kv0, kv0r, qmask, kmask, *w1, cur0, bup, ob, lg, lb],
        [((half, HD), f32)],
        flops=2 * half * (2 * n * d + d * d + 2 * d * f),
        name="first_layer",
        after=(w2p[0],),
        vmem=8,
    )
    w2 = (w2p[0], w2p[1], swap_dp(w2p[0], 1), swap_dp(later(pos, w2p[1], "second_copy", (low1,)), 1))
    q1, kv1, wq1 = call(
        qkv_next_kernel,
        [((half, d), bf16), ((half, 2 * d), bf16), ((d, 3 * d), bf16)],
        [pos, low1, *w2, bqv],
        flops=2 * half * d * 3 * d,
        name="qkv_next",
        vmem=12,
    )
    kv1r = swap_dp(kv1, 1)
    lse1, final, gmix1, gbm1, delta1, keep1, send1, vec1 = call(
        last_layer_kernel,
        [
            ((8, half), f32), ((half, d), bf16), ((half, d), bf16), ((half, d), f32), ((8, half), f32),
            ((4, width * rest, HD), bf16), ((4, width * rest, HD), bf16), ((16, d), f32),
        ],
        [pos, q1, kv1, kv1r, qmask, kmask, *w2, n2, cot, bup, ob, lg, lb],
        [
            ((half, HD), f32), ((half, d), f32), ((d, d), bf16), ((d, f), bf16), ((f, d), bf16),
            ((half, d), f32), ((half, HD), f32), ((half, f), bf16), ((half, f), bf16), ((half, d), f32),
            ((half, HD), f32), ((half, d), bf16), ((half, f), bf16), ((half, d), bf16), ((f, d), bf16), ((d, f), bf16),
            ((d, d), bf16),
        ],
        flops=2 * half * (2 * n * d + d * d + 2 * d * f) * 3,
        name="last_layer",
        vmem=18,
    )
    sent = []
    final_rows = from_sequences(final, z, sent)
    four1 = split(pos, keep1, swap_dp(send1, 1), "add_pair_last")
    def attention_back(q, kv, kvr, delta, gmix, lse, name, after=(), beside=()):
        dq, dkva, dkvb = call(
            attention_back_kernel,
            [((half, d), bf16), ((half, 2 * d), bf16), ((half, 2 * d), bf16)],
            [pos, gmix, delta, q, kvr, kv, lse, qmask, kmask],
            [((d // HD, HD, half), f32)],
            flops=2 * half * 5 * n * d,
            name=name,
            vmem=10,
            after=after,
        )
        return dq, dkva, swap_dp(later(pos, dkvb, "keys", beside) if beside else dkvb, 1)

    dq1, dkva1, dkvr1 = attention_back(q1, kv1, kv1r, delta1, gmix1, lse1, "attention_back_last")
    gmix0, gbm0, delta0, keep2, send2, vec = call(
        middle_kernel,
        [
            ((half, d), bf16), ((half, d), f32), ((8, half), f32),
            ((4, width * (first + rest), HD), bf16), ((4, width * (first + rest), HD), bf16), ((24, d), f32),
        ],
        [
            pos, dq1, dkva1, dkvr1, wq1, gbm1, n2, inv2, wd, dgel, wu, n1, inv1, wo, act, mix0, vec1, lg, lb,
        ],
        [
            ((half, 3 * d), bf16), ((d, 3 * d), bf16), ((half, d), f32),
            ((half, d), bf16), ((half, f), bf16), ((half, d), bf16),
            ((f, d), bf16), ((d, f), bf16), ((d, d), bf16),
        ],
        flops=2 * half * (6 * d * d + 2 * d * d + 4 * d * f),
        name="middle",
        after=four1,
        vmem=13,
    )
    late1 = swap_dp(four1[1], 2, 4)
    two1 = split(pos, four1[0], late1, "add_plane_last")
    four2 = split(pos, keep2, swap_dp(later(pos, send2, "grads_middle", (late1,)), 1), "add_pair", (two1[0],))
    late1b = swap_dp(two1[1], 4, 2)
    dq0, dkva0, dkvr0 = attention_back(
        q0, kv0, kv0r, delta0, gmix0, lse0, "attention_back_first", (*four2, *two1), (late1b,)
    )
    two2 = split(pos, four2[0], swap_dp(four2[1], 2, 4), "add_plane")
    shares1 = call(
        join_kernel,
        [((rest, HD), bf16)] * width,
        [pos, two1[0], late1b],
        name="join_last",
        vmem=8,
    )
    shared_rows = -(-(24 + fdim) // 128) * 128
    share = shared_rows // 8 * (d // HD)
    keep3, send3, gnorm, sums = call(
        entry_kernel,
        [
            ((4, width * first + share, HD), bf16), ((4, width * first + share, HD), bf16),
            ((half, fdim), f32), ((16, fdim), f32),
        ],
        [pos, dq0, dkva0, dkvr0, low0, wq0, gbm0, normed, enc_w, feat_own, vec, stats],
        [((half, 3 * d), bf16), ((d, 3 * d), bf16), ((shared_rows, d), f32)],
        flops=2 * half * (6 * d * d + 2 * d * HD),
        name="entry",
        after=(*two2, *shares1),
        vmem=12,
    )
    shares2 = call(
        join_kernel,
        [((first + rest, HD), bf16)] * width,
        [pos, two2[0], swap_dp(two2[1], 4, 2)],
        name="join",
        vmem=10,
    )
    four3 = split(pos, keep3, swap_dp(send3, 1), "add_pair_entry")
    two3 = split(pos, four3[0], swap_dp(four3[1], 2, 4), "add_plane_entry")
    shares3 = call(
        join_last_kernel,
        [((first + share, HD), bf16)] * width,
        [pos, two3[0], swap_dp(two3[1], 4, 2)],
        name="join_entry",
        vmem=6,
    )
    piece = jnp.concatenate([sum_z([sum_far(part) for part in shares1]), sum_z([sum_far(part) for part in shares2])])
    r1 = over_pair(*over_plane(pos, piece, "results_plane"))
    r2 = over_pair(*over_plane(pos, sum_z([sum_far(part) for part in shares3]), "results_plane_entry"))
    (g_feat,) = call(
        features_back_kernel,
        [((half, fdim), f32)],
        [pos, gnorm, feat_own, stats, sums, swap_dp(sums, 1)],
        name="features_back",
        vmem=6,
    )
    grad_features = from_sequences(g_feat, z)
    g_qkv, g_out, g_up, g_down, g_enc_w, g_enc_b, g_bqv, g_ob, g_lg, g_lb, g_bup = call(
        result_kernel,
        [
            ((layers, 3, d, HD), f32), ((layers, HD, d), f32), ((layers, d, f_part), f32), ((layers, f_part, d), f32),
            ((fdim, d), f32), ((1, d), f32), ((layers, 2, HD), f32), ((layers, 2, d), f32), ((layers, 2, d), f32),
            ((layers, 2, d), f32), ((layers, f_part), f32),
        ],
        [pos, *r1, *r2],
        [((shared_rows, d), f32)],
        name="results",
        vmem=10,
    )
    return (
        final_rows, grad_features, g_enc_w, g_enc_b[0], g_qkv, g_bqv, g_out, g_ob, g_lg, g_lb, g_up, g_bup, g_down,
    )


def solution(mesh):
    size, width = mesh.shape["dp"], mesh.shape["tensor"]
    mesh = jax.sharding.Mesh(mesh.devices.reshape(size // 8, 4, 2, width), ("far", "plane", "pair", "tensor"))
    dp = ("far", "plane", "pair")
    rows, ids = P("tensor", dp, None), P(None, dp)
    qkv, bqv = P(None, None, None, "tensor"), P(None, None, "tensor")
    mid, last = P(None, "tensor", None), P(None, None, "tensor")
    in_specs = (rows, ids, ids, P(), P(), qkv, bqv, mid, P(), P(), P(), last, P(None, "tensor"), mid, rows)
    out_specs = (rows, rows, P(), P(), qkv, bqv, mid, P(), P(), P(), last, P(None, "tensor"), mid)
    return jax.shard_map(local, mesh=mesh, in_specs=in_specs, out_specs=out_specs, check_vma=False)
```

```python
import functools
import math

import jax
import jax.numpy as jnp
from jax import lax
from jax.experimental import pallas as pl
from jax.experimental.pallas import tpu as pltpu
from jax.sharding import PartitionSpec as P

HD = 128
NTAB = 5
spread_floor = 0.1
norm_eps = 1e-05
f32 = jnp.float32
bf16 = jnp.bfloat16
LOG2E = 1.4426950408889634
MIB = 1024 * 1024


def mm(a, b):
    return lax.dot_general(a, b, (((1,), (0,)), ((), ())), preferred_element_type=f32)


def mm_nt(a, b):
    return lax.dot_general(a, b, (((1,), (1,)), ((), ())), preferred_element_type=f32)


def mm_tn(a, b):
    return lax.dot_general(a, b, (((0,), (0,)), ((), ())), preferred_element_type=f32)


class Stage:
    def __init__(self, loads, stores):
        self.loads = {id(ref): copy for ref, copy in loads}
        self.stores = {id(ref): copy for ref, copy in stores}
        self.started = []
        for copy in self.loads.values():
            copy.start()

    def need(self, *refs):
        for ref in refs:
            copy = self.loads.pop(id(ref), None)
            if copy is not None:
                copy.wait()

    def done(self, *refs):
        for ref in refs:
            copy = self.stores.pop(id(ref), None)
            if copy is not None:
                copy.start()
                self.started.append(copy)

    def finish(self):
        for copy in self.stores.values():
            copy.start()
        for copy in list(self.loads.values()) + self.started + list(self.stores.values()):
            copy.wait()


def call(body, outs, args, scratch=(), flops=0, name=None, after=(), far=(), vmem=16, staged=False):
    shapes = [jax.ShapeDtypeStruct(shape, dtype) for shape, dtype in outs]
    size = lambda a: a.size * a.dtype.itemsize
    moved = sum(size(a) for a in args) + sum(size(a) for a in shapes)
    count, results, extra = len(args), len(shapes), len(scratch)
    large_in = [at for at in range(1, count) if staged and at not in far and size(args[at]) >= 65536]
    large_out = [at for at in range(results) if staged and size(shapes[at]) >= 65536]
    near = pl.BlockSpec(memory_space=pltpu.VMEM)
    hbm = pl.BlockSpec(memory_space=pl.ANY)

    def run(*refs):
        ins = list(refs[:count])
        out = list(refs[count + len(after) :][:results])
        rest = refs[count + len(after) + results :]
        mine, rest = rest[:extra], rest[extra:]
        held_in, held_out, sems = rest[: len(large_in)], rest[len(large_in) : -1], rest[-1]
        loads, stores = [], []
        for at, ref in zip(large_in, held_in):
            loads.append((ref, pltpu.make_async_copy(ins[at], ref, sems.at[len(loads)])))
            ins[at] = ref
        for at, ref in zip(large_out, held_out):
            stores.append((ref, pltpu.make_async_copy(ref, out[at], sems.at[len(loads) + len(stores)])))
            out[at] = ref
        stage = Stage(loads, stores)
        body(stage, *ins, *out, *mine)
        stage.finish()

    return pl.pallas_call(
        run,
        out_shape=shapes,
        in_specs=[pl.BlockSpec(memory_space=pltpu.SMEM)]
        + [hbm if at in far or at in large_in else near for at in range(1, count)]
        + [hbm] * len(after),
        out_specs=[hbm if at in large_out else near for at in range(results)],
        scratch_shapes=[
            pltpu.SemaphoreType.DMA(shape) if dtype is None else pltpu.VMEM(shape, dtype) for shape, dtype in scratch
        ]
        + [pltpu.VMEM(args[at].shape, args[at].dtype) for at in large_in]
        + [pltpu.VMEM(shapes[at].shape, shapes[at].dtype) for at in large_out]
        + [pltpu.SemaphoreType.DMA((max(1, len(large_in) + len(large_out)),))],
        compiler_params=pltpu.CompilerParams(vmem_limit_bytes=vmem * MIB),
        cost_estimate=pl.CostEstimate(flops=flops, bytes_accessed=moved, transcendentals=0),
        name=name,
    )(*args, *after)


def blocks(kind, d, f_part, q, z):
    if kind == "qkv":
        n = d // 8
        return [(c * n, n, q * n, c * d + z * HD) for c in range(3)]
    if kind == "out":
        n = HD // 8
        return [(c * n, n, z * HD + q * n, c * HD) for c in range(d // HD)]
    if kind == "up":
        n = d // 8
        return [(c * n, n, q * n, z * f_part + c * HD) for c in range(f_part // HD)]
    n = f_part // 8
    return [(c * n, n, z * f_part + q * n, c * HD) for c in range(d // HD)]


def aligned(value, unit):
    return value if isinstance(value, int) else pl.multiple_of(value, unit)


def unpack(pos, buffers, row0, kind, whole, d, f_part):
    base = 0
    for src in buffers:

        def step(e, carry, src=src, base=base):
            q = pos[base + e]
            for k in range(src.shape[1]):
                for at, n, row, col in blocks(kind, d, f_part, q, pos[8 + k]):
                    whole[pl.ds(aligned(row, 16), n), pl.ds(aligned(col, HD), HD)] = src[
                        e, k, row0 + at : row0 + at + n, :
                    ]
            return carry

        lax.fori_loop(0, src.shape[0], step, 0)
        base += src.shape[0]


def pack(pos, whole, row0, kind, halves, d, f_part, width, piece, order=12):
    for c in range(2):
        dst = halves[c]

        def step(e, carry, dst=dst, c=c):
            q = pos[order + c * 4 + e]
            for k in range(width):
                for at, n, row, col in blocks(kind, d, f_part, q, pos[8 + k]):
                    at += k * piece + row0
                    dst[e, at : at + n, :] = whole[
                        pl.ds(aligned(row, 16), n), pl.ds(aligned(col, HD), HD)
                    ]
            return carry

        lax.fori_loop(0, 4, step, 0)


def copy_all(pairs, sems):
    copies = [pltpu.make_async_copy(src, dst, sems.at[at]) for at, (src, dst) in enumerate(pairs)]
    for copy in copies:
        copy.start()
    for copy in copies:
        copy.wait()


def qkv_copies(l, q, wqkv, to):
    n = wqkv.shape[2] // 8
    row = pl.multiple_of(q * n, 16)
    return [(wqkv.at[l, c, pl.ds(row, n), :], to.at[pl.ds(c * n, n), :]) for c in range(3)]


def pack_first_kernel(stage, pos, wqkv, bqv, bup, g0, sems):
    d, f_part = wqkv.shape[2], bup.shape[1]
    rows = [bqv[0], bqv[1]]
    rows += [bup[l : l + 1, c * HD : (c + 1) * HD] for l in range(2) for c in range(f_part // HD)]
    rows = jnp.concatenate(rows, 0)
    high = rows.astype(bf16).astype(f32)
    g0[3 * d // 8 :, :] = jnp.concatenate([high, rows - high], 0).astype(bf16)
    copy_all(qkv_copies(0, pos[0], wqkv, g0), sems)


def rest_copies(l, q, wout, wup, wdown, to, base):
    d, f_part = wup.shape[1], wup.shape[2]
    n, m, r = d // 8, HD // 8, f_part // 8
    pairs = []
    for src, count, cols in ((wout, m, d), (wup, n, f_part), (wdown, r, d)):
        for c in range(cols // HD):
            block = src.at[l, pl.ds(pl.multiple_of(q * count, 16), count), pl.ds(c * HD, HD)]
            pairs.append((block, to.at[pl.ds(base, count), :]))
            base += count
    return pairs


def pack_rest_kernel(stage, pos, wout, wup, wdown, g1, sems):
    copy_all(rest_copies(0, pos[0], wout, wup, wdown, g1, 0), sems)


def pack_second_kernel(stage, pos, wqkv, wout, wup, wdown, g2, sems):
    pairs = qkv_copies(1, pos[0], wqkv, g2)
    copy_all(pairs + rest_copies(1, pos[0], wout, wup, wdown, g2, 3 * wqkv.shape[2] // 8), sems)


def add_kernel(stage, pos, a, b, low, high):
    m = a.shape[0] // 2
    low[...] = (a[:m].astype(f32) + b[:m].astype(f32)).astype(bf16)
    high[...] = (a[m:].astype(f32) + b[m:].astype(f32)).astype(bf16)


def join_kernel(stage, pos, b, c, *shares):
    m = b.shape[1] // len(shares)
    for k, out in enumerate(shares):
        at = slice(k * m, (k + 1) * m)
        out[...] = (b[0, at, :].astype(f32) + c[0, at, :].astype(f32)).astype(bf16)


def join_last_kernel(stage, pos, b, c, *shares):
    width = len(shares)
    m = (b.shape[1] - shares[0].shape[0]) // (width - 1)
    for k, out in enumerate(shares):
        at = slice(k * m, (k + 1) * m)
        out[:m, :] = (b[0, at, :].astype(f32) + c[0, at, :].astype(f32)).astype(bf16)
        at = slice(width * m, b.shape[1])
        out[m:, :] = (b[0, at, :].astype(f32) + c[0, at, :].astype(f32)).astype(bf16)


def gelu_pair(h):
    bell = jnp.exp2(h * h * (-0.5 * LOG2E))
    t = 1.0 / (1.0 + jnp.abs(h) * (0.3275911 * math.sqrt(0.5)))
    poly = 0.5 * 1.061405429
    for c in (-1.453152027, 1.421413741, -0.284496736, 0.254829592):
        poly = poly * t + 0.5 * c
    tail = poly * t * bell
    cdf = jnp.where(h < 0.0, tail, 1.0 - tail)
    return h * cdf, cdf + h * bell * (1.0 / math.sqrt(2.0 * math.pi))


def normalize(u):
    centre = u - jnp.mean(u, -1, keepdims=True)
    inv = lax.rsqrt(jnp.mean(centre * centre, -1, keepdims=True) + norm_eps)
    return centre * inv, inv


def norm_back(grad, normal, inv, gain):
    e = grad * gain
    return (e - jnp.mean(e, -1, keepdims=True) - normal * jnp.mean(e * normal, -1, keepdims=True)) * inv


def rowsum(x):
    return jnp.sum(x, 0, keepdims=True)


def row_codes(block, features):
    return block[:, features : features + 1].astype(jnp.int32)


def query_mask(code):
    lane = lax.broadcasted_iota(jnp.int32, (code.shape[0], HD), 1)
    return jnp.where((lane > NTAB) | (lane == (code >> 1)), 0.0, -1e30).astype(bf16)


def key_mask(code):
    lane = lax.broadcasted_iota(jnp.int32, (code.shape[0], HD), 1)
    return jnp.where((lane == (code >> 1)) | ((lane == NTAB) & ((code & 1) == 0)), 1.0, 0.0).astype(bf16)


def features_kernel(stage, pos, fa, fb, encw, encb, cur, low, normed, stats, qmask, kmask):
    stage.need(fa, fb, encw)
    features = encw.shape[0]
    half = fa.shape[0]
    own, other = fa[:, :features], fb[:, :features]
    code_a, code_b = row_codes(fa, features), row_codes(fb, features)
    qmask[...] = query_mask(code_a)
    kmask[:half, :] = key_mask(code_a)
    kmask[half:, :] = key_mask(code_b)
    mean_rows = jnp.zeros_like(own)
    scale_rows = jnp.zeros_like(own)
    for t in range(NTAB):
        pa = (code_a == 2 * t + 1).astype(f32)
        pb = (code_b == 2 * t + 1).astype(f32)
        count = rowsum(pa) + rowsum(pb)
        mean = (rowsum(pa * own) + rowsum(pb * other)) / count
        da, db = own - mean, other - mean
        excess = (rowsum(pa * da * da) + rowsum(pb * db * db)) / count
        scale = lax.rsqrt(jnp.maximum(excess, spread_floor))
        stats[t : t + 1, :] = mean
        stats[8 + t : 9 + t, :] = scale
        stats[16 + t : 17 + t, :] = excess
        stats[24 + t : 25 + t, :] = jnp.broadcast_to(count, mean.shape)
        here = (code_a >> 1) == t
        mean_rows = jnp.where(here, mean, mean_rows)
        scale_rows = jnp.where(here, scale, scale_rows)
    z = ((own - mean_rows) * scale_rows).astype(bf16)
    normed[...] = z
    out = mm(z, encw[...]) + encb[...].reshape(1, -1)
    cur[...] = out
    low[...] = out.astype(bf16)


def project(stage, x, w, bias, q, kv, layer, d):
    kv[:, :d] = mm(x, w[:, d : 2 * d]).astype(bf16)
    kv[:, d:] = (mm(x, w[:, 2 * d :]) + bias[2 * layer + 1 : 2 * layer + 2, :]).astype(bf16)
    stage.done(kv)
    q[...] = (mm(x, w[:, :d]) + bias[2 * layer : 2 * layer + 1, :]).astype(bf16)


def qkv_first_kernel(stage, pos, low, ga, gb, gc, gd, q, kv, w, bqv, bup):
    d = low.shape[1]
    buffers = (ga, gb, gc, gd)
    stage.need(*buffers)
    unpack(pos, buffers, 0, "qkv", w, d, 0)
    stage.done(w)
    base = 3 * d // 8
    f_part = 2 * HD
    for k in range(ga.shape[1]):
        z = pos[8 + k]
        rows = ga[0, k, base : base + 16, :].astype(f32)
        rows = rows[:8] + rows[8:]
        for j in range(4):
            bqv[j : j + 1, pl.ds(pl.multiple_of(z * HD, HD), HD)] = rows[j : j + 1]
            col = z * f_part + (j % 2) * HD
            bup[j // 2 : j // 2 + 1, pl.ds(pl.multiple_of(col, HD), HD)] = rows[4 + j : 5 + j]
    stage.need(low)
    project(stage, low[...], w, bqv, q, kv, 0, d)


def qkv_next_kernel(stage, pos, low, ga, gb, gc, gd, bqv, q, kv, w):
    d = low.shape[1]
    stage.need(ga, gb, gc, gd)
    unpack(pos, (ga, gb, gc, gd), 0, "qkv", w, d, 0)
    stage.done(w)
    stage.need(low)
    project(stage, low[...], w, bqv, q, kv, 1, d)


def attention_rows(rows, q, kva, kvb, qmask, kmask, mix, lse, d):
    n = kva.shape[0]
    factor = LOG2E / math.sqrt(HD)
    count = rows.size
    lane = lax.broadcasted_iota(jnp.int32, (count, HD), 1)
    totals = jnp.zeros((count, HD), f32)
    for h in range(d // HD):
        cols = slice(h * HD, (h + 1) * HD)
        vals = slice(d + h * HD, d + (h + 1) * HD)
        qh = jnp.concatenate([q[rows, cols], qmask[rows, :]], 1)
        ta = mm_nt(qh, jnp.concatenate([kva[:, cols], kmask[:n, :]], 1))
        tb = mm_nt(qh, jnp.concatenate([kvb[:, cols], kmask[n:, :]], 1))
        top = jnp.maximum(jnp.max(ta, -1, keepdims=True), jnp.max(tb, -1, keepdims=True)) * factor
        ea, eb = jnp.exp2(ta * factor - top), jnp.exp2(tb * factor - top)
        total = jnp.sum(ea, -1, keepdims=True) + jnp.sum(eb, -1, keepdims=True)
        out = mm(ea.astype(bf16), kva[:, vals]) + mm(eb.astype(bf16), kvb[:, vals])
        mix[rows, cols] = out / total
        totals = jnp.where(lane == h, top + jnp.log2(total), totals)
    lse[rows, :] = totals


def layer_rows(rows, cur, mix, wo, wu, wd, bup, ob, lg, lb, layer, n1, inv1, act, dgel, n2, inv2):
    l = layer
    u = cur + mm(mix[rows, :].astype(bf16), wo[...]) + ob[l, 0:1, :]
    normal, inv = normalize(u)
    n1[rows, :] = normal
    inv1[rows, :] = jnp.broadcast_to(inv, (rows.size, HD))
    middle = normal * lg[l, 0:1, :] + lb[l, 0:1, :]
    hidden = mm(middle.astype(bf16), wu[...]) + bup[l : l + 1, :]
    value, slope = gelu_pair(hidden)
    value = value.astype(bf16)
    act[rows, :] = value
    dgel[rows, :] = slope.astype(bf16)
    u = middle + mm(value, wd[...]) + ob[l, 1:2, :]
    normal, inv = normalize(u)
    n2[rows, :] = normal
    inv2[rows, :] = jnp.broadcast_to(inv, (rows.size, HD))
    return normal * lg[l, 1:2, :] + lb[l, 1:2, :]


def attention(stage, q, kva, kvb, qmask, kmask, mix, lse, raw, d):
    stage.need(q, kva, kvb)

    def step(i, carry):
        rows = pl.ds(pl.multiple_of(i * CHUNK, CHUNK), CHUNK)
        attention_rows(rows, q, kva, kvb, qmask, kmask, mix, raw, d)
        return carry

    lax.fori_loop(0, q.shape[0] // CHUNK, step, 0)
    stage.done(mix)
    lse[...] = raw[...].T[:8]


def unpack_rest(stage, pos, buffers, row0, wo, wu, wd, d, f_part):
    m = HD // 8 * (d // HD)
    stage.need(*buffers)
    unpack(pos, buffers, row0, "out", wo, d, f_part)
    unpack(pos, buffers, row0 + m, "up", wu, d, f_part)
    unpack(pos, buffers, row0 + m + d // 8 * (f_part // HD), "down", wd, d, f_part)
    stage.done(wo, wu, wd)


def first_layer_kernel(
    stage, pos, q, kva, kvb, qmask, kmask, ga, gb, gc, gd, cur, bup, ob, lg, lb,
    mix, lse, n1, inv1, act, dgel, n2, inv2, low, wo, wu, wd,
    raw,
):
    d = q.shape[1]
    attention(stage, q, kva, kvb, qmask, kmask, mix, lse, raw, d)
    unpack_rest(stage, pos, (ga, gb, gc, gd), 0, wo, wu, wd, d, wu.shape[1] // ga.shape[1])
    stage.need(cur)

    def step(i, carry):
        rows = pl.ds(pl.multiple_of(i * CHUNK, CHUNK), CHUNK)
        out = layer_rows(
            rows, cur[rows, :], mix, wo, wu, wd, bup, ob, lg, lb, 0, n1, inv1, act, dgel, n2, inv2
        )
        low[rows, :] = out.astype(bf16)
        return carry

    lax.fori_loop(0, q.shape[0] // CHUNK, step, 0)


CHUNK = 512


def ffn_back(
    stage, pos, grad, l, n1, inv1, act, dgel, n2, inv2, mix, wo, wu, wd, lg, lb,
    gmix, gbm, delta, keep, send, vec, vrow, gl, gh, g1, dwd, dwu, dwo, d, f_part, width, piece, order, base,
):
    gain0, gain1 = lg[l, 0:1, :], lg[l, 1:2, :]
    shift0 = lb[l, 0:1, :]
    f = wu.shape[1]

    def step(i, carry):
        rows = pl.ds(pl.multiple_of(i * CHUNK, CHUNK), CHUNK)
        top = grad[rows, :].astype(f32)
        normal = n2[rows, :]
        bo = norm_back(top, normal, inv2[rows, :1], gain1)
        low = bo.astype(bf16)
        gl[rows, :] = low
        back = mm_nt(low, wd[...])
        back = (back * dgel[rows, :].astype(f32)).astype(bf16)
        gh[rows, :] = back
        gm = bo + mm_nt(back, wu[...])
        first = n1[rows, :]
        bm = norm_back(gm, first, inv1[rows, :1], gain0)
        gbm[rows, :] = bm
        attn = bm.astype(bf16)
        g1[rows, :] = attn
        gmix[rows, :] = mm_nt(attn, wo[...]).astype(bf16)
        sums = (
            rowsum(gm * first),
            rowsum(top * normal),
            rowsum(gm),
            rowsum(top),
            rowsum(attn.astype(f32)),
            rowsum(low.astype(f32)),
        )
        hidden = rowsum(back.astype(f32))
        for j in range(6):
            vec[vrow + j : vrow + j + 1, :] += sums[j]
        for j in range(f // d):
            at = vrow + 8 + j
            vec[at : at + 1, :] += hidden[:, j * d : (j + 1) * d]
        return carry

    lax.fori_loop(0, act.shape[0] // CHUNK, step, 0)
    stage.done(gmix, gbm)
    for h in range(d // HD):
        cols = slice(h * HD, (h + 1) * HD)
        prod = gmix[:, cols].astype(f32) * mix[:, cols]
        delta[h : h + 1, :] = jnp.sum(prod.T, 0, keepdims=True)
    m = HD // 8 * (d // HD)
    dwd[...] = mm_tn(act[...], gl[...]).astype(bf16)
    middle = (n1[...] * gain0 + shift0).astype(bf16)
    dwu[...] = mm_tn(middle, gh[...]).astype(bf16)
    dwo[...] = mm_tn(mix[...].astype(bf16), g1[...]).astype(bf16)
    pack(pos, dwd, base + m + d // 8 * (f_part // HD), "down", (keep, send), d, f_part, width, piece, order)
    pack(pos, dwu, base + m, "up", (keep, send), d, f_part, width, piece, order)
    pack(pos, dwo, base, "out", (keep, send), d, f_part, width, piece, order)


def last_layer_kernel(
    stage, pos, q, kva, kvb, qmask, kmask, ga, gb, gc, gd, n2in, cot, bup, ob, lg, lb,
    lse, final, gmix, gbm, delta, keep, send, vec,
    raw, mix, wo, wu, wd, n1, inv1, act, dgel, n2, inv2, gl, gh, g1, dwd, dwu, dwo,
):
    d = q.shape[1]
    width = ga.shape[1]
    f_part = wu.shape[1] // width
    attention(stage, q, kva, kvb, qmask, kmask, mix, lse, raw, d)
    unpack_rest(stage, pos, (ga, gb, gc, gd), 3 * d // 8, wo, wu, wd, d, f_part)
    stage.need(n2in)

    def step(i, carry):
        rows = pl.ds(pl.multiple_of(i * CHUNK, CHUNK), CHUNK)
        cur = n2in[rows, :] * lg[0, 1:2, :] + lb[0, 1:2, :]
        out = layer_rows(
            rows, cur, mix, wo, wu, wd, bup, ob, lg, lb, 1, n1, inv1, act, dgel, n2, inv2
        )
        final[rows, :] = out.astype(bf16)
        return carry

    lax.fori_loop(0, q.shape[0] // CHUNK, step, 0)
    stage.done(final)
    vec[...] = jnp.zeros_like(vec)
    stage.need(cot)
    ffn_back(
        stage, pos, cot, 1, n1, inv1, act, dgel, n2, inv2, mix, wo, wu, wd, lg, lb,
        gmix, gbm, delta, keep, send, vec, 0, gl, gh, g1, dwd, dwu, dwo, d, f_part, width, keep.shape[1] // width, 0, 0,
    )


def attention_back_kernel(stage, pos, gmix, delta, q, kvb, kva, lse, qmask, kmask, dq, dkva, dkvb, acc):
    d = q.shape[1]
    n = kva.shape[0]
    scaling = 1.0 / math.sqrt(HD)
    factor = LOG2E * scaling
    block = 512
    stage.need(gmix)
    acc[...] = jnp.zeros_like(acc)
    stage.need(q)
    for src, dst, off in ((kvb, dkvb, n), (kva, dkva, 0)):
        stage.need(src)

        def step(i, carry, src=src, dst=dst, off=off):
            rows = pl.ds(pl.multiple_of(i * block, block), block)
            brow = pl.ds(pl.multiple_of(off + i * block, block), block)
            for h in range(d // HD):
                cols = slice(h * HD, (h + 1) * HD)
                vals = slice(d + h * HD, d + (h + 1) * HD)
                qh, gh = q[:, cols], gmix[:, cols]
                kh, vh = src[rows, cols], src[rows, vals]
                scores = mm_nt(
                    jnp.concatenate([kh, kmask[brow, :]], 1), jnp.concatenate([qh, qmask[...]], 1)
                )
                probs = jnp.exp2(scores * factor - lse[h : h + 1, :])
                ds = (probs * (mm_nt(vh, gh) - delta[h : h + 1, :])).astype(bf16)
                dst[rows, vals] = mm(probs.astype(bf16), gh).astype(dst.dtype)
                dst[rows, cols] = (mm(ds, qh) * scaling).astype(dst.dtype)
                acc[h, :, :] += mm_tn(kh, ds)
            return carry

        lax.fori_loop(0, n // block, step, 0)
        stage.done(dst)
    for h in range(d // HD):
        dq[:, h * HD : (h + 1) * HD] = (acc[h].T * scaling).astype(bf16)


def projection_back(
    stage, pos, dq, dkva, dkvr, low, w, gbm, proj, dw, keep, send, vec, vrow, d, width, piece, order
):
    stage.need(dq, dkva, dkvr)
    proj[:, :d] = dq[...]
    proj[:, d:] = (dkva[...].astype(f32) + dkvr[...].astype(f32)).astype(bf16)
    vec[vrow : vrow + 1, :] = rowsum(dq[...].astype(f32))
    vec[vrow + 1 : vrow + 2, :] = rowsum(proj[:, 2 * d :].astype(f32))
    dw[...] = mm_tn(low(), proj[...]).astype(bf16)
    stage.need(w, gbm)
    grad = gbm[...] + mm_nt(proj[...], w[...])
    pack(pos, dw, 0, "qkv", (keep, send), d, 0, width, piece, order)
    return grad


def middle_kernel(
    stage, pos, dq, dkva, dkvr, w, gbm1, n2, inv2, wd, dgel, wu, n1, inv1, wo, act, mix, vec1, lg, lb,
    gmix, gbm, delta, keep, send, vec,
    proj, dw, grad, gl, gh, g1, dwd, dwu, dwo,
):
    d = grad.shape[1]
    width = d // HD
    first = 3 * d // 8
    piece = keep.shape[1] // width
    vec[...] = jnp.zeros_like(vec)
    for j in range(10):
        vec[10 + j : 11 + j, :] = vec1[j : j + 1, :]

    def low():
        return (n2[...] * lg[0, 1:2, :] + lb[0, 1:2, :]).astype(bf16)

    grad[...] = projection_back(
        stage, pos, dq, dkva, dkvr, low, w, gbm1, proj, dw, keep, send, vec, 16, d, width, piece, 0
    )
    ffn_back(
        stage, pos, grad, 0, n1, inv1, act, dgel, n2, inv2, mix, wo, wu, wd, lg, lb,
        gmix, gbm, delta, keep, send, vec, 0, gl, gh, g1, dwd, dwu, dwo, d, wu.shape[1] // width,
        width, piece, 0, first,
    )


def entry_kernel(
    stage, pos, dq, dkva, dkvr, low0, w0, gbm0, normed, encw, fa, vec, stats,
    keep, send, gnorm, sums,
    proj, dw, shared,
):
    d = dq.shape[1]
    features = encw.shape[0]
    width = d // HD
    first = 3 * d // 8
    shared[...] = jnp.zeros_like(shared)
    shared[:24, :] = vec[...]
    def low():
        stage.need(low0)
        return low0[...]

    grad = projection_back(
        stage, pos, dq, dkva, dkvr, low, w0, gbm0, proj, dw, keep, send, shared, 6, d, width, first, 0
    )
    stage.need(normed, encw, fa)
    low = grad.astype(bf16)
    shared[20:21, :] = rowsum(low.astype(f32))
    shared[24 : 24 + features, :] = mm_tn(normed[...], low)
    back = mm_nt(low, encw[...])
    gnorm[...] = back
    code = row_codes(fa, features) >> 1
    centred = fa[:, :features]
    sums[...] = jnp.zeros_like(sums)
    for t in range(NTAB):
        here = code == t
        part = jnp.where(here, back, 0.0)
        sums[t : t + 1, :] = rowsum(part)
        sums[8 + t : 9 + t, :] = rowsum(part * (centred - stats[t : t + 1, :]))
    share = shared.shape[0] // 8
    for c, dst in ((0, keep), (1, send)):

        def step(e, carry, dst=dst, c=c):
            row = pl.multiple_of(pos[c * 4 + e] * share, 8)
            for j in range(d // HD):
                piece = shared[pl.ds(row, share), j * HD : (j + 1) * HD].astype(bf16)
                at = width * first + j * share
                dst[e, at : at + share, :] = piece
            return carry

        lax.fori_loop(0, 4, step, 0)


def features_back_kernel(stage, pos, gnorm, fa, stats, mine, theirs, out):
    total = mine[...] + theirs[...]
    stage.need(gnorm, fa)
    back = gnorm[...]
    code = row_codes(fa, back.shape[1])
    x = fa[:, : back.shape[1]]
    scale_rows = jnp.zeros_like(x)
    flat = jnp.zeros_like(x)
    slope = jnp.zeros_like(x)
    for t in range(NTAB):
        mean, scale = stats[t : t + 1, :], stats[8 + t : 9 + t, :]
        excess, count = stats[16 + t : 17 + t, :], stats[24 + t : 25 + t, :]
        plain, centred = total[t : t + 1, :], total[8 + t : 9 + t, :]
        g_excess = jnp.where(excess > spread_floor, -0.5 * scale * scale * scale * centred, 0.0)
        g_mean = -scale * plain - 2.0 * mean * g_excess
        scale_rows = jnp.where((code >> 1) == t, scale, scale_rows)
        chosen = code == 2 * t + 1
        flat = jnp.where(chosen, g_mean / count, flat)
        slope = jnp.where(chosen, 2.0 * g_excess / count, slope)
    out[...] = back * scale_rows + flat + x * slope


def result_kernel(
    stage, pos, ra, rb, rc, rd, ea, eb, ec, ed, gqkv, gout, gup, gdown, genc_w, genc_b, gbqv, gob, glg, glb, gbup, rows
):
    d, f_part = gqkv.shape[2], gup.shape[2]
    n, m, r = d // 8, HD // 8, f_part // 8
    first = 3 * n
    share = rows.shape[0] // 8
    after = m * (d // HD) + n * (f_part // HD) + r * (d // HD)

    def rest(l, src, e, q, base):
        for c in range(d // HD):
            gout[l, pl.ds(pl.multiple_of(q * m, 16), m), c * HD : (c + 1) * HD] = src[
                e, base + c * m : base + (c + 1) * m, :
            ].astype(f32)
        base += d // HD * m
        for c in range(f_part // HD):
            gup[l, pl.ds(pl.multiple_of(q * n, 16), n), c * HD : (c + 1) * HD] = src[
                e, base + c * n : base + (c + 1) * n, :
            ].astype(f32)
        base += f_part // HD * n
        for c in range(d // HD):
            gdown[l, pl.ds(pl.multiple_of(q * r, 16), r), c * HD : (c + 1) * HD] = src[
                e, base + c * r : base + (c + 1) * r, :
            ].astype(f32)

    for part, (src, end) in enumerate(((ra, ea), (rb, eb), (rc, ec), (rd, ed))):
        stage.need(src, end)

        def step(e, carry, part=part, src=src, end=end):
            q = pos[part * 2 + e]
            for l, ref, base in ((1, src, after), (0, end, 0)):
                for c in range(3):
                    gqkv[l, c, pl.ds(pl.multiple_of(q * n, 16), n), :] = ref[
                        e, base + c * n : base + (c + 1) * n, :
                    ].astype(f32)
            rest(1, src, e, q, 0)
            rest(0, src, e, q, after + first)
            for j in range(d // HD):
                rows[pl.ds(pl.multiple_of(q * share, 8), share), j * HD : (j + 1) * HD] = end[
                    e, first + j * share : first + (j + 1) * share, :
                ].astype(f32)
            return carry

        lax.fori_loop(0, src.shape[0], step, 0)
    z = pos[8]
    d = genc_w.shape[1]
    layers = gob.shape[0]
    genc_w[...] = rows[24 : 24 + genc_w.shape[0], :]
    genc_b[...] = rows[10 * layers : 10 * layers + 1, :]
    for l in range(layers):
        at = 10 * l
        for j in range(2):
            glg[l, j : j + 1, :] = rows[at + j : at + j + 1, :]
            glb[l, j : j + 1, :] = rows[at + 2 + j : at + 3 + j, :]
            gob[l, j : j + 1, :] = rows[at + 4 + j : at + 5 + j, :]
            gbqv[l, j : j + 1, :] = rows[at + 6 + j : at + 7 + j, pl.ds(pl.multiple_of(z * HD, HD), HD)]
        row = at + 8 + (z * f_part) // d
        col = pl.multiple_of((z * f_part) % d, HD)
        gbup[l : l + 1, :] = rows[pl.ds(row, 1), pl.ds(col, f_part)]


def swap_dp(values, even, odd=None):
    odd = even if odd is None else odd
    return lax.ppermute(values, ("plane", "pair"), [(i, i ^ (odd if i % 2 else even)) for i in range(8)])


def swap_z(values, mask):
    size = lax.axis_size("tensor")
    return lax.ppermute(values, "tensor", [(i, i ^ mask) for i in range(size)])


def relay_pairs(step):
    width = lax.axis_size("tensor")
    return [
        (p * width + z, z // 2 * width + 2 * p + (step ^ (z & 1))) for p in range(2) for z in range(width)
    ]


def pick(values, index, axis=0):
    return lax.dynamic_index_in_dim(values, index, axis, keepdims=False)


def to_sequences(one_block, z):
    got = [lax.ppermute(one_block(step ^ (z & 1)), ("pair", "tensor"), relay_pairs(step)) for step in range(2)]
    return jnp.concatenate(got)


def from_sequences(values, z, sent=None):
    part = values.shape[0] // 2
    got = [
        lax.ppermute(
            values[step * part : (step + 1) * part],
            ("pair", "tensor"),
            [(b, a) for a, b in relay_pairs(step)],
        )
        for step in range(2)
    ]
    if sent is not None:
        sent.extend(got)
    odd = (z & 1) == 1
    return jnp.stack([jnp.where(odd, got[1], got[0]), jnp.where(odd, got[0], got[1])], 1)


def stack_kernel(stage, pos, *refs):
    out = refs[-1]
    for at, ref in enumerate(refs[:-1]):
        out[at] = ref[...]


def stack(pos, pieces, name, after=()):
    shape = (len(pieces),) + pieces[0].shape
    return call(stack_kernel, [(shape, bf16)], [pos] + pieces, name=name, after=after, vmem=6)[0]


def copy_kernel(stage, pos, src, out):
    out[...] = src[...]


def later(pos, values, name, after):
    return call(copy_kernel, [(values.shape, values.dtype)], [pos, values], name=name, after=after, vmem=4)[0]


def over_z(pos, piece, name, after=()):
    pieces = [piece] + [swap_z(piece, k) for k in range(1, lax.axis_size("tensor"))]
    return stack(pos, pieces, name, after)


def over_plane(pos, piece, name, after=()):
    two = stack(pos, [piece, swap_dp(piece, 4, 2)], name, after)
    return two, swap_dp(two, 2, 4)


def over_pair(two, more):
    return two, more, swap_dp(two, 1), swap_dp(more, 1)


def add(a, b):
    return (a.astype(f32) + b.astype(f32)).astype(bf16)


def sum_far(values):
    return lax.psum(values.astype(f32), "far").astype(bf16) if lax.axis_size("far") > 1 else values


def split(pos, a, b, name, after=()):
    outs = [((a.shape[0] // 2,) + a.shape[1:], bf16)] * 2
    return call(add_kernel, outs, [pos, a, b], name=name, vmem=12, after=after)


def sum_z(shares):
    total = shares[0].astype(f32)
    for k in range(1, len(shares)):
        total = total + swap_z(shares[k], k).astype(f32)
    return total.astype(bf16)


def local(
    features,
    table_ids,
    train_flags,
    enc_w,
    enc_b,
    w_qkv,
    b_qv,
    w_out,
    out_bias,
    ln_gain,
    ln_bias,
    w_up,
    b_up,
    w_down,
    cotangent,
):
    part, _, fdim = features.shape
    width = lax.axis_size("tensor")
    layers, d, f_part = w_qkv.shape[0], w_qkv.shape[2], w_up.shape[2]
    f = f_part * width
    half = 2 * part
    n = 2 * half
    z, p, o = lax.axis_index("tensor"), lax.axis_index("pair"), lax.axis_index("plane")
    ox, oy = o & 1, o >> 1
    relative, absolute = [], []
    for c in range(2):
        for r1 in range(2):
            for r2 in range(2):
                pd = p ^ c
                rx, ry = jnp.where(pd == 0, r1, r2), jnp.where(pd == 0, r2, r1)
                relative.append(pd * 4 + (oy ^ ry) * 2 + (ox ^ rx))
                absolute.append(pd * 4 + r1 * 2 + r2)
    pos = jnp.stack(relative + [z ^ k for k in range(width)] + absolute).astype(jnp.int32)
    rest = HD // 8 * (d // HD) + d // 8 * (f_part // HD) + f_part // 8 * (d // HD)
    first = 3 * d // 8

    codes = lax.dynamic_slice_in_dim(table_ids, z * part, part) * 2
    codes = (codes + lax.dynamic_slice_in_dim(train_flags, z * part, part)).astype(f32)

    def feature_block(j):
        space = jnp.zeros((part, HD - fdim - 1), f32)
        return jnp.concatenate([pick(features, j, 1), pick(codes, j, 1)[:, None], space], 1)

    feat_own = to_sequences(feature_block, z)
    feat_other = swap_dp(feat_own, 1)
    (g0,) = call(
        pack_first_kernel,
        [((first + 16, HD), bf16)],
        [pos, w_qkv, b_qv, b_up],
        [((3,), None)],
        name="pack_first",
        vmem=4,
        far=(1,),
    )
    w0z = over_z(pos, g0, "first_z", (feat_own,))
    w0p = over_plane(pos, w0z, "first_plane", (feat_other,))
    w0 = over_pair(*w0p)
    (g1,) = call(
        pack_rest_kernel,
        [((rest, HD), bf16)],
        [pos, w_out, w_up, w_down],
        [((16,), None)],
        name="pack_rest",
        vmem=4,
        far=(1, 2, 3),
        after=(w0z,),
    )
    w1z = over_z(pos, g1, "rest_z")
    cur0, low0, normed, stats, qmask, kmask = call(
        features_kernel,
        [
            ((half, d), f32), ((half, d), bf16), ((half, fdim), bf16), ((32, fdim), f32),
            ((half, HD), bf16), ((n, HD), bf16),
        ],
        [pos, feat_own, feat_other, enc_w, enc_b[None]],
        flops=2 * half * d * HD,
        name="features",
        vmem=8,
    )
    (g2,) = call(
        pack_second_kernel,
        [((first + rest, HD), bf16)],
        [pos, w_qkv, w_out, w_up, w_down],
        [((16,), None)],
        name="pack_second",
        vmem=4,
        far=(1, 2, 3, 4),
        after=(w1z,),
    )
    w1p = over_plane(pos, w1z, "rest_plane", (g2, w0p[1]))
    w1 = over_pair(*w1p)
    q0, kv0, wq0, bqv, bup = call(
        qkv_first_kernel,
        [((half, d), bf16), ((half, 2 * d), bf16), ((d, 3 * d), bf16), ((8, d), f32), ((8, f), f32)],
        [pos, low0, *w0],
        flops=2 * half * d * 3 * d,
        name="qkv_first",
        vmem=10,
    )
    cot = to_sequences(lambda j: later(pos, pick(cotangent, j, 1), "cotangent", (w1p[0],)), z)
    w2z = over_z(pos, g2, "second_z", (w1p[0],))
    w2p = over_plane(pos, w2z, "second_plane", (w1p[1], q0, cot))

    kv0r = swap_dp(kv0, 1)
    ob, lg, lb = out_bias, ln_gain, ln_bias
    mix0, lse0, n1, inv1, act, dgel, n2, inv2, low1, wo, wu, wd = call(
        first_layer_kernel,
        [
            ((half, d), f32), ((8, half), f32), ((half, d), f32), ((half, HD), f32), ((half, f), bf16),
            ((half, f), bf16), ((half, d), f32), ((half, HD), f32), ((half, d), bf16),
            ((d, d), bf16), ((d, f), bf16), ((f, d), bf16),
        ],
        [pos, q0, kv0, kv0r, qmask, kmask, *w1, cur0, bup, ob, lg, lb],
        [((half, HD), f32)],
        flops=2 * half * (2 * n * d + d * d + 2 * d * f),
        name="first_layer",
        after=(w2p[0],),
        vmem=8,
    )
    w2 = (w2p[0], w2p[1], swap_dp(w2p[0], 1), swap_dp(later(pos, w2p[1], "second_copy", (low1,)), 1))
    q1, kv1, wq1 = call(
        qkv_next_kernel,
        [((half, d), bf16), ((half, 2 * d), bf16), ((d, 3 * d), bf16)],
        [pos, low1, *w2, bqv],
        flops=2 * half * d * 3 * d,
        name="qkv_next",
        vmem=12,
    )
    kv1r = swap_dp(kv1, 1)
    lse1, final, gmix1, gbm1, delta1, keep1, send1, vec1 = call(
        last_layer_kernel,
        [
            ((8, half), f32), ((half, d), bf16), ((half, d), bf16), ((half, d), f32), ((8, half), f32),
            ((4, width * rest, HD), bf16), ((4, width * rest, HD), bf16), ((16, d), f32),
        ],
        [pos, q1, kv1, kv1r, qmask, kmask, *w2, n2, cot, bup, ob, lg, lb],
        [
            ((half, HD), f32), ((half, d), f32), ((d, d), bf16), ((d, f), bf16), ((f, d), bf16),
            ((half, d), f32), ((half, HD), f32), ((half, f), bf16), ((half, f), bf16), ((half, d), f32),
            ((half, HD), f32), ((half, d), bf16), ((half, f), bf16), ((half, d), bf16), ((f, d), bf16), ((d, f), bf16),
            ((d, d), bf16),
        ],
        flops=2 * half * (2 * n * d + d * d + 2 * d * f) * 3,
        name="last_layer",
        vmem=18,
    )
    sent = []
    final_rows = from_sequences(final, z, sent)
    four1 = split(pos, keep1, swap_dp(send1, 1), "add_pair_last")
    def attention_back(q, kv, kvr, delta, gmix, lse, name, after=(), beside=()):
        dq, dkva, dkvb = call(
            attention_back_kernel,
            [((half, d), bf16), ((half, 2 * d), bf16), ((half, 2 * d), bf16)],
            [pos, gmix, delta, q, kvr, kv, lse, qmask, kmask],
            [((d // HD, HD, half), f32)],
            flops=2 * half * 5 * n * d,
            name=name,
            vmem=10,
            after=after,
        )
        return dq, dkva, swap_dp(later(pos, dkvb, "keys", beside) if beside else dkvb, 1)

    dq1, dkva1, dkvr1 = attention_back(q1, kv1, kv1r, delta1, gmix1, lse1, "attention_back_last")
    gmix0, gbm0, delta0, keep2, send2, vec = call(
        middle_kernel,
        [
            ((half, d), bf16), ((half, d), f32), ((8, half), f32),
            ((4, width * (first + rest), HD), bf16), ((4, width * (first + rest), HD), bf16), ((24, d), f32),
        ],
        [
            pos, dq1, dkva1, dkvr1, wq1, gbm1, n2, inv2, wd, dgel, wu, n1, inv1, wo, act, mix0, vec1, lg, lb,
        ],
        [
            ((half, 3 * d), bf16), ((d, 3 * d), bf16), ((half, d), f32),
            ((half, d), bf16), ((half, f), bf16), ((half, d), bf16),
            ((f, d), bf16), ((d, f), bf16), ((d, d), bf16),
        ],
        flops=2 * half * (6 * d * d + 2 * d * d + 4 * d * f),
        name="middle",
        after=four1,
        vmem=13,
    )
    late1 = swap_dp(four1[1], 2, 4)
    two1 = split(pos, four1[0], late1, "add_plane_last")
    four2 = split(pos, keep2, swap_dp(later(pos, send2, "grads_middle", (late1,)), 1), "add_pair", (two1[0],))
    late1b = swap_dp(two1[1], 4, 2)
    dq0, dkva0, dkvr0 = attention_back(
        q0, kv0, kv0r, delta0, gmix0, lse0, "attention_back_first", (*four2, *two1), (late1b,)
    )
    two2 = split(pos, four2[0], swap_dp(four2[1], 2, 4), "add_plane")
    shares1 = call(
        join_kernel,
        [((rest, HD), bf16)] * width,
        [pos, two1[0], late1b],
        name="join_last",
        vmem=8,
    )
    shared_rows = -(-(24 + fdim) // 128) * 128
    share = shared_rows // 8 * (d // HD)
    keep3, send3, gnorm, sums = call(
        entry_kernel,
        [
            ((4, width * first + share, HD), bf16), ((4, width * first + share, HD), bf16),
            ((half, fdim), f32), ((16, fdim), f32),
        ],
        [pos, dq0, dkva0, dkvr0, low0, wq0, gbm0, normed, enc_w, feat_own, vec, stats],
        [((half, 3 * d), bf16), ((d, 3 * d), bf16), ((shared_rows, d), f32)],
        flops=2 * half * (6 * d * d + 2 * d * HD),
        name="entry",
        after=(*two2, *shares1),
        vmem=12,
    )
    shares2 = call(
        join_kernel,
        [((first + rest, HD), bf16)] * width,
        [pos, two2[0], swap_dp(two2[1], 4, 2)],
        name="join",
        vmem=10,
    )
    four3 = split(pos, keep3, swap_dp(send3, 1), "add_pair_entry")
    two3 = split(pos, four3[0], swap_dp(four3[1], 2, 4), "add_plane_entry")
    shares3 = call(
        join_last_kernel,
        [((first + share, HD), bf16)] * width,
        [pos, two3[0], swap_dp(two3[1], 4, 2)],
        name="join_entry",
        vmem=6,
    )
    piece = jnp.concatenate([sum_z([sum_far(part) for part in shares1]), sum_z([sum_far(part) for part in shares2])])
    r1 = over_pair(*over_plane(pos, piece, "results_plane"))
    r2 = over_pair(*over_plane(pos, sum_z([sum_far(part) for part in shares3]), "results_plane_entry"))
    (g_feat,) = call(
        features_back_kernel,
        [((half, fdim), f32)],
        [pos, gnorm, feat_own, stats, sums, swap_dp(sums, 1)],
        name="features_back",
        vmem=6,
    )
    grad_features = from_sequences(g_feat, z)
    g_qkv, g_out, g_up, g_down, g_enc_w, g_enc_b, g_bqv, g_ob, g_lg, g_lb, g_bup = call(
        result_kernel,
        [
            ((layers, 3, d, HD), f32), ((layers, HD, d), f32), ((layers, d, f_part), f32), ((layers, f_part, d), f32),
            ((fdim, d), f32), ((1, d), f32), ((layers, 2, HD), f32), ((layers, 2, d), f32), ((layers, 2, d), f32),
            ((layers, 2, d), f32), ((layers, f_part), f32),
        ],
        [pos, *r1, *r2],
        [((shared_rows, d), f32)],
        name="results",
        vmem=10,
    )
    return (
        final_rows, grad_features, g_enc_w, g_enc_b[0], g_qkv, g_bqv, g_out, g_ob, g_lg, g_lb, g_up, g_bup, g_down,
    )


def solution(mesh):
    size, width = mesh.shape["dp"], mesh.shape["tensor"]
    mesh = jax.sharding.Mesh(mesh.devices.reshape(size // 8, 4, 2, width), ("far", "plane", "pair", "tensor"))
    dp = ("far", "plane", "pair")
    rows, ids = P("tensor", dp, None), P(None, dp)
    qkv, bqv = P(None, None, None, "tensor"), P(None, None, "tensor")
    mid, last = P(None, "tensor", None), P(None, None, "tensor")
    in_specs = (rows, ids, ids, P(), P(), qkv, bqv, mid, P(), P(), P(), last, P(None, "tensor"), mid, rows)
    out_specs = (rows, rows, P(), P(), qkv, bqv, mid, P(), P(), P(), last, P(None, "tensor"), mid)
    return jax.shard_map(local, mesh=mesh, in_specs=in_specs, out_specs=out_specs, check_vma=False)
```
